128 devices in a mesh: seq: 8 (over x_lo, z), ch: 16 (over y, x_hi, core).
Axes of the slice: x: 4 (x_hi: 2, x_lo: 2; x = x_hi * 2 + x_lo), y: 4, z: 4, core: 2. Of those that a mesh axis runs over, the one named last changes fastest.
Arguments:
- query_stream: bfloat16 [256, 131072], P(None, ('seq', 'ch')), may hold values from -6 to 6
- key_stream: bfloat16 [256, 131072], P(None, ('seq', 'ch')), may hold values from -6 to 6
- value_stream: bfloat16 [256, 131072], P(None, ('seq', 'ch')), may hold values from -6 to 6
- short_taps: float32 [3, 3, 256], replicated, may hold values from -3.5 to 3.5
- long_filter: bfloat16 [16, 8, 2, 131072], P('ch', 'seq'), may hold values from -0.015625 to 0.015625
- skip_gain: float32 [256], replicated, may hold values from -4 to 4
Outputs:
- gated_output: bfloat16 [256, 131072], P(None, ('seq', 'ch'))
The draws below stay inside these ranges and needn't reach their ends.
All inputs are finite; a program needn't handle non-finite values.
Results may differ from the reference program's by a relative error of at most 0.0085.
Values may be sent and summed in bfloat16 or wider, within the bound.
No kernel may reach another device: no remote copies, remote signals or barrier semaphores. Data moves between devices by JAX's collectives and lax.ppermute only.
A program may use at most 64 MiB of HBM per device.

```python
import math
import jax
import jax.numpy as jnp
from jax import lax

C = 256
TAPS = 3
SEQ_BLOCKS = 8
CHAN_GROUPS = 16
CP = 2
L = 131072


def shard_levels(stream_key, dims, cuts, low, high):
    loudness = 1.0
    for position, parts in cuts:
        steps = jax.random.uniform(jax.random.fold_in(jax.random.fold_in(stream_key, 6), position), (parts,), jnp.float32, low / len(cuts), high / len(cuts))
        loudness = loudness * jnp.repeat(jnp.exp(steps), dims[position] // parts).reshape((-1,) + (1,) * (len(dims) - 1 - position))
    return loudness


def gaussian(rng, extent, width, most, split=(), dtype=jnp.bfloat16):
    factor_of = shard_levels(rng, extent, split, -0.22, 0.18) if split else 1.0
    drawn = jax.random.normal(rng, extent, jnp.float32) * width * factor_of
    return jnp.minimum(jnp.maximum(drawn, -most), most).astype(dtype)


def setup_inputs(seed: int = 0) -> dict:
    key_of = jax.random.split(jax.random.key(seed), 7)
    query_stream = gaussian(key_of[0], (C, L), 1.0, 6.0, ((1, 128),))
    key_stream = gaussian(key_of[1], (C, L), 1.0, 6.0, ((1, 128),))
    value_stream = gaussian(key_of[2], (C, L), 1.0, 6.0, ((1, 128),))
    short_taps = gaussian(key_of[3], (3, TAPS, C), TAPS ** -0.5, 3.5, (), jnp.float32)
    long_filter = gaussian(key_of[4], (CHAN_GROUPS, SEQ_BLOCKS, CP, L), L ** -0.5, 0.015625, ((0, 16), (1, 8)))
    skip_gain = gaussian(key_of[5], (C,), 1.0, 4.0, (), jnp.float32)
    return dict(query_stream=query_stream, key_stream=key_stream, value_stream=value_stream, short_taps=short_taps, long_filter=long_filter, skip_gain=skip_gain)


def causal_taps(stream, taps):
    padded = jnp.pad(stream.astype(jnp.float32), ((0, 0), (2, 0)))
    result = taps[0][:, None] * padded[:, 2:] + taps[1][:, None] * padded[:, 1:-1]
    return result + taps[2][:, None] * padded[:, :-2]


def reference(query_stream, key_stream, value_stream, short_taps, long_filter, skip_gain):
    query_conv = causal_taps(query_stream, short_taps[0])
    key_conv = causal_taps(key_stream, short_taps[1])
    value_conv = causal_taps(value_stream, short_taps[2])
    gated = (key_conv * value_conv).astype(jnp.bfloat16)
    gated = lax.optimization_barrier(gated)
    filters = long_filter.reshape(C, L)
    width_block = math.gcd(C, 16)
    fft_length = 2 * L

    def one_block(blocks_pair):
        signal, taps_long = blocks_pair
        spectrum = jnp.fft.rfft(signal.astype(jnp.float32), n=fft_length) * jnp.fft.rfft(taps_long.astype(jnp.float32), n=fft_length)
        return jnp.fft.irfft(spectrum, n=fft_length)[:, :L].astype(jnp.float32)

    long_result = lax.map(one_block, (gated.reshape(C // width_block, width_block, L), filters.reshape(C // width_block, width_block, L)))
    long_result = long_result.reshape(C, L).astype(jnp.bfloat16)
    long_result = lax.optimization_barrier(long_result)
    mixed_out = query_conv * (long_result.astype(jnp.float32) + skip_gain[:, None] * gated.astype(jnp.float32))
    return mixed_out.astype(jnp.bfloat16)
```

```python
import functools
import math

import jax
import jax.numpy as jnp
import ml_dtypes
import numpy as np
from jax import lax
from jax.experimental import pallas as pl
from jax.experimental.pallas import tpu as pltpu
from jax.sharding import PartitionSpec as P

F32 = jnp.float32
BF16 = jnp.bfloat16
LANES = 128
OUTER = 1024
LENGTH = OUTER * LANES
CHANNELS = 256
TOKENS = 1024
TILES = TOKENS // LANES
SEQ = 8
CH = 16
ROWS = 32
CHUNK = 256
AXES = ("seq", "ch")
VMEM = pl.BlockSpec(memory_space=pltpu.VMEM)


def tables():
    step = 2.0 * math.pi
    a = np.arange(OUTER)[None, :]
    k1 = np.arange(OUTER)[:, None]
    outer_phase = ((4 * a + 1) * (4 * k1 + 1) % (16 * OUTER)) * (step / (16 * OUTER))
    outer = np.stack([np.cos(outer_phase), -np.sin(outer_phase)]).astype(ml_dtypes.bfloat16)
    lane = np.arange(LANES)[None, :]
    turn_phase = (k1 + 0.25) * (lane / LENGTH - 1.0 / (4 * OUTER)) * step
    turn = np.stack([np.cos(turn_phase), -np.sin(turn_phase)]).astype(np.float32)
    inner_phase = (lane * lane.T % LANES) * (step / LANES)
    cos, sin = np.cos(inner_phase), np.sin(inner_phase)
    forward = np.block([[cos, -sin], [sin, cos]]).astype(ml_dtypes.bfloat16)
    inverse = np.block([[cos, sin], [-sin, cos]]).astype(ml_dtypes.bfloat16)
    return outer, turn, forward, inverse


def dot(left, right):
    return jnp.dot(left, right, preferred_element_type=F32)


def call(body, out_shape, scratch, flops, nbytes, name, **kwargs):
    return pl.pallas_call(
        body,
        out_shape=out_shape,
        scratch_shapes=scratch,
        compiler_params=pltpu.CompilerParams(vmem_limit_bytes=48 * 1024 * 1024),
        cost_estimate=pl.CostEstimate(flops=flops, bytes_accessed=nbytes, transcendentals=0),
        name=name,
        **kwargs,
    )


def tails_body(q_ref, k_ref, v_ref, out_ref):
    row = lax.broadcasted_iota(jnp.int32, (16, LANES), 0)
    col = lax.broadcasted_iota(jnp.int32, (16, LANES), 1)
    total = jnp.zeros((16, CHANNELS), F32)
    for i, ref in enumerate((q_ref, k_ref, v_ref)):
        pick = (row - 2 * i == col - (LANES - 2)) & (col >= LANES - 2)
        total += lax.dot_general(
            pick.astype(BF16), ref[...], (((1,), (1,)), ((), ())), preferred_element_type=F32
        )
    out_ref[...] = total.astype(BF16)


def tails(q, k, v):
    last = pl.BlockSpec((CHANNELS, LANES), lambda i: (0, TILES - 1))
    return call(
        tails_body,
        jax.ShapeDtypeStruct((16, CHANNELS), BF16),
        [],
        4 * 10**6,
        200 * 1024,
        "tails",
        grid=(1,),
        in_specs=[last] * 3,
        out_specs=pl.BlockSpec((16, CHANNELS), lambda i: (0, 0)),
    )(q, k, v)


def rim_columns(rim):
    row = lax.broadcasted_iota(jnp.int32, (16, LANES), 0)
    col = lax.broadcasted_iota(jnp.int32, (16, LANES), 1)
    eye = (row == col).astype(BF16)
    return lax.dot_general(rim, eye, (((0,), (0,)), ((), ())), preferred_element_type=F32)


def short_conv(x, cols, rim, stream):
    lane = lax.broadcasted_iota(jnp.int32, x.shape, 1)
    older = rim[:, 2 * stream : 2 * stream + 1]
    newer = rim[:, 2 * stream + 1 : 2 * stream + 2]
    back1 = jnp.where(lane == 0, newer, pltpu.roll(x, 1, 1))
    back2 = jnp.where(lane == 0, older, jnp.where(lane == 1, newer, pltpu.roll(x, 2, 1)))
    tap = [cols[:, 3 * stream + i : 3 * stream + i + 1] for i in range(3)]
    return tap[0] * x + tap[1] * back1 + tap[2] * back2


def gate_body(k_ref, v_ref, rim_ref, cols_ref, gated_ref, out_ref, rim_cols, rows):
    rim_cols[...] = rim_columns(rim_ref[...])
    groups = ROWS // (2 * SEQ)
    for step in range(CHANNELS // ROWS):
        at = slice(step * ROWS, (step + 1) * ROWS)
        cols = cols_ref[at, :]
        rim = rim_cols[at, :]
        key = short_conv(k_ref[at, :].astype(F32), cols, rim, 1)
        value = short_conv(v_ref[at, :].astype(F32), cols, rim, 2)
        gated = (key * value).astype(BF16)
        gated_ref[at, :] = gated
        wide = gated.astype(F32)
        for c in range(TILES):
            rows[pl.ds(c, ROWS, stride=TILES), :] = wide[:, c * LANES : (c + 1) * LANES]
        message = rows[...].reshape(groups, SEQ, 2 * TILES, LANES).astype(BF16)
        for g in range(groups):
            out_ref[:, step * groups + g] = message[g]


def gate(k, v, rim, cols):
    return call(
        gate_body,
        (
            jax.ShapeDtypeStruct((CHANNELS, TOKENS), BF16),
            jax.ShapeDtypeStruct((SEQ, CH, 2 * TILES, LANES), BF16),
        ),
        [pltpu.VMEM((CHANNELS, LANES), F32), pltpu.VMEM((ROWS * TILES, LANES), F32)],
        10**7,
        2 * 1024 * 1024,
        "gate",
        in_specs=[VMEM] * 4,
        out_specs=(VMEM, VMEM),
    )(k, v, rim, cols)


def forward_chunk(at, signal, outer_ref, turn_ref, forward):
    section_real = dot(outer_ref[0, at, :], signal)
    section_imag = dot(outer_ref[1, at, :], signal)
    turn_real, turn_imag = turn_ref[0, at, :], turn_ref[1, at, :]
    spectra = []
    for j in range(2):
        half = slice(j * LANES, (j + 1) * LANES)
        real, imag = section_real[:, half], section_imag[:, half]
        turned = [real * turn_real - imag * turn_imag, imag * turn_real + real * turn_imag]
        spectra.append(dot(jnp.concatenate(turned, axis=1).astype(BF16), forward))
    return spectra


def filter_body(filt_ref, outer_ref, turn_ref, forward_ref, spec_ref):
    signal = jnp.concatenate([filt_ref[0], filt_ref[1]], axis=1)
    for step in range(OUTER // CHUNK):
        at = slice(step * CHUNK, (step + 1) * CHUNK)
        spectra = forward_chunk(at, signal, outer_ref, turn_ref, forward_ref[...])
        for j in range(2):
            spec_ref[j, at, :] = spectra[j] * (1.0 / LENGTH)


def filter_spectra(filt, outer, turn, forward):
    return call(
        filter_body,
        jax.ShapeDtypeStruct((2, OUTER, 2 * LANES), F32),
        [],
        14 * 10**8,
        8 * 1024 * 1024,
        "filter_spectra",
        in_specs=[VMEM] * 4,
        out_specs=VMEM,
    )(filt, outer, turn, forward)


def conv_body(
    arrived_ref, spec_ref, outer_ref, turn_ref, forward_ref, inverse_ref, out_ref, back_ref
):
    arrived = arrived_ref[...].astype(F32)
    halves = [arrived[:, j * TILES : (j + 1) * TILES, :].reshape(OUTER, LANES) for j in range(2)]
    signal = jnp.concatenate(halves, axis=1).astype(BF16)
    for step in range(OUTER // CHUNK):
        at = slice(step * CHUNK, (step + 1) * CHUNK)
        spectra = forward_chunk(at, signal, outer_ref, turn_ref, forward_ref[...])
        turn_real, turn_imag = turn_ref[0, at, :], turn_ref[1, at, :]
        for j in range(2):
            real, imag = spectra[j][:, :LANES], spectra[j][:, LANES:]
            filt_real, filt_imag = spec_ref[j, at, :LANES], spec_ref[j, at, LANES:]
            parts = [real * filt_real - imag * filt_imag, real * filt_imag + imag * filt_real]
            inner = dot(jnp.concatenate(parts, axis=1).astype(BF16), inverse_ref[...])
            real, imag = inner[:, :LANES], inner[:, LANES:]
            half = slice(j * LANES, (j + 1) * LANES)
            back_ref[0, at, half] = (real * turn_real + imag * turn_imag).astype(BF16)
            back_ref[1, at, half] = (imag * turn_real - real * turn_imag).astype(BF16)
    blocks = CHUNK // TILES
    for step in range(OUTER // CHUNK):
        at = slice(step * CHUNK, (step + 1) * CHUNK)
        result = dot(outer_ref[0, at, :], back_ref[0]) + dot(outer_ref[1, at, :], back_ref[1])
        halves = [
            result[:, j * LANES : (j + 1) * LANES].reshape(blocks, TILES, LANES) for j in range(2)
        ]
        out_ref[step * blocks : (step + 1) * blocks] = jnp.concatenate(halves, axis=1).astype(BF16)


def conv(arrived, spec, outer, turn, forward, inverse):
    return call(
        conv_body,
        jax.ShapeDtypeStruct((SEQ * CH, 2 * TILES, LANES), BF16),
        [pltpu.VMEM((2, OUTER, 2 * LANES), BF16)],
        28 * 10**8,
        8 * 1024 * 1024,
        "conv",
        in_specs=[VMEM] * 6,
        out_specs=VMEM,
    )(arrived, spec, outer, turn, forward, inverse)


def final_body(returned_ref, gated_ref, q_ref, rim_ref, cols_ref, out_ref, rim_cols, rows):
    rim_cols[...] = rim_columns(rim_ref[...])
    groups = ROWS // (2 * SEQ)
    per_group = ROWS * TILES // groups
    for step in range(CHANNELS // ROWS):
        at = slice(step * ROWS, (step + 1) * ROWS)
        cols = cols_ref[at, :]
        for g in range(groups):
            message = returned_ref[:, step * groups + g].astype(F32)
            rows[g * per_group : (g + 1) * per_group, :] = message.reshape(per_group, LANES)
        long_result = jnp.concatenate(
            [rows[pl.ds(c, ROWS, stride=TILES), :] for c in range(TILES)], axis=1
        )
        query = short_conv(q_ref[at, :].astype(F32), cols, rim_cols[at, :], 0)
        mixed = query * (long_result + cols[:, 9:10] * gated_ref[at, :].astype(F32))
        out_ref[at, :] = mixed.astype(BF16)


def final(returned, gated, q, rim, cols):
    return call(
        final_body,
        jax.ShapeDtypeStruct((CHANNELS, TOKENS), BF16),
        [pltpu.VMEM((CHANNELS, LANES), F32), pltpu.VMEM((ROWS * TILES, LANES), F32)],
        10**7,
        2 * 1024 * 1024,
        "final",
        in_specs=[VMEM] * 5,
        out_specs=VMEM,
    )(returned, gated, q, rim, cols)


def exchange(messages):
    flat = messages.reshape(SEQ * CH, 2 * TILES, LANES)
    return lax.all_to_all(flat, AXES, split_axis=0, concat_axis=0, tiled=True)


def shards(consts, query_stream, key_stream, value_stream, short_taps, long_filter, skip_gain):
    outer, turn, forward, inverse = (jnp.asarray(c) for c in consts)
    count = lax.axis_size("seq") * lax.axis_size("ch")
    ends = tails(query_stream, key_stream, value_stream)
    rim = lax.ppermute(ends, AXES, [(i, i + 1) for i in range(count - 1)])
    cols = jnp.concatenate([short_taps.reshape(9, CHANNELS), skip_gain[None]]).T
    gated, messages = gate(key_stream, value_stream, rim, cols)
    arrived = exchange(messages)
    spec = filter_spectra(long_filter.reshape(2, OUTER, LANES), outer, turn, forward)
    results = conv(arrived, spec, outer, turn, forward, inverse)
    returned = exchange(results).reshape(SEQ, CH, 2 * TILES, LANES)
    return final(returned, gated, query_stream, rim, cols)


def solution(mesh):
    tokens = P(None, AXES)
    placed = (tokens, tokens, tokens, P(), P("ch", "seq", None, None), P())
    return jax.shard_map(
        functools.partial(shards, tables()),
        mesh=mesh,
        in_specs=placed,
        out_specs=tokens,
        check_vma=False,
    )
```

```python
import functools
import math

import jax
import jax.numpy as jnp
import ml_dtypes
import numpy as np
from jax import lax
from jax.experimental import pallas as pl
from jax.experimental.pallas import tpu as pltpu
from jax.sharding import PartitionSpec as P

F32 = jnp.float32
BF16 = jnp.bfloat16
LANES = 128
TOKENS = 1024
TILES = TOKENS // LANES
BLOCKS = 128
LENGTH = BLOCKS * TOKENS
CHANNELS = 256
SEQ = 8
CH = 16
BODY = 2 * TILES
EDGE = 8
MESSAGE = BODY + EDGE
ROWS = 32
GROUPS = ROWS // (2 * SEQ)
STEPS = CHANNELS // ROWS
AXES = ("seq", "ch")
VMEM = pl.BlockSpec(memory_space=pltpu.VMEM)
HBM = pl.BlockSpec(memory_space=pltpu.HBM)


def tables():
    step = 2.0 * math.pi
    tile = np.arange(TILES)[:, None, None]
    k1 = np.arange(BLOCKS)[None, :, None]
    block = np.arange(BLOCKS)[None, None, :]
    phase = ((TILES * block + tile) * (4 * k1 + 1) % (4 * TOKENS)) * (step / (4 * TOKENS))
    outer = np.concatenate([np.cos(phase), -np.sin(phase)], axis=1)
    lane = np.arange(LANES)[None, :]
    phase = lane * (np.arange(BLOCKS)[:, None] + 0.25) * (step / LENGTH)
    turn = np.stack([np.cos(phase), -np.sin(phase)])
    lane = np.arange(LANES)[None, :, None]
    k2 = np.arange(LANES)[None, None, :]
    phase = (lane * (TILES * k2 + tile) % TOKENS) * (step / TOKENS)
    cos, sin = np.cos(phase), np.sin(phase)
    inner = np.concatenate(
        [np.concatenate([cos, -sin], axis=2), np.concatenate([sin, cos], axis=2)], axis=1
    )
    narrow = ml_dtypes.bfloat16
    return dict(
        outer=outer.astype(narrow),
        outer_back=outer.swapaxes(1, 2).astype(narrow),
        turn=turn.astype(np.float32),
        inner=inner.astype(narrow),
        inner_back=inner.swapaxes(1, 2).astype(narrow),
    )


def dot(left, right):
    return jnp.dot(left, right, preferred_element_type=F32)


def call(body, name, out_shape, scratch, in_specs, out_specs, flops, nbytes):
    return pl.pallas_call(
        body,
        out_shape=out_shape,
        in_specs=in_specs,
        out_specs=out_specs,
        scratch_shapes=scratch,
        compiler_params=pltpu.CompilerParams(vmem_limit_bytes=24 * 1024 * 1024),
        cost_estimate=pl.CostEstimate(flops=flops, bytes_accessed=nbytes, transcendentals=0),
        name=name,
    )


def shape(dims, dtype):
    return jax.ShapeDtypeStruct(dims, dtype)


def lanes_of(x):
    return lax.broadcasted_iota(jnp.int32, x.shape, 1)


def columns(rows, tap_rows):
    tap_rows[...] = jnp.zeros(tap_rows.shape, F32)
    at = 0
    for row in rows:
        tap_rows[at : at + row.shape[0], :] = row
        at += row.shape[0]
    return tap_rows[...].T


def split_conv(x, cols, first):
    taps = [cols[:, first + i : first + i + 1] for i in range(3)]
    back1 = pltpu.roll(x, 1, 1)
    back2 = pltpu.roll(x, 2, 1)
    whole = taps[0] * x + taps[1] * back1 + taps[2] * back2
    x, back1, back2 = (part[:, :LANES] for part in (x, back1, back2))
    lane = lanes_of(x)
    own = taps[0] * x + jnp.where(lane < 1, 0.0, taps[1] * back1)
    own = own + jnp.where(lane < 2, 0.0, taps[2] * back2)
    onward = jnp.where(lane < 1, taps[1] * back1, 0.0) + jnp.where(lane < 2, taps[2] * back2, 0.0)
    return jnp.concatenate([own, whole[:, LANES:]], axis=1), own, onward


def in_two(x):
    rest = x - x.astype(BF16).astype(F32)
    return jnp.where(lanes_of(x) < 2, x, pltpu.roll(rest, 2, 1))


def gate_body(
    k_ref, v_ref, taps_ref, gated_ref, first_ref, out_ref, k_buf, v_buf, tap_rows, cols_buf, rows, edge, sems
):
    copies = []
    for step in range(STEPS):
        at = pl.ds(step * ROWS, ROWS)
        copies.append(
            [
                pltpu.make_async_copy(ref.at[at], buf.at[at], sems.at[i, step])
                for i, (ref, buf) in enumerate(((k_ref, k_buf), (v_ref, v_buf)))
            ]
        )
    for pair in copies:
        for copy in pair:
            copy.start()
    cols_buf[...] = columns([taps_ref[1], taps_ref[2]], tap_rows)
    for step in range(STEPS):
        for copy in copies[step]:
            copy.wait()
        at = slice(step * ROWS, (step + 1) * ROWS)
        cols = cols_buf[at, :]
        key, key_own, key_onward = split_conv(k_buf[at, :].astype(F32), cols, 0)
        value, value_own, value_onward = split_conv(v_buf[at, :].astype(F32), cols, 3)
        gated = (key * value).astype(BF16)
        gated_ref[at, :] = gated
        first_ref[0, at, :] = key_own
        first_ref[1, at, :] = value_own
        wide = gated.astype(F32)
        for c in range(TILES):
            rows[pl.ds(c, ROWS, stride=TILES), :] = wide[:, c * LANES : (c + 1) * LANES]
        for m, part in enumerate((key_own, value_own, key_onward, value_onward)):
            edge[pl.ds(m, ROWS, stride=4), :] = in_two(part)
        body = rows[...].reshape(ROWS // 2, BODY, LANES)
        message = jnp.concatenate([body, edge[...].reshape(ROWS // 2, EDGE, LANES)], axis=1)
        message = message.astype(BF16)
        for g in range(GROUPS):
            out_ref[:, step * GROUPS + g] = message[g * SEQ : (g + 1) * SEQ]


def gate(k, v, taps):
    return call(
        gate_body,
        "gate",
        (
            shape((CHANNELS, TOKENS), BF16),
            shape((2, CHANNELS, LANES), F32),
            shape((SEQ, CH, MESSAGE, LANES), BF16),
        ),
        [
            pltpu.VMEM((CHANNELS, TOKENS), BF16),
            pltpu.VMEM((CHANNELS, TOKENS), BF16),
            pltpu.VMEM((LANES, CHANNELS), F32),
            pltpu.VMEM((CHANNELS, LANES), F32),
            pltpu.VMEM((ROWS * TILES, LANES), F32),
            pltpu.VMEM((ROWS * 4, LANES), F32),
            pltpu.SemaphoreType.DMA((2, STEPS)),
        ],
        [HBM, HBM, VMEM],
        (VMEM, VMEM, VMEM),
        10**7,
        2 * 1024 * 1024,
    )(k, v, taps)


def eight_points(re, im):
    half = math.sqrt(0.5)
    out_re, out_im = [None] * 8, [None] * 8

    def four_points(re, im, first):
        sum_re = [re[i] + re[i + 2] for i in range(2)]
        sum_im = [im[i] + im[i + 2] for i in range(2)]
        dif_re = [re[i] - re[i + 2] for i in range(2)]
        dif_im = [im[i] - im[i + 2] for i in range(2)]
        out_re[first], out_im[first] = sum_re[0] + sum_re[1], sum_im[0] + sum_im[1]
        out_re[first + 4], out_im[first + 4] = sum_re[0] - sum_re[1], sum_im[0] - sum_im[1]
        out_re[first + 2], out_im[first + 2] = dif_re[0] + dif_im[1], dif_im[0] - dif_re[1]
        out_re[first + 6], out_im[first + 6] = dif_re[0] - dif_im[1], dif_im[0] + dif_re[1]

    four_points([re[i] + re[i + 4] for i in range(4)], [im[i] + im[i + 4] for i in range(4)], 0)
    re = [re[i] - re[i + 4] for i in range(4)]
    im = [im[i] - im[i + 4] for i in range(4)]
    turned_re = [re[0], (re[1] + im[1]) * half, im[2], (im[3] - re[3]) * half]
    turned_im = [im[0], (im[1] - re[1]) * half, -re[2], (re[3] + im[3]) * -half]
    four_points(turned_re, turned_im, 1)
    return out_re, out_im


def forward(signals, outer_ref, turn_ref, section, turned):
    for c in range(TILES):
        section[c] = dot(outer_ref[c], signals[c])
    for row in range(0, BLOCKS, 16):
        turn_re, turn_im = turn_ref[0, row : row + 16, :], turn_ref[1, row : row + 16, :]
        for j in range(2):
            half = slice(j * LANES, (j + 1) * LANES)
            re = [section[c, row : row + 16, half] for c in range(TILES)]
            im = [section[c, BLOCKS + row : BLOCKS + row + 16, half] for c in range(TILES)]
            re, im = eight_points(re, im)
            at = slice(j * BLOCKS + row, j * BLOCKS + row + 16)
            for kc in range(TILES):
                turned[kc, at, :LANES] = (re[kc] * turn_re - im[kc] * turn_im).astype(BF16)
                turned[kc, at, LANES:] = (re[kc] * turn_im + im[kc] * turn_re).astype(BF16)


def filter_body(
    filt_ref, outer_ref, turn_ref, inner_ref, q_ref, k_ref, v_ref, gated_ref, spec_ref, ends_ref,
    rows, section, turned, last, sems
):
    del gated_ref
    copies = [
        pltpu.make_async_copy(
            ref.at[:, pl.ds(TOKENS - LANES, LANES)], last.at[i], sems.at[i]
        )
        for i, ref in enumerate((q_ref, k_ref, v_ref))
    ]
    for copy in copies:
        copy.start()
    rows[...] = filt_ref[...].astype(F32).reshape(2 * BLOCKS * TILES, LANES)
    signals = []
    for c in range(TILES):
        halves = [rows[pl.ds(j * TOKENS + c, BLOCKS, stride=TILES), :] for j in range(2)]
        signals.append(jnp.concatenate(halves, axis=1).astype(BF16))
    forward(signals, outer_ref, turn_ref, section, turned)
    for kc in range(TILES):
        spec_ref[kc] = dot(turned[kc], inner_ref[kc]) * (1.0 / LENGTH)
    row = lax.broadcasted_iota(jnp.int32, (16, LANES), 0)
    lane = lax.broadcasted_iota(jnp.int32, (16, LANES), 1)
    total = jnp.zeros((16, CHANNELS), F32)
    for i in range(3):
        copies[i].wait()
        pick = (row - 2 * i == lane - (LANES - 2)) & (lane >= LANES - 2)
        total += lax.dot_general(
            pick.astype(BF16), last[i], (((1,), (1,)), ((), ())), preferred_element_type=F32
        )
    ends_ref[...] = total.astype(BF16)


def filter_spectra(filt, consts, q, k, v, gated):
    return call(
        filter_body,
        "filter_spectra",
        (shape((TILES, 2 * BLOCKS, 2 * LANES), F32), shape((16, CHANNELS), BF16)),
        [
            pltpu.VMEM((2 * BLOCKS * TILES, LANES), F32),
            pltpu.VMEM((TILES, 2 * BLOCKS, 2 * LANES), F32),
            pltpu.VMEM((TILES, 2 * BLOCKS, 2 * LANES), BF16),
            pltpu.VMEM((3, CHANNELS, LANES), BF16),
            pltpu.SemaphoreType.DMA((3,)),
        ],
        [VMEM, VMEM, VMEM, VMEM, HBM, HBM, HBM, pl.BlockSpec(memory_space=pl.ANY)],
        (VMEM, VMEM),
        10**9,
        8 * 1024 * 1024,
    )(filt, consts["outer"], consts["turn"], consts["inner"], q, k, v, gated)


def conv_body(
    arrived_ref, spec_ref, outer_ref, outer_back_ref, turn_ref, inner_ref, inner_back_ref, out_ref,
    rows, section, turned, back
):
    rows[:MESSAGE, :] = jnp.zeros((MESSAGE, LANES), F32)
    rows[MESSAGE:, :] = arrived_ref[...].astype(F32).reshape(BLOCKS * MESSAGE, LANES)

    def picked(row, before=0):
        return rows[pl.ds((1 - before) * MESSAGE + row, BLOCKS, stride=MESSAGE), :]

    def edge(j, m, before):
        part = picked(BODY + 4 * j + m, before)
        return part + pltpu.roll(part, LANES - 2, 1)

    signals = []
    for c in range(TILES):
        halves = [picked(j * TILES + c) for j in range(2)]
        if c == 0:
            for j in range(2):
                key = edge(j, 0, 0) + edge(j, 2, 1)
                value = edge(j, 1, 0) + edge(j, 3, 1)
                halves[j] = jnp.where(lanes_of(key) < 2, key * value, halves[j])
        signals.append(jnp.concatenate(halves, axis=1).astype(BF16))
    forward(signals, outer_ref, turn_ref, section, turned)
    for kc in range(TILES):
        spectrum = dot(turned[kc], inner_ref[kc])
        re, im = spectrum[:, :LANES], spectrum[:, LANES:]
        filt_re, filt_im = spec_ref[kc, :, :LANES], spec_ref[kc, :, LANES:]
        parts = [re * filt_re - im * filt_im, re * filt_im + im * filt_re]
        section[kc] = dot(jnp.concatenate(parts, axis=1).astype(BF16), inner_back_ref[kc])
    for row in range(0, BLOCKS, 16):
        turn_re, turn_im = turn_ref[0, row : row + 16, :], turn_ref[1, row : row + 16, :]
        for j in range(2):
            at = slice(j * BLOCKS + row, j * BLOCKS + row + 16)
            re, im = [], []
            for kc in range(TILES):
                part_re, part_im = section[kc, at, :LANES], section[kc, at, LANES:]
                re.append(part_re * turn_re + part_im * turn_im)
                im.append(part_im * turn_re - part_re * turn_im)
            im, re = eight_points(im, re)
            half = slice(j * LANES, (j + 1) * LANES)
            for c in range(TILES):
                back[c, row : row + 16, half] = re[c].astype(BF16)
                back[c, BLOCKS + row : BLOCKS + row + 16, half] = im[c].astype(BF16)
    for c in range(TILES):
        result = dot(outer_back_ref[c], back[c])
        for j in range(2):
            rows[pl.ds(j * TILES + c, BLOCKS, stride=BODY), :] = result[:, j * LANES : (j + 1) * LANES]
    out_ref[...] = rows[: BLOCKS * BODY, :].reshape(BLOCKS, BODY, LANES).astype(BF16)


def conv(arrived, spec, consts):
    names = ("outer", "outer_back", "turn", "inner", "inner_back")
    return call(
        conv_body,
        "conv",
        shape((BLOCKS, BODY, LANES), BF16),
        [
            pltpu.VMEM(((BLOCKS + 1) * MESSAGE, LANES), F32),
            pltpu.VMEM((TILES, 2 * BLOCKS, 2 * LANES), F32),
            pltpu.VMEM((TILES, 2 * BLOCKS, 2 * LANES), BF16),
            pltpu.VMEM((TILES, 2 * BLOCKS, 2 * LANES), BF16),
        ],
        [VMEM] * 7,
        VMEM,
        10**9,
        8 * 1024 * 1024,
    )(arrived, spec, *(consts[name] for name in names))


def direct_body(
    q_ref, gated_ref, first_ref, rim_ref, taps_ref, skip_ref, query_ref, direct_ref, tap_rows, cols_buf, rim_buf
):
    cols_buf[...] = columns([taps_ref[0], taps_ref[1], taps_ref[2], skip_ref[...]], tap_rows)
    tap_rows[:16, :] = rim_ref[...].astype(F32)
    rim_buf[...] = tap_rows[...].T
    for step in range(STEPS):
        at = slice(step * ROWS, (step + 1) * ROWS)
        cols, rim = cols_buf[at, :], rim_buf[at, :]
        lane = lax.broadcasted_iota(jnp.int32, (ROWS, LANES), 1)

        def before(stream):
            older, newer = rim[:, 2 * stream : 2 * stream + 1], rim[:, 2 * stream + 1 : 2 * stream + 2]
            one, two = cols[:, 3 * stream + 1 : 3 * stream + 2], cols[:, 3 * stream + 2 : 3 * stream + 3]
            return jnp.where(
                lane == 0, one * newer + two * older, jnp.where(lane == 1, two * newer, 0.0)
            )

        query, query_own, _ = split_conv(q_ref[at, :].astype(F32), cols, 0)
        query_ref[at, :] = query
        query_ref[at, :LANES] = query_own + before(0)
        skip = cols[:, 9:10]
        direct_ref[at, :] = skip * gated_ref[at, :].astype(F32)
        start = (first_ref[0, at, :] + before(1)) * (first_ref[1, at, :] + before(2))
        direct_ref[at, :LANES] = skip * start.astype(BF16).astype(F32)


def direct(q, gated, first, rim, taps, skip):
    return call(
        direct_body,
        "direct",
        (shape((CHANNELS, TOKENS), F32), shape((CHANNELS, TOKENS), F32)),
        [
            pltpu.VMEM((LANES, CHANNELS), F32),
            pltpu.VMEM((CHANNELS, LANES), F32),
            pltpu.VMEM((CHANNELS, LANES), F32),
        ],
        [VMEM] * 6,
        (VMEM, VMEM),
        10**7,
        4 * 1024 * 1024,
    )(q, gated, first, rim, taps, skip)


def final_body(returned_ref, query_ref, direct_ref, out_ref, rows, out_buf, sems):
    per_group = ROWS * TILES // GROUPS
    copies = []
    for step in range(STEPS):
        at = slice(step * ROWS, (step + 1) * ROWS)
        for g in range(GROUPS):
            message = returned_ref[:, step * GROUPS + g].astype(F32)
            rows[g * per_group : (g + 1) * per_group, :] = message.reshape(per_group, LANES)
        for c in range(TILES):
            lanes = slice(c * LANES, (c + 1) * LANES)
            long_result = rows[pl.ds(c, ROWS, stride=TILES), :]
            mixed = query_ref[at, lanes] * (long_result + direct_ref[at, lanes])
            out_buf[at, lanes] = mixed.astype(BF16)
        place = pl.ds(step * ROWS, ROWS)
        copies.append(pltpu.make_async_copy(out_buf.at[place], out_ref.at[place], sems.at[step]))
        copies[-1].start()
    for copy in copies:
        copy.wait()


def final(returned, query, direct_term):
    return call(
        final_body,
        "final",
        shape((CHANNELS, TOKENS), BF16),
        [
            pltpu.VMEM((ROWS * TILES, LANES), F32),
            pltpu.VMEM((CHANNELS, TOKENS), BF16),
            pltpu.SemaphoreType.DMA((STEPS,)),
        ],
        [VMEM] * 3,
        HBM,
        10**6,
        2 * 1024 * 1024,
    )(returned, query, direct_term)


def exchange(messages):
    return lax.all_to_all(messages, AXES, split_axis=0, concat_axis=0, tiled=True)


def shards(consts, q, k, v, short_taps, long_filter, skip_gain):
    consts = {name: jnp.asarray(table) for name, table in consts.items()}
    count = lax.axis_size("seq") * lax.axis_size("ch")
    gated, first, messages = gate(k, v, short_taps)
    arrived = exchange(messages.reshape(BLOCKS, MESSAGE, LANES))
    filt = long_filter.reshape(2, BLOCKS * TILES, LANES)
    spec, ends = filter_spectra(filt, consts, q, k, v, gated)
    rim = lax.ppermute(ends, AXES, [(i, i + 1) for i in range(count - 1)])
    query, direct_term = direct(q, gated, first, rim, short_taps, skip_gain[None])
    results = conv(arrived, spec, consts)
    returned = exchange(results).reshape(SEQ, CH, BODY, LANES)
    return final(returned, query, direct_term)


def solution(mesh):
    tokens = P(None, AXES)
    placed = (tokens, tokens, tokens, P(), P("ch", "seq", None, None), P())
    return jax.shard_map(
        functools.partial(shards, tables()),
        mesh=mesh,
        in_specs=placed,
        out_specs=tokens,
        check_vma=False,
    )
```

```python
import functools
import math

import jax
import jax.numpy as jnp
import ml_dtypes
import numpy as np
from jax import lax
from jax.experimental import pallas as pl
from jax.experimental.pallas import tpu as pltpu
from jax.sharding import PartitionSpec as P

F32 = jnp.float32
BF16 = jnp.bfloat16
LANES = 128
TOKENS = 1024
TILES = TOKENS // LANES
BLOCKS = 128
LENGTH = BLOCKS * TOKENS
CHANNELS = 256
SEQ = 8
CH = 16
BODY = 2 * TILES
EDGE = 8
GATE_LIMIT, BESIDE_LIMIT, CONV_LIMIT, FINAL_LIMIT = 60, 16, 16, 16
MESSAGE = BODY + EDGE
ROWS = 64
GROUPS = ROWS // (2 * SEQ)
STEPS = CHANNELS // ROWS
AXES = ("seq", "ch")
VMEM = pl.BlockSpec(memory_space=pltpu.VMEM)
HBM = pl.BlockSpec(memory_space=pltpu.HBM)


def tables():
    step = 2.0 * math.pi
    tile = np.arange(TILES)[:, None, None]
    k1 = np.arange(BLOCKS)[None, :, None]
    block = np.arange(BLOCKS)[None, None, :]
    phase = ((TILES * block + tile) * (4 * k1 + 1) % (4 * TOKENS)) * (step / (4 * TOKENS))
    outer = np.concatenate([np.cos(phase), -np.sin(phase)], axis=1)
    lane = np.arange(LANES)[None, :]
    phase = lane * (np.arange(BLOCKS)[:, None] + 0.25) * (step / LENGTH)
    turn = np.stack([np.cos(phase), -np.sin(phase)])
    lane = np.arange(LANES)[None, :, None]
    k2 = np.arange(LANES)[None, None, :]
    phase = (lane * (TILES * k2 + tile) % TOKENS) * (step / TOKENS)
    cos, sin = np.cos(phase), np.sin(phase)
    inner = np.concatenate(
        [np.concatenate([cos, -sin], axis=2), np.concatenate([sin, cos], axis=2)], axis=1
    )
    narrow = ml_dtypes.bfloat16
    return dict(
        outer=outer.astype(narrow),
        outer_back=outer.swapaxes(1, 2).astype(narrow),
        turn=turn.astype(np.float32),
        inner=inner.astype(narrow),
    )


def dot(left, right):
    return jnp.dot(left, right, preferred_element_type=F32)


def dot_back(left, right):
    dims = (((1,), (1,)), ((), ()))
    return lax.dot_general(left, right, dims, preferred_element_type=F32)


def call(body, name, out_shape, scratch, in_specs, out_specs, flops, nbytes, limit=16):
    return pl.pallas_call(
        body,
        out_shape=out_shape,
        in_specs=in_specs,
        out_specs=out_specs,
        scratch_shapes=scratch,
        compiler_params=pltpu.CompilerParams(vmem_limit_bytes=limit * 1024 * 1024),
        cost_estimate=pl.CostEstimate(flops=flops, bytes_accessed=nbytes, transcendentals=0),
        name=name,
    )


def shape(dims, dtype):
    return jax.ShapeDtypeStruct(dims, dtype)


def lanes_of(x):
    return lax.broadcasted_iota(jnp.int32, x.shape, 1)


def columns(rows, tap_rows):
    tap_rows[...] = jnp.zeros(tap_rows.shape, F32)
    at = 0
    for row in rows:
        tap_rows[at : at + row.shape[0], :] = row
        at += row.shape[0]
    return tap_rows[...].T


def taps_of(cols, stream):
    return [cols[:, 3 * stream + i : 3 * stream + i + 1] for i in range(3)]


def causal(x, taps):
    return taps[0] * x + taps[1] * pltpu.roll(x, 1, 1) + taps[2] * pltpu.roll(x, 2, 1)


def with_edges(x, taps):
    back1, back2 = pltpu.roll(x, 1, 1), pltpu.roll(x, 2, 1)
    sums = taps[0] * x + taps[1] * back1 + taps[2] * back2
    lane = lax.broadcasted_iota(jnp.int32, (x.shape[0], LANES), 1)
    near = jnp.where(lane < 1, back1[:, :LANES], 0.0)
    far = jnp.where(lane < 2, back2[:, :LANES], 0.0)
    onward = taps[1] * near + taps[2] * far
    return sums, sums[:, :LANES] - onward, onward


def gate_body(
    q_ref, k_ref, v_ref, taps_ref, skip_ref, out_ref,
    taps_buf, skip_buf, q_buf, k_buf, v_buf, out_buf, tap_rows, cols_buf, rows, edge, small, sems, out_sems
):
    def small_copies():
        pairs = [(taps_ref, taps_buf), (skip_ref, skip_buf)]
        pairs += [
            (q_ref.at[:, pl.ds(i * (TOKENS - LANES), LANES)], q_buf.at[i]) for i in range(2)
        ]
        return [pltpu.make_async_copy(a, b, small.at[i]) for i, (a, b) in enumerate(pairs)]

    copies = []
    for step in range(STEPS):
        at = pl.ds(step * ROWS, ROWS)
        copies.append(
            [
                pltpu.make_async_copy(ref.at[at], buf.at[at], sems.at[i, step])
                for i, (ref, buf) in enumerate(((k_ref, k_buf), (v_ref, v_buf)))
            ]
        )
    first = small_copies()
    for copy in first:
        copy.start()
    for pair in copies:
        for copy in pair:
            copy.start()
    for copy in first:
        copy.wait()
    cols_buf[...] = columns([taps_buf[0], taps_buf[1], taps_buf[2], skip_buf[...]], tap_rows)
    out_copies = []
    for step in range(STEPS):
        for copy in copies[step]:
            copy.wait()
        at = slice(step * ROWS, (step + 1) * ROWS)
        cols = cols_buf[at, :]
        query_taps, key_taps, value_taps = (taps_of(cols, stream) for stream in range(3))
        key, key_own, key_onward = with_edges(k_buf[at, :].astype(F32), key_taps)
        value, value_own, value_onward = with_edges(v_buf[at, :].astype(F32), value_taps)
        query = jnp.concatenate([q_buf[0, at, :], q_buf[1, at, :]], axis=1).astype(F32)
        _, query_own, query_onward = with_edges(query, query_taps)
        gated = key * value
        for c in range(TILES):
            rows[pl.ds(c, ROWS, stride=TILES), :] = gated[:, c * LANES : (c + 1) * LANES]
        lane = lanes_of(key_own)
        parts = (
            jnp.where(lane < 2, key_own, pltpu.roll(query_own, 2, 1)),
            jnp.where(lane < 2, value_own, cols[:, 9:10]),
            jnp.where(lane < 2, key_onward, pltpu.roll(query_onward, 2, 1)),
            value_onward,
        )
        for m, part in enumerate(parts):
            edge[pl.ds(m, ROWS, stride=4), :] = part
        body = rows[...].reshape(ROWS // 2, BODY, LANES)
        message = jnp.concatenate([body, edge[...].reshape(ROWS // 2, EDGE, LANES)], axis=1)
        message = message.astype(BF16)
        for g in range(GROUPS):
            out_buf[:, step * GROUPS + g] = message[g * SEQ : (g + 1) * SEQ]
        place = pl.ds(step * GROUPS, GROUPS)
        out_copies.append(
            pltpu.make_async_copy(out_buf.at[:, place], out_ref.at[:, place], out_sems.at[step])
        )
        out_copies[-1].start()
    for copy in out_copies:
        copy.wait()


def gate(q, k, v, taps, skip):
    return call(
        gate_body,
        "gate",
        shape((SEQ, CH, MESSAGE, LANES), BF16),
        [
            pltpu.VMEM((3, 3, CHANNELS), F32),
            pltpu.VMEM((1, CHANNELS), F32),
            pltpu.VMEM((2, CHANNELS, LANES), BF16),
            pltpu.VMEM((CHANNELS, TOKENS), BF16),
            pltpu.VMEM((CHANNELS, TOKENS), BF16),
            pltpu.VMEM((SEQ, CH, MESSAGE, LANES), BF16),
            pltpu.VMEM((LANES, CHANNELS), F32),
            pltpu.VMEM((CHANNELS, LANES), F32),
            pltpu.VMEM((ROWS * TILES, LANES), F32),
            pltpu.VMEM((ROWS * 4, LANES), F32),
            pltpu.SemaphoreType.DMA((4,)),
            pltpu.SemaphoreType.DMA((2, STEPS)),
            pltpu.SemaphoreType.DMA((STEPS,)),
        ],
        [HBM] * 5,
        HBM,
        10**7,
        2 * 1024 * 1024,
        GATE_LIMIT,
    )(q, k, v, taps, skip)


def eight_points(re, im):
    half = math.sqrt(0.5)
    out_re, out_im = [None] * 8, [None] * 8

    def four_points(re, im, first):
        sum_re = [re[i] + re[i + 2] for i in range(2)]
        sum_im = [im[i] + im[i + 2] for i in range(2)]
        dif_re = [re[i] - re[i + 2] for i in range(2)]
        dif_im = [im[i] - im[i + 2] for i in range(2)]
        out_re[first], out_im[first] = sum_re[0] + sum_re[1], sum_im[0] + sum_im[1]
        out_re[first + 4], out_im[first + 4] = sum_re[0] - sum_re[1], sum_im[0] - sum_im[1]
        out_re[first + 2], out_im[first + 2] = dif_re[0] + dif_im[1], dif_im[0] - dif_re[1]
        out_re[first + 6], out_im[first + 6] = dif_re[0] - dif_im[1], dif_im[0] + dif_re[1]

    four_points([re[i] + re[i + 4] for i in range(4)], [im[i] + im[i + 4] for i in range(4)], 0)
    re = [re[i] - re[i + 4] for i in range(4)]
    im = [im[i] - im[i + 4] for i in range(4)]
    turned_re = [re[0], (re[1] + im[1]) * half, im[2], (im[3] - re[3]) * half]
    turned_im = [im[0], (im[1] - re[1]) * half, -re[2], (re[3] + im[3]) * -half]
    four_points(turned_re, turned_im, 1)
    return out_re, out_im


def forward(signals, outer_ref, turn_ref, section, turned):
    for c in range(TILES):
        section[c] = dot(outer_ref[c], signals[c])
    for row in range(0, BLOCKS, 16):
        turn_re, turn_im = turn_ref[0, row : row + 16, :], turn_ref[1, row : row + 16, :]
        for j in range(2):
            half = slice(j * LANES, (j + 1) * LANES)
            re = [section[c, row : row + 16, half] for c in range(TILES)]
            im = [section[c, BLOCKS + row : BLOCKS + row + 16, half] for c in range(TILES)]
            re, im = eight_points(re, im)
            at = slice(j * BLOCKS + row, j * BLOCKS + row + 16)
            for kc in range(TILES):
                turned[kc, at, :LANES] = (re[kc] * turn_re - im[kc] * turn_im).astype(BF16)
                turned[kc, at, LANES:] = (re[kc] * turn_im + im[kc] * turn_re).astype(BF16)


def beside_body(
    filt_ref, outer_ref, turn_ref, inner_ref, outer_back_ref, q_ref, k_ref, v_ref, taps_ref, skip_ref,
    spec_ref, query_ref, direct_ref, rows, section, turned, tap_rows, cols_buf
):
    del outer_back_ref
    rows[...] = filt_ref[...].astype(F32).reshape(2 * BLOCKS * TILES, LANES)
    signals = []
    for c in range(TILES):
        halves = [rows[pl.ds(j * TOKENS + c, BLOCKS, stride=TILES), :] for j in range(2)]
        signals.append(jnp.concatenate(halves, axis=1).astype(BF16))
    forward(signals, outer_ref, turn_ref, section, turned)
    for kc in range(TILES):
        spec_ref[kc] = (dot(turned[kc], inner_ref[kc]) * (1.0 / LENGTH)).astype(BF16)
    cols_buf[...] = columns([taps_ref[0], taps_ref[1], taps_ref[2], skip_ref[...]], tap_rows)
    for step in range(STEPS):
        at = slice(step * ROWS, (step + 1) * ROWS)
        cols = cols_buf[at, :]
        query, key, value = (
            causal(ref[at, :].astype(F32), taps_of(cols, stream))
            for stream, ref in enumerate((q_ref, k_ref, v_ref))
        )
        query_ref[at, :] = query
        direct_ref[at, :] = cols[:, 9:10] * (key * value).astype(BF16).astype(F32)


def beside(filt, consts, q, k, v, taps, skip):
    names = ("outer", "turn", "inner", "outer_back")
    return call(
        beside_body,
        "beside",
        (
            shape((TILES, 2 * BLOCKS, 2 * LANES), BF16),
            shape((CHANNELS, TOKENS), F32),
            shape((CHANNELS, TOKENS), F32),
        ),
        [
            pltpu.VMEM((2 * BLOCKS * TILES, LANES), F32),
            pltpu.VMEM((TILES, 2 * BLOCKS, 2 * LANES), F32),
            pltpu.VMEM((TILES, 2 * BLOCKS, 2 * LANES), BF16),
            pltpu.VMEM((LANES, CHANNELS), F32),
            pltpu.VMEM((CHANNELS, LANES), F32),
        ],
        [VMEM] * 10,
        (VMEM,) * 3,
        10**9,
        8 * 1024 * 1024,
        BESIDE_LIMIT,
    )(filt, *(consts[name] for name in names), q, k, v, taps, skip)


def conv_body(
    arrived_ref, spec_ref, outer_ref, outer_back_ref, turn_ref, inner_ref, out_ref,
    rows, section, turned, back, edges
):
    rows[:MESSAGE, :] = jnp.zeros((MESSAGE, LANES), F32)
    rows[MESSAGE:, :] = arrived_ref[...].astype(F32).reshape(BLOCKS * MESSAGE, LANES)

    def picked(row, before=0):
        return rows[pl.ds((1 - before) * MESSAGE + row, BLOCKS, stride=MESSAGE), :]

    signals = []
    for c in range(TILES):
        halves = [picked(j * TILES + c) for j in range(2)]
        if c == 0:
            for j in range(2):
                edge = BODY + 4 * j
                key_query = picked(edge) + picked(edge + 2, 1)
                value_skip = picked(edge + 1) + picked(edge + 3, 1)
                gated = (key_query * value_skip).astype(BF16).astype(F32)
                edges[0, j] = pltpu.roll(key_query, LANES - 2, 1)
                edges[1, j] = pltpu.roll(value_skip, LANES - 2, 1) * gated
                halves[j] = jnp.where(lanes_of(gated) < 2, gated, halves[j])
        signals.append(jnp.concatenate(halves, axis=1).astype(BF16))
    forward(signals, outer_ref, turn_ref, section, turned)
    for kc in range(TILES):
        spectrum = dot(turned[kc], inner_ref[kc])
        re, im = spectrum[:, :LANES], spectrum[:, LANES:]
        spec = spec_ref[kc].astype(F32)
        filt_re, filt_im = spec[:, :LANES], spec[:, LANES:]
        parts = [re * filt_re - im * filt_im, re * filt_im + im * filt_re]
        section[kc] = dot_back(jnp.concatenate(parts, axis=1).astype(BF16), inner_ref[kc])
    for row in range(0, BLOCKS, 16):
        turn_re, turn_im = turn_ref[0, row : row + 16, :], turn_ref[1, row : row + 16, :]
        for j in range(2):
            at = slice(j * BLOCKS + row, j * BLOCKS + row + 16)
            re, im = [], []
            for kc in range(TILES):
                part_re, part_im = section[kc, at, :LANES], section[kc, at, LANES:]
                re.append(part_re * turn_re + part_im * turn_im)
                im.append(part_im * turn_re - part_re * turn_im)
            im, re = eight_points(im, re)
            half = slice(j * LANES, (j + 1) * LANES)
            for c in range(TILES):
                back[c, row : row + 16, half] = re[c].astype(BF16)
                back[c, BLOCKS + row : BLOCKS + row + 16, half] = im[c].astype(BF16)
    for c in range(TILES):
        result = dot(outer_back_ref[c], back[c])
        for j in range(2):
            half = result[:, j * LANES : (j + 1) * LANES]
            if c == 0:
                start = edges[0, j] * (half.astype(BF16).astype(F32) + edges[1, j])
                half = jnp.where(lanes_of(half) < 2, start, half)
            rows[pl.ds(j * TILES + c, BLOCKS, stride=BODY), :] = half
    out_ref[...] = rows[: BLOCKS * BODY, :].reshape(BLOCKS, BODY, LANES).astype(BF16)


def conv(arrived, spec, consts):
    names = ("outer", "outer_back", "turn", "inner")
    return call(
        conv_body,
        "conv",
        shape((BLOCKS, BODY, LANES), BF16),
        [
            pltpu.VMEM(((BLOCKS + 1) * MESSAGE, LANES), F32),
            pltpu.VMEM((TILES, 2 * BLOCKS, 2 * LANES), F32),
            pltpu.VMEM((TILES, 2 * BLOCKS, 2 * LANES), BF16),
            pltpu.VMEM((TILES, 2 * BLOCKS, 2 * LANES), BF16),
            pltpu.VMEM((2, 2, BLOCKS, LANES), F32),
        ],
        [VMEM] * 6,
        VMEM,
        10**9,
        8 * 1024 * 1024,
        CONV_LIMIT,
    )(arrived, spec, *(consts[name] for name in names))


def final_body(returned_ref, query_ref, direct_ref, out_ref, rows, out_buf, sems):
    per_group = ROWS * TILES // GROUPS
    copies = []
    for step in range(STEPS):
        at = slice(step * ROWS, (step + 1) * ROWS)
        for g in range(GROUPS):
            message = returned_ref[:, step * GROUPS + g].astype(F32)
            rows[g * per_group : (g + 1) * per_group, :] = message.reshape(per_group, LANES)
        for c in range(TILES):
            lanes = slice(c * LANES, (c + 1) * LANES)
            long_result = rows[pl.ds(c, ROWS, stride=TILES), :]
            mixed = query_ref[at, lanes] * (long_result + direct_ref[at, lanes])
            if c == 0:
                mixed = jnp.where(lanes_of(mixed) < 2, long_result, mixed)
            out_buf[at, lanes] = mixed.astype(BF16)
        place = pl.ds(step * ROWS, ROWS)
        copies.append(pltpu.make_async_copy(out_buf.at[place], out_ref.at[place], sems.at[step]))
        copies[-1].start()
    for copy in copies:
        copy.wait()


def final(returned, query, direct_term):
    return call(
        final_body,
        "final",
        shape((CHANNELS, TOKENS), BF16),
        [
            pltpu.VMEM((ROWS * TILES, LANES), F32),
            pltpu.VMEM((CHANNELS, TOKENS), BF16),
            pltpu.SemaphoreType.DMA((STEPS,)),
        ],
        [VMEM] * 3,
        HBM,
        10**6,
        2 * 1024 * 1024,
        FINAL_LIMIT,
    )(returned, query, direct_term)


def exchange(messages):
    return lax.all_to_all(messages, AXES, split_axis=0, concat_axis=0, tiled=True)


def shards(consts, q, k, v, short_taps, long_filter, skip_gain):
    consts = {name: jnp.asarray(table) for name, table in consts.items()}
    skip = skip_gain[None]
    messages = gate(q, k, v, short_taps, skip)
    messages, q, k, v, long_filter = lax.optimization_barrier((messages, q, k, v, long_filter))
    arrived = exchange(messages.reshape(BLOCKS, MESSAGE, LANES))
    filt = long_filter.reshape(2, BLOCKS * TILES, LANES)
    spec, query, direct_term = beside(filt, consts, q, k, v, short_taps, skip)
    results = conv(arrived, spec, consts)
    returned = exchange(results).reshape(SEQ, CH, BODY, LANES)
    return final(returned, query, direct_term)


def solution(mesh):
    tokens = P(None, AXES)
    placed = (tokens, tokens, tokens, P(), P("ch", "seq", None, None), P())
    return jax.shard_map(
        functools.partial(shards, tables()),
        mesh=mesh,
        in_specs=placed,
        out_specs=tokens,
        check_vma=False,
    )
```

```python
import functools
import math

import jax
import jax.numpy as jnp
import ml_dtypes
import numpy as np
from jax import lax
from jax.experimental import pallas as pl
from jax.experimental.pallas import tpu as pltpu
from jax.sharding import PartitionSpec as P

F32 = jnp.float32
BF16 = jnp.bfloat16
LANES = 128
TOKENS = 1024
TILES = TOKENS // LANES
BLOCKS = 128
LENGTH = BLOCKS * TOKENS
CHANNELS = 256
SEQ = 8
CH = 16
BODY = 2 * TILES
WIDTH = TILES + 1
GATE_LIMIT, BESIDE_LIMIT, CONV_LIMIT, FINAL_LIMIT = 60, 60, 51, 16
ROWS = 64
STEPS = CHANNELS // ROWS
AXES = ("seq", "ch")
OWNERS = ("ch", "seq")
VMEM = pl.BlockSpec(memory_space=pltpu.VMEM)
HBM = pl.BlockSpec(memory_space=pltpu.HBM)


def tables():
    step = 2.0 * math.pi
    tile = np.arange(TILES)[:, None, None]
    k1 = np.arange(BLOCKS)[None, :, None]
    block = np.arange(BLOCKS).reshape(SEQ, CH).T.reshape(1, 1, BLOCKS)
    phase = ((TILES * block + tile) * (4 * k1 + 1) % (4 * TOKENS)) * (step / (4 * TOKENS))
    outer = np.concatenate([np.cos(phase), -np.sin(phase)], axis=1)
    lane = np.arange(LANES)[None, :]
    phase = lane * (np.arange(BLOCKS)[:, None] + 0.25) * (step / LENGTH)
    turn = np.stack([np.cos(phase), -np.sin(phase)])
    lane = np.arange(LANES)[None, :, None]
    k2 = np.arange(LANES)[None, None, :]
    phase = (lane * (TILES * k2 + tile) % TOKENS) * (step / TOKENS)
    cos, sin = np.cos(phase), np.sin(phase)
    inner = np.concatenate(
        [np.concatenate([cos, -sin], axis=2), np.concatenate([sin, cos], axis=2)], axis=1
    )
    narrow = ml_dtypes.bfloat16
    return dict(
        outer=outer.astype(narrow),
        outer_back=outer.swapaxes(1, 2).astype(narrow),
        turn=turn.astype(np.float32),
        inner=inner.astype(narrow),
    )


def dot(left, right):
    return jnp.dot(left, right, preferred_element_type=F32)


def dot_back(left, right):
    dims = (((1,), (1,)), ((), ()))
    return lax.dot_general(left, right, dims, preferred_element_type=F32)


def call(body, name, out_shape, scratch, in_specs, out_specs, flops, nbytes, limit=16):
    return pl.pallas_call(
        body,
        out_shape=out_shape,
        in_specs=in_specs,
        out_specs=out_specs,
        scratch_shapes=scratch,
        compiler_params=pltpu.CompilerParams(vmem_limit_bytes=limit * 1024 * 1024),
        cost_estimate=pl.CostEstimate(flops=flops, bytes_accessed=nbytes, transcendentals=0),
        name=name,
    )


def shape(dims, dtype):
    return jax.ShapeDtypeStruct(dims, dtype)


def lanes_of(x):
    return lax.broadcasted_iota(jnp.int32, x.shape, 1)


def columns(rows, tap_rows):
    tap_rows[...] = jnp.zeros(tap_rows.shape, F32)
    at = 0
    for row in rows:
        tap_rows[at : at + row.shape[0], :] = row
        at += row.shape[0]
    return tap_rows[...].T


def taps_of(cols, stream):
    return [cols[:, 3 * stream + i : 3 * stream + i + 1] for i in range(3)]


def causal(x, taps):
    return taps[0] * x + taps[1] * pltpu.roll(x, 1, 1) + taps[2] * pltpu.roll(x, 2, 1)


def with_edges(x, taps):
    back1, back2 = pltpu.roll(x, 1, 1), pltpu.roll(x, 2, 1)
    sums = taps[0] * x + taps[1] * back1 + taps[2] * back2
    lane = lax.broadcasted_iota(jnp.int32, (x.shape[0], LANES), 1)
    near = jnp.where(lane < 1, back1[:, :LANES], 0.0)
    far = jnp.where(lane < 2, back2[:, :LANES], 0.0)
    onward = taps[1] * near + taps[2] * far
    return sums, sums[:, :LANES] - onward, onward


def gate_body(
    q_ref, k_ref, v_ref, taps_ref, skip_ref, out_ref,
    taps_buf, skip_buf, q_buf, k_buf, v_buf, tap_rows, cols_buf, rows, small, sems
):
    def small_copies():
        pairs = [(taps_ref, taps_buf), (skip_ref, skip_buf)]
        pairs += [
            (q_ref.at[:, pl.ds(i * (TOKENS - LANES), LANES)], q_buf.at[i]) for i in range(2)
        ]
        return [pltpu.make_async_copy(a, b, small.at[i]) for i, (a, b) in enumerate(pairs)]

    copies = []
    for step in range(STEPS):
        at = pl.ds(step * ROWS, ROWS)
        copies.append(
            [
                pltpu.make_async_copy(ref.at[at], buf.at[at], sems.at[i, step])
                for i, (ref, buf) in enumerate(((k_ref, k_buf), (v_ref, v_buf)))
            ]
        )
    first = small_copies()
    for copy in first:
        copy.start()
    for pair in copies:
        for copy in pair:
            copy.start()
    for copy in first:
        copy.wait()
    cols_buf[...] = columns([taps_buf[0], taps_buf[1], taps_buf[2], skip_buf[...]], tap_rows)
    for step in range(STEPS):
        for copy in copies[step]:
            copy.wait()
        at = slice(step * ROWS, (step + 1) * ROWS)
        cols = cols_buf[at, :]
        query_taps, key_taps, value_taps = (taps_of(cols, stream) for stream in range(3))
        key, key_own, key_onward = with_edges(k_buf[at, :].astype(F32), key_taps)
        value, value_own, value_onward = with_edges(v_buf[at, :].astype(F32), value_taps)
        query = jnp.concatenate([q_buf[0, at, :], q_buf[1, at, :]], axis=1).astype(F32)
        _, query_own, query_onward = with_edges(query, query_taps)
        gated = key * value
        for c in range(TILES):
            rows[pl.ds(c, ROWS, stride=WIDTH), :] = gated[:, c * LANES : (c + 1) * LANES]
        lane = lanes_of(key_own)
        own = jnp.where(lane < 2, key_own, pltpu.roll(query_own, 2, 1))
        own_value = pltpu.roll(jnp.where(lane < 2, value_own, cols[:, 9:10]), 4, 1)
        onward = key_onward + pltpu.roll(query_onward, 2, 1) + pltpu.roll(value_onward, 4, 1)
        edge = jnp.where(lane < 8, own_value, pltpu.roll(onward, 8, 1))
        rows[pl.ds(TILES, ROWS, stride=WIDTH), :] = jnp.where(lane < 4, own, edge)
        out_ref[step * ROWS * WIDTH : (step + 1) * ROWS * WIDTH, :] = rows[...].astype(BF16)


def gate(q, k, v, taps, skip):
    return call(
        gate_body,
        "gate",
        shape((CHANNELS * WIDTH, LANES), BF16),
        [
            pltpu.VMEM((3, 3, CHANNELS), F32),
            pltpu.VMEM((1, CHANNELS), F32),
            pltpu.VMEM((2, CHANNELS, LANES), BF16),
            pltpu.VMEM((CHANNELS, TOKENS), BF16),
            pltpu.VMEM((CHANNELS, TOKENS), BF16),
            pltpu.VMEM((LANES, CHANNELS), F32),
            pltpu.VMEM((CHANNELS, LANES), F32),
            pltpu.VMEM((ROWS * WIDTH, LANES), F32),
            pltpu.SemaphoreType.DMA((4,)),
            pltpu.SemaphoreType.DMA((2, STEPS)),
        ],
        [HBM] * 5,
        VMEM,
        10**7,
        2 * 1024 * 1024,
        GATE_LIMIT,
    )(q, k, v, taps, skip)


def eight_points(re, im):
    half = math.sqrt(0.5)
    out_re, out_im = [None] * 8, [None] * 8

    def four_points(re, im, first):
        sum_re = [re[i] + re[i + 2] for i in range(2)]
        sum_im = [im[i] + im[i + 2] for i in range(2)]
        dif_re = [re[i] - re[i + 2] for i in range(2)]
        dif_im = [im[i] - im[i + 2] for i in range(2)]
        out_re[first], out_im[first] = sum_re[0] + sum_re[1], sum_im[0] + sum_im[1]
        out_re[first + 4], out_im[first + 4] = sum_re[0] - sum_re[1], sum_im[0] - sum_im[1]
        out_re[first + 2], out_im[first + 2] = dif_re[0] + dif_im[1], dif_im[0] - dif_re[1]
        out_re[first + 6], out_im[first + 6] = dif_re[0] - dif_im[1], dif_im[0] + dif_re[1]

    four_points([re[i] + re[i + 4] for i in range(4)], [im[i] + im[i + 4] for i in range(4)], 0)
    re = [re[i] - re[i + 4] for i in range(4)]
    im = [im[i] - im[i + 4] for i in range(4)]
    turned_re = [re[0], (re[1] + im[1]) * half, im[2], (im[3] - re[3]) * half]
    turned_im = [im[0], (im[1] - re[1]) * half, -re[2], (re[3] + im[3]) * -half]
    four_points(turned_re, turned_im, 1)
    return out_re, out_im


def forward(signals, outer_ref, turn_ref, section, turned):
    for c in range(TILES):
        section[c] = dot(outer_ref[c], signals[c])
    for row in range(0, BLOCKS, 16):
        turn_re, turn_im = turn_ref[0, row : row + 16, :], turn_ref[1, row : row + 16, :]
        for j in range(2):
            half = slice(j * LANES, (j + 1) * LANES)
            re = [section[c, row : row + 16, half] for c in range(TILES)]
            im = [section[c, BLOCKS + row : BLOCKS + row + 16, half] for c in range(TILES)]
            re, im = eight_points(re, im)
            at = slice(j * BLOCKS + row, j * BLOCKS + row + 16)
            for kc in range(TILES):
                turned[kc, at, :LANES] = (re[kc] * turn_re - im[kc] * turn_im).astype(BF16)
                turned[kc, at, LANES:] = (re[kc] * turn_im + im[kc] * turn_re).astype(BF16)


def beside_body(
    filt_ref, outer_ref, turn_ref, inner_ref, q_ref, k_ref, v_ref, taps_ref, skip_ref,
    spec_ref, query_ref, direct_ref,
    filt_buf, outer_buf, turn_buf, inner_buf, streams, taps_buf, skip_buf, spec_buf, query_buf, direct_buf,
    rows, section, turned, tap_rows, cols_buf, small, in_sems, table_sems, out_sems, spec_sems
):
    first = [
        pltpu.make_async_copy(taps_ref, taps_buf, small.at[0]),
        pltpu.make_async_copy(skip_ref, skip_buf, small.at[1]),
    ]
    places = [pl.ds(step * ROWS, ROWS) for step in range(STEPS)]
    copies = [
        [
            pltpu.make_async_copy(ref.at[place], streams.at[i, place], in_sems.at[i, step])
            for i, ref in enumerate((q_ref, k_ref, v_ref))
        ]
        for step, place in enumerate(places)
    ]
    pairs = ((filt_ref, filt_buf), (outer_ref, outer_buf), (turn_ref, turn_buf), (inner_ref, inner_buf))
    tables_in = [
        pltpu.make_async_copy(a, b, table_sems.at[i]) for i, (a, b) in enumerate(pairs)
    ]
    for copy in first + [copy for group in copies for copy in group] + tables_in:
        copy.start()
    for copy in first:
        copy.wait()
    out_copies = []
    cols_buf[...] = columns([taps_buf[0], taps_buf[1], taps_buf[2], skip_buf[...]], tap_rows)
    for step in range(STEPS):
        for copy in copies[step]:
            copy.wait()
        at = slice(step * ROWS, (step + 1) * ROWS)
        cols = cols_buf[at, :]
        query, key, value = (
            causal(streams[i, at, :].astype(F32), taps_of(cols, i)) for i in range(3)
        )
        query_buf[at, :] = query
        direct_buf[at, :] = cols[:, 9:10] * (key * value).astype(BF16).astype(F32)
        for i, (buf, ref) in enumerate(((query_buf, query_ref), (direct_buf, direct_ref))):
            out_copies.append(
                pltpu.make_async_copy(buf.at[places[step]], ref.at[places[step]], out_sems.at[i, step])
            )
            out_copies[-1].start()
    for copy in tables_in:
        copy.wait()
    rows[...] = filt_buf[...].astype(F32)
    signals = []
    for c in range(TILES):
        halves = []
        for j in range(2):
            parts = [
                rows[pl.ds(2 * (g * TILES + c) + j, SEQ, stride=2 * TILES * CH), :]
                for g in range(CH)
            ]
            halves.append(jnp.concatenate(parts, axis=0))
        signals.append(jnp.concatenate(halves, axis=1).astype(BF16))
    forward(signals, outer_buf, turn_buf, section, turned)
    for kc in range(TILES):
        spec_buf[kc] = (dot(turned[kc], inner_buf[kc]) * (1.0 / LENGTH)).astype(BF16)
        out_copies.append(pltpu.make_async_copy(spec_buf.at[kc], spec_ref.at[kc], spec_sems.at[kc]))
        out_copies[-1].start()
    for copy in out_copies:
        copy.wait()


def beside(filt, consts, q, k, v, taps, skip):
    names = ("outer", "turn", "inner")
    spec = (TILES, 2 * BLOCKS, 2 * LANES)
    return call(
        beside_body,
        "beside",
        (shape(spec, BF16), shape((CHANNELS, TOKENS), F32), shape((CHANNELS, TOKENS), F32)),
        [
            pltpu.VMEM((2 * BLOCKS * TILES, LANES), BF16),
            pltpu.VMEM((TILES, 2 * BLOCKS, LANES), BF16),
            pltpu.VMEM((2, BLOCKS, LANES), F32),
            pltpu.VMEM((TILES, 2 * LANES, 2 * LANES), BF16),
            pltpu.VMEM((3, CHANNELS, TOKENS), BF16),
            pltpu.VMEM((3, 3, CHANNELS), F32),
            pltpu.VMEM((1, CHANNELS), F32),
            pltpu.VMEM(spec, BF16),
            pltpu.VMEM((CHANNELS, TOKENS), F32),
            pltpu.VMEM((CHANNELS, TOKENS), F32),
            pltpu.VMEM((2 * BLOCKS * TILES, LANES), F32),
            pltpu.VMEM(spec, F32),
            pltpu.VMEM(spec, BF16),
            pltpu.VMEM((LANES, CHANNELS), F32),
            pltpu.VMEM((CHANNELS, LANES), F32),
            pltpu.SemaphoreType.DMA((2,)),
            pltpu.SemaphoreType.DMA((3, STEPS)),
            pltpu.SemaphoreType.DMA((4,)),
            pltpu.SemaphoreType.DMA((2, STEPS)),
            pltpu.SemaphoreType.DMA((TILES,)),
        ],
        [HBM] * 9,
        (HBM,) * 3,
        10**9,
        8 * 1024 * 1024,
        BESIDE_LIMIT,
    )(filt, *(consts[name] for name in names), q, k, v, taps, skip)


def conv_body(
    arrived_ref, spec_ref, outer_ref, outer_back_ref, turn_ref, inner_ref, out_ref,
    rows, section, turned, back, edges, inner_buf, spec_buf, sems
):
    copies = [
        [
            pltpu.make_async_copy(ref.at[kc], buf.at[kc], sems.at[i, kc])
            for i, (ref, buf) in enumerate(((inner_ref, inner_buf), (spec_ref, spec_buf)))
        ]
        for kc in range(TILES)
    ]
    for pair in copies:
        for copy in pair:
            copy.start()
    rows[...] = arrived_ref[...].astype(F32)

    def arrived(j, c):
        return rows[pl.ds(j * WIDTH + c, BLOCKS, stride=2 * WIDTH), :]

    signals = []
    for c in range(TILES):
        halves = [arrived(j, c) for j in range(2)]
        if c == 0:
            for j in range(2):
                edge = arrived(j, TILES)
                last = edge[BLOCKS - SEQ :]
                step = lax.broadcasted_iota(jnp.int32, last.shape, 0)
                last = jnp.where(step == 0, 0.0, pltpu.roll(last, 1, 0))
                before = jnp.concatenate([last, edge[: BLOCKS - SEQ]], axis=0)
                total = edge + pltpu.roll(before, LANES - 8, 1)
                gated = (total * pltpu.roll(total, LANES - 4, 1)).astype(BF16).astype(F32)
                edges[0, j] = pltpu.roll(total, LANES - 2, 1)
                edges[1, j] = pltpu.roll(total, LANES - 6, 1) * gated
                halves[j] = jnp.where(lanes_of(gated) < 2, gated, halves[j])
        signals.append(jnp.concatenate(halves, axis=1).astype(BF16))
    forward(signals, outer_ref, turn_ref, section, turned)
    for kc in range(TILES):
        for copy in copies[kc]:
            copy.wait()
        spectrum = dot(turned[kc], inner_buf[kc])
        re, im = spectrum[:, :LANES], spectrum[:, LANES:]
        spec = spec_buf[kc].astype(F32)
        filt_re, filt_im = spec[:, :LANES], spec[:, LANES:]
        parts = [re * filt_re - im * filt_im, re * filt_im + im * filt_re]
        section[kc] = dot_back(jnp.concatenate(parts, axis=1).astype(BF16), inner_buf[kc])
    for row in range(0, BLOCKS, 16):
        turn_re, turn_im = turn_ref[0, row : row + 16, :], turn_ref[1, row : row + 16, :]
        for j in range(2):
            at = slice(j * BLOCKS + row, j * BLOCKS + row + 16)
            re, im = [], []
            for kc in range(TILES):
                part_re, part_im = section[kc, at, :LANES], section[kc, at, LANES:]
                re.append(part_re * turn_re + part_im * turn_im)
                im.append(part_im * turn_re - part_re * turn_im)
            im, re = eight_points(im, re)
            half = slice(j * LANES, (j + 1) * LANES)
            for c in range(TILES):
                back[c, row : row + 16, half] = re[c].astype(BF16)
                back[c, BLOCKS + row : BLOCKS + row + 16, half] = im[c].astype(BF16)
    for c in range(TILES):
        result = dot(outer_back_ref[c], back[c])
        for j in range(2):
            half = result[:, j * LANES : (j + 1) * LANES]
            if c == 0:
                start = edges[0, j] * (half.astype(BF16).astype(F32) + edges[1, j])
                half = jnp.where(lanes_of(half) < 2, start, half)
            rows[pl.ds(j * TILES + c, BLOCKS, stride=BODY), :] = half
    out_ref[...] = rows[: BLOCKS * BODY, :].reshape(BLOCKS, BODY, LANES).astype(BF16)


def conv(arrived, spec, consts):
    names = ("outer", "outer_back", "turn", "inner")
    return call(
        conv_body,
        "conv",
        shape((BLOCKS, BODY, LANES), BF16),
        [
            pltpu.VMEM((BLOCKS * 2 * WIDTH, LANES), F32),
            pltpu.VMEM((TILES, 2 * BLOCKS, 2 * LANES), F32),
            pltpu.VMEM((TILES, 2 * BLOCKS, 2 * LANES), BF16),
            pltpu.VMEM((TILES, 2 * BLOCKS, 2 * LANES), BF16),
            pltpu.VMEM((2, 2, BLOCKS, LANES), F32),
            pltpu.VMEM((TILES, 2 * LANES, 2 * LANES), BF16),
            pltpu.VMEM((TILES, 2 * BLOCKS, 2 * LANES), BF16),
            pltpu.SemaphoreType.DMA((2, TILES)),
        ],
        [VMEM, HBM, VMEM, VMEM, VMEM, HBM],
        VMEM,
        10**9,
        8 * 1024 * 1024,
        CONV_LIMIT,
    )(arrived, spec, *(consts[name] for name in names))


def final_body(returned_ref, query_ref, direct_ref, out_ref, rows, out_buf, sems):
    copies = []
    for step in range(STEPS):
        at = slice(step * ROWS, (step + 1) * ROWS)
        message = returned_ref[step * ROWS // 2 : (step + 1) * ROWS // 2].astype(F32)
        rows[...] = message.reshape(ROWS * TILES, LANES)
        for c in range(TILES):
            lanes = slice(c * LANES, (c + 1) * LANES)
            long_result = rows[pl.ds(c, ROWS, stride=TILES), :]
            mixed = query_ref[at, lanes] * (long_result + direct_ref[at, lanes])
            if c == 0:
                mixed = jnp.where(lanes_of(mixed) < 2, long_result, mixed)
            out_buf[at, lanes] = mixed.astype(BF16)
        place = pl.ds(step * ROWS, ROWS)
        copies.append(pltpu.make_async_copy(out_buf.at[place], out_ref.at[place], sems.at[step]))
        copies[-1].start()
    for copy in copies:
        copy.wait()


def final(returned, query, direct_term):
    return call(
        final_body,
        "final",
        shape((CHANNELS, TOKENS), BF16),
        [
            pltpu.VMEM((ROWS * TILES, LANES), F32),
            pltpu.VMEM((CHANNELS, TOKENS), BF16),
            pltpu.SemaphoreType.DMA((STEPS,)),
        ],
        [VMEM] * 3,
        HBM,
        10**6,
        2 * 1024 * 1024,
        FINAL_LIMIT,
    )(returned, query, direct_term)


def exchange(messages):
    return lax.all_to_all(messages, OWNERS, split_axis=0, concat_axis=0, tiled=True)


def shards(consts, q, k, v, short_taps, long_filter, skip_gain):
    consts = {name: jnp.asarray(table) for name, table in consts.items()}
    skip = skip_gain[None]
    messages = gate(q, k, v, short_taps, skip).reshape(BLOCKS, WIDTH, 2, LANES)
    messages, q, k, v, long_filter = lax.optimization_barrier((messages, q, k, v, long_filter))
    arrived = exchange(messages).reshape(BLOCKS * 2 * WIDTH, LANES)
    filt = long_filter.reshape(2, BLOCKS * TILES, LANES).swapaxes(0, 1)
    filt = filt.reshape(2 * BLOCKS * TILES, LANES)
    spec, query, direct_term = beside(filt, consts, q, k, v, short_taps, skip)
    returned = exchange(conv(arrived, spec, consts))
    return final(returned, query, direct_term)


def solution(mesh):
    tokens = P(None, AXES)
    placed = (tokens, tokens, tokens, P(), P("ch", "seq", None, None), P())
    return jax.shard_map(
        functools.partial(shards, tables()),
        mesh=mesh,
        in_specs=placed,
        out_specs=tokens,
        check_vma=False,
    )
```

```python
import functools
import math

import jax
import jax.numpy as jnp
import ml_dtypes
import numpy as np
from jax import lax
from jax.experimental import pallas as pl
from jax.experimental.pallas import tpu as pltpu
from jax.sharding import PartitionSpec as P

F32 = jnp.float32
BF16 = jnp.bfloat16
LANES = 128
TOKENS = 1024
TILES = TOKENS // LANES
BLOCKS = 128
LENGTH = BLOCKS * TOKENS
CHANNELS = 256
SEQ = 8
CH = 16
BODY = 2 * TILES
WIDTH = TILES + 1
GATE_LIMIT, BESIDE_LIMIT, CONV_LIMIT, FINAL_LIMIT = 60, 60, 16, 16
ROWS = 64
STEPS = CHANNELS // ROWS
AXES = ("seq", "ch")
OWNERS = ("ch", "seq")
VMEM = pl.BlockSpec(memory_space=pltpu.VMEM)
HBM = pl.BlockSpec(memory_space=pltpu.HBM)


def tables():
    step = 2.0 * math.pi
    tile = np.arange(TILES)[:, None, None]
    k1 = np.arange(BLOCKS)[None, :, None]
    block = np.arange(BLOCKS).reshape(SEQ, CH).T.reshape(1, 1, BLOCKS)
    phase = ((TILES * block + tile) * (4 * k1 + 1) % (4 * TOKENS)) * (step / (4 * TOKENS))
    outer = np.concatenate([np.cos(phase), -np.sin(phase)], axis=1)
    lane = np.arange(LANES)[None, :]
    phase = lane * (np.arange(BLOCKS)[:, None] + 0.25) * (step / LENGTH)
    turn = np.stack([np.cos(phase), -np.sin(phase)])
    lane = np.arange(LANES)[None, :, None]
    k2 = np.arange(LANES)[None, None, :]
    phase = (lane * (TILES * k2 + tile) % TOKENS) * (step / TOKENS)
    cos, sin = np.cos(phase), np.sin(phase)
    inner = np.concatenate(
        [np.concatenate([cos, -sin], axis=2), np.concatenate([sin, cos], axis=2)], axis=1
    )
    narrow = ml_dtypes.bfloat16
    return dict(
        outer=outer.astype(narrow),
        turn=turn.astype(np.float32),
        inner=inner.astype(narrow),
    )


def dot(left, right):
    return jnp.dot(left, right, preferred_element_type=F32)


def dot_back(left, right):
    dims = (((1,), (1,)), ((), ()))
    return lax.dot_general(left, right, dims, preferred_element_type=F32)


def call(body, name, out_shape, scratch, in_specs, out_specs, flops, nbytes, limit=16):
    return pl.pallas_call(
        body,
        out_shape=out_shape,
        in_specs=in_specs,
        out_specs=out_specs,
        scratch_shapes=scratch,
        compiler_params=pltpu.CompilerParams(vmem_limit_bytes=limit * 1024 * 1024),
        cost_estimate=pl.CostEstimate(flops=flops, bytes_accessed=nbytes, transcendentals=0),
        name=name,
    )


def shape(dims, dtype):
    return jax.ShapeDtypeStruct(dims, dtype)


def lanes_of(x):
    return lax.broadcasted_iota(jnp.int32, x.shape, 1)


def columns(rows, tap_rows):
    tap_rows[...] = jnp.zeros(tap_rows.shape, F32)
    at = 0
    for row in rows:
        tap_rows[at : at + row.shape[0], :] = row
        at += row.shape[0]
    return tap_rows[...].T


def taps_of(cols, stream):
    return [cols[:, 3 * stream + i : 3 * stream + i + 1] for i in range(3)]


def causal(x, taps):
    return taps[0] * x + taps[1] * pltpu.roll(x, 1, 1) + taps[2] * pltpu.roll(x, 2, 1)


def with_edges(x, taps):
    back1, back2 = pltpu.roll(x, 1, 1), pltpu.roll(x, 2, 1)
    sums = taps[0] * x + taps[1] * back1 + taps[2] * back2
    lane = lax.broadcasted_iota(jnp.int32, (x.shape[0], LANES), 1)
    near = jnp.where(lane < 1, back1[:, :LANES], 0.0)
    far = jnp.where(lane < 2, back2[:, :LANES], 0.0)
    onward = taps[1] * near + taps[2] * far
    return sums, sums[:, :LANES] - onward, onward


def gate_body(
    q_ref, k_ref, v_ref, taps_ref, skip_ref, out_ref,
    taps_buf, skip_buf, q_buf, k_buf, v_buf, tap_rows, cols_buf, rows, small, sems
):
    def small_copies():
        pairs = [(taps_ref, taps_buf), (skip_ref, skip_buf)]
        pairs += [
            (q_ref.at[:, pl.ds(i * (TOKENS - LANES), LANES)], q_buf.at[i]) for i in range(2)
        ]
        return [pltpu.make_async_copy(a, b, small.at[i]) for i, (a, b) in enumerate(pairs)]

    copies = []
    for step in range(STEPS):
        at = pl.ds(step * ROWS, ROWS)
        copies.append(
            [
                pltpu.make_async_copy(ref.at[at], buf.at[at], sems.at[i, step])
                for i, (ref, buf) in enumerate(((k_ref, k_buf), (v_ref, v_buf)))
            ]
        )
    first = small_copies()
    for copy in first:
        copy.start()
    for pair in copies:
        for copy in pair:
            copy.start()
    for copy in first:
        copy.wait()
    cols_buf[...] = columns([taps_buf[0], taps_buf[1], taps_buf[2], skip_buf[...]], tap_rows)
    for step in range(STEPS):
        for copy in copies[step]:
            copy.wait()
        at = slice(step * ROWS, (step + 1) * ROWS)
        cols = cols_buf[at, :]
        query_taps, key_taps, value_taps = (taps_of(cols, stream) for stream in range(3))
        key, key_own, key_onward = with_edges(k_buf[at, :].astype(F32), key_taps)
        value, value_own, value_onward = with_edges(v_buf[at, :].astype(F32), value_taps)
        query = jnp.concatenate([q_buf[0, at, :], q_buf[1, at, :]], axis=1).astype(F32)
        _, query_own, query_onward = with_edges(query, query_taps)
        gated = key * value
        for c in range(TILES):
            rows[pl.ds(c, ROWS, stride=WIDTH), :] = gated[:, c * LANES : (c + 1) * LANES]
        lane = lanes_of(key_own)
        own = jnp.where(lane < 2, key_own, pltpu.roll(query_own, 2, 1))
        own_value = pltpu.roll(jnp.where(lane < 2, value_own, cols[:, 9:10]), 4, 1)
        onward = key_onward + pltpu.roll(query_onward, 2, 1) + pltpu.roll(value_onward, 4, 1)
        edge = jnp.where(lane < 8, own_value, pltpu.roll(onward, 8, 1))
        rows[pl.ds(TILES, ROWS, stride=WIDTH), :] = jnp.where(lane < 4, own, edge)
        out_ref[step * ROWS * WIDTH : (step + 1) * ROWS * WIDTH, :] = rows[...].astype(BF16)


def gate(q, k, v, taps, skip):
    return call(
        gate_body,
        "gate",
        shape((CHANNELS * WIDTH, LANES), BF16),
        [
            pltpu.VMEM((3, 3, CHANNELS), F32),
            pltpu.VMEM((1, CHANNELS), F32),
            pltpu.VMEM((2, CHANNELS, LANES), BF16),
            pltpu.VMEM((CHANNELS, TOKENS), BF16),
            pltpu.VMEM((CHANNELS, TOKENS), BF16),
            pltpu.VMEM((LANES, CHANNELS), F32),
            pltpu.VMEM((CHANNELS, LANES), F32),
            pltpu.VMEM((ROWS * WIDTH, LANES), F32),
            pltpu.SemaphoreType.DMA((4,)),
            pltpu.SemaphoreType.DMA((2, STEPS)),
        ],
        [HBM] * 5,
        VMEM,
        10**7,
        2 * 1024 * 1024,
        GATE_LIMIT,
    )(q, k, v, taps, skip)


def eight_points(re, im):
    half = math.sqrt(0.5)
    out_re, out_im = [None] * 8, [None] * 8

    def four_points(re, im, first):
        sum_re = [re[i] + re[i + 2] for i in range(2)]
        sum_im = [im[i] + im[i + 2] for i in range(2)]
        dif_re = [re[i] - re[i + 2] for i in range(2)]
        dif_im = [im[i] - im[i + 2] for i in range(2)]
        out_re[first], out_im[first] = sum_re[0] + sum_re[1], sum_im[0] + sum_im[1]
        out_re[first + 4], out_im[first + 4] = sum_re[0] - sum_re[1], sum_im[0] - sum_im[1]
        out_re[first + 2], out_im[first + 2] = dif_re[0] + dif_im[1], dif_im[0] - dif_re[1]
        out_re[first + 6], out_im[first + 6] = dif_re[0] - dif_im[1], dif_im[0] + dif_re[1]

    four_points([re[i] + re[i + 4] for i in range(4)], [im[i] + im[i + 4] for i in range(4)], 0)
    re = [re[i] - re[i + 4] for i in range(4)]
    im = [im[i] - im[i + 4] for i in range(4)]
    turned_re = [re[0], (re[1] + im[1]) * half, im[2], (im[3] - re[3]) * half]
    turned_im = [im[0], (im[1] - re[1]) * half, -re[2], (re[3] + im[3]) * -half]
    four_points(turned_re, turned_im, 1)
    return out_re, out_im


def forward(signals, outer_ref, turn_ref, section, turned):
    for c in range(TILES):
        section[c] = dot(outer_ref[c], signals[c])
    for row in range(0, BLOCKS, 16):
        turn_re, turn_im = turn_ref[0, row : row + 16, :], turn_ref[1, row : row + 16, :]
        for j in range(2):
            half = slice(j * LANES, (j + 1) * LANES)
            re = [section[c, row : row + 16, half] for c in range(TILES)]
            im = [section[c, BLOCKS + row : BLOCKS + row + 16, half] for c in range(TILES)]
            re, im = eight_points(re, im)
            at = slice(j * BLOCKS + row, j * BLOCKS + row + 16)
            for kc in range(TILES):
                turned[kc, at, :LANES] = (re[kc] * turn_re - im[kc] * turn_im).astype(BF16)
                turned[kc, at, LANES:] = (re[kc] * turn_im + im[kc] * turn_re).astype(BF16)


def beside_body(
    filt_ref, outer_ref, turn_ref, inner_ref, q_ref, k_ref, v_ref, taps_ref, skip_ref,
    spec_ref, query_ref, direct_ref,
    filt_buf, outer_buf, turn_buf, inner_buf, streams, taps_buf, skip_buf, spec_buf, query_buf, direct_buf,
    rows, section, turned, tap_rows, cols_buf, small, in_sems, table_sems, out_sems, spec_sems
):
    first = [
        pltpu.make_async_copy(taps_ref, taps_buf, small.at[0]),
        pltpu.make_async_copy(skip_ref, skip_buf, small.at[1]),
    ]
    places = [pl.ds(step * ROWS, ROWS) for step in range(STEPS)]
    copies = [
        [
            pltpu.make_async_copy(ref.at[place], streams.at[i, place], in_sems.at[i, step])
            for i, ref in enumerate((q_ref, k_ref, v_ref))
        ]
        for step, place in enumerate(places)
    ]
    pairs = ((filt_ref, filt_buf), (outer_ref, outer_buf), (turn_ref, turn_buf), (inner_ref, inner_buf))
    tables_in = [
        pltpu.make_async_copy(a, b, table_sems.at[i]) for i, (a, b) in enumerate(pairs)
    ]
    for copy in first + [copy for group in copies for copy in group] + tables_in:
        copy.start()
    for copy in first:
        copy.wait()
    out_copies = []
    cols_buf[...] = columns([taps_buf[0], taps_buf[1], taps_buf[2], skip_buf[...]], tap_rows)
    for step in range(STEPS):
        for copy in copies[step]:
            copy.wait()
        at = slice(step * ROWS, (step + 1) * ROWS)
        cols = cols_buf[at, :]
        query, key, value = (
            causal(streams[i, at, :].astype(F32), taps_of(cols, i)) for i in range(3)
        )
        query_buf[at, :] = query
        direct_buf[at, :] = cols[:, 9:10] * (key * value).astype(BF16).astype(F32)
        for i, (buf, ref) in enumerate(((query_buf, query_ref), (direct_buf, direct_ref))):
            out_copies.append(
                pltpu.make_async_copy(buf.at[places[step]], ref.at[places[step]], out_sems.at[i, step])
            )
            out_copies[-1].start()
    for copy in tables_in:
        copy.wait()
    rows[...] = filt_buf[...].astype(F32)
    signals = []
    for c in range(TILES):
        halves = []
        for j in range(2):
            parts = [
                rows[pl.ds(2 * (g * TILES + c) + j, SEQ, stride=2 * TILES * CH), :]
                for g in range(CH)
            ]
            halves.append(jnp.concatenate(parts, axis=0))
        signals.append(jnp.concatenate(halves, axis=1).astype(BF16))
    forward(signals, outer_buf, turn_buf, section, turned)
    for kc in range(TILES):
        spec_buf[kc] = (dot(turned[kc], inner_buf[kc]) * (1.0 / LENGTH)).astype(BF16)
        out_copies.append(pltpu.make_async_copy(spec_buf.at[kc], spec_ref.at[kc], spec_sems.at[kc]))
        out_copies[-1].start()
    for copy in out_copies:
        copy.wait()


def beside(filt, consts, q, k, v, taps, skip):
    names = ("outer", "turn", "inner")
    spec = (TILES, 2 * BLOCKS, 2 * LANES)
    return call(
        beside_body,
        "beside",
        (shape(spec, BF16), shape((CHANNELS, TOKENS), F32), shape((CHANNELS, TOKENS), F32)),
        [
            pltpu.VMEM((2 * BLOCKS * TILES, LANES), BF16),
            pltpu.VMEM((TILES, 2 * BLOCKS, LANES), BF16),
            pltpu.VMEM((2, BLOCKS, LANES), F32),
            pltpu.VMEM((TILES, 2 * LANES, 2 * LANES), BF16),
            pltpu.VMEM((3, CHANNELS, TOKENS), BF16),
            pltpu.VMEM((3, 3, CHANNELS), F32),
            pltpu.VMEM((1, CHANNELS), F32),
            pltpu.VMEM(spec, BF16),
            pltpu.VMEM((CHANNELS, TOKENS), F32),
            pltpu.VMEM((CHANNELS, TOKENS), F32),
            pltpu.VMEM((2 * BLOCKS * TILES, LANES), F32),
            pltpu.VMEM(spec, F32),
            pltpu.VMEM(spec, BF16),
            pltpu.VMEM((LANES, CHANNELS), F32),
            pltpu.VMEM((CHANNELS, LANES), F32),
            pltpu.SemaphoreType.DMA((2,)),
            pltpu.SemaphoreType.DMA((3, STEPS)),
            pltpu.SemaphoreType.DMA((4,)),
            pltpu.SemaphoreType.DMA((2, STEPS)),
            pltpu.SemaphoreType.DMA((TILES,)),
        ],
        [HBM] * 9,
        (HBM,) * 3,
        10**9,
        8 * 1024 * 1024,
        BESIDE_LIMIT,
    )(filt, *(consts[name] for name in names), q, k, v, taps, skip)


def touch_body(spec_ref, *refs):
    out_ref = refs[-1]
    out_ref[...] = spec_ref[0, :16, :LANES].astype(F32)


def touch(spec, consts):
    return call(
        touch_body, "touch", shape((16, LANES), F32), [], [VMEM] * 4, VMEM, 10**4, 10**6, CONV_LIMIT
    )(spec, *(consts[name] for name in ('outer', 'turn', 'inner')))


def conv_body(
    arrived_ref, spec_ref, outer_ref, turn_ref, inner_ref, touched_ref, out_ref,
    rows, section, turned, back, edges
):
    del touched_ref
    rows[...] = arrived_ref[...].astype(F32)

    def arrived(j, c):
        return rows[pl.ds(j * WIDTH + c, BLOCKS, stride=2 * WIDTH), :]

    signals = []
    for c in range(TILES):
        halves = [arrived(j, c) for j in range(2)]
        if c == 0:
            for j in range(2):
                edge = arrived(j, TILES)
                last = edge[BLOCKS - SEQ :]
                step = lax.broadcasted_iota(jnp.int32, last.shape, 0)
                last = jnp.where(step == 0, 0.0, pltpu.roll(last, 1, 0))
                before = jnp.concatenate([last, edge[: BLOCKS - SEQ]], axis=0)
                total = edge + pltpu.roll(before, LANES - 8, 1)
                gated = (total * pltpu.roll(total, LANES - 4, 1)).astype(BF16).astype(F32)
                edges[0, j] = pltpu.roll(total, LANES - 2, 1)
                edges[1, j] = pltpu.roll(total, LANES - 6, 1) * gated
                halves[j] = jnp.where(lanes_of(gated) < 2, gated, halves[j])
        signals.append(jnp.concatenate(halves, axis=1).astype(BF16))
    forward(signals, outer_ref, turn_ref, section, turned)
    for kc in range(TILES):
        spectrum = dot(turned[kc], inner_ref[kc])
        re, im = spectrum[:, :LANES], spectrum[:, LANES:]
        spec = spec_ref[kc].astype(F32)
        filt_re, filt_im = spec[:, :LANES], spec[:, LANES:]
        parts = [re * filt_re - im * filt_im, re * filt_im + im * filt_re]
        section[kc] = dot_back(jnp.concatenate(parts, axis=1).astype(BF16), inner_ref[kc])
    for row in range(0, BLOCKS, 16):
        turn_re, turn_im = turn_ref[0, row : row + 16, :], turn_ref[1, row : row + 16, :]
        for j in range(2):
            at = slice(j * BLOCKS + row, j * BLOCKS + row + 16)
            re, im = [], []
            for kc in range(TILES):
                part_re, part_im = section[kc, at, :LANES], section[kc, at, LANES:]
                re.append(part_re * turn_re + part_im * turn_im)
                im.append(part_im * turn_re - part_re * turn_im)
            im, re = eight_points(im, re)
            half = slice(j * LANES, (j + 1) * LANES)
            for c in range(TILES):
                back[c, row : row + 16, half] = re[c].astype(BF16)
                back[c, BLOCKS + row : BLOCKS + row + 16, half] = im[c].astype(BF16)
    for c in range(TILES):
        result = lax.dot_general(
            outer_ref[c], back[c], (((0,), (0,)), ((), ())), preferred_element_type=F32
        )
        for j in range(2):
            half = result[:, j * LANES : (j + 1) * LANES]
            if c == 0:
                start = edges[0, j] * (half.astype(BF16).astype(F32) + edges[1, j])
                half = jnp.where(lanes_of(half) < 2, start, half)
            rows[pl.ds(j * TILES + c, BLOCKS, stride=BODY), :] = half
    out_ref[...] = rows[: BLOCKS * BODY, :].reshape(BLOCKS, BODY, LANES).astype(BF16)


def conv(arrived, spec, consts, touched):
    names = ("outer", "turn", "inner")
    return call(
        conv_body,
        "conv",
        shape((BLOCKS, BODY, LANES), BF16),
        [
            pltpu.VMEM((BLOCKS * 2 * WIDTH, LANES), F32),
            pltpu.VMEM((TILES, 2 * BLOCKS, 2 * LANES), F32),
            pltpu.VMEM((TILES, 2 * BLOCKS, 2 * LANES), BF16),
            pltpu.VMEM((TILES, 2 * BLOCKS, 2 * LANES), BF16),
            pltpu.VMEM((2, 2, BLOCKS, LANES), F32),
        ],
        [VMEM] * 6,
        VMEM,
        10**9,
        8 * 1024 * 1024,
        CONV_LIMIT,
    )(arrived, spec, *(consts[name] for name in names), touched)


def final_body(returned_ref, query_ref, direct_ref, out_ref, rows, out_buf, sems):
    copies = []
    for step in range(STEPS):
        at = slice(step * ROWS, (step + 1) * ROWS)
        message = returned_ref[step * ROWS // 2 : (step + 1) * ROWS // 2].astype(F32)
        rows[...] = message.reshape(ROWS * TILES, LANES)
        for c in range(TILES):
            lanes = slice(c * LANES, (c + 1) * LANES)
            long_result = rows[pl.ds(c, ROWS, stride=TILES), :]
            mixed = query_ref[at, lanes] * (long_result + direct_ref[at, lanes])
            if c == 0:
                mixed = jnp.where(lanes_of(mixed) < 2, long_result, mixed)
            out_buf[at, lanes] = mixed.astype(BF16)
        place = pl.ds(step * ROWS, ROWS)
        copies.append(pltpu.make_async_copy(out_buf.at[place], out_ref.at[place], sems.at[step]))
        copies[-1].start()
    for copy in copies:
        copy.wait()


def final(returned, query, direct_term):
    return call(
        final_body,
        "final",
        shape((CHANNELS, TOKENS), BF16),
        [
            pltpu.VMEM((ROWS * TILES, LANES), F32),
            pltpu.VMEM((CHANNELS, TOKENS), BF16),
            pltpu.SemaphoreType.DMA((STEPS,)),
        ],
        [VMEM] * 3,
        HBM,
        10**6,
        2 * 1024 * 1024,
        FINAL_LIMIT,
    )(returned, query, direct_term)


def exchange(messages):
    return lax.all_to_all(messages, OWNERS, split_axis=0, concat_axis=0, tiled=True)


def shards(consts, q, k, v, short_taps, long_filter, skip_gain):
    consts = {name: jnp.asarray(table) for name, table in consts.items()}
    skip = skip_gain[None]
    messages = gate(q, k, v, short_taps, skip).reshape(BLOCKS, WIDTH, 2, LANES)
    messages, q, k, v, long_filter = lax.optimization_barrier((messages, q, k, v, long_filter))
    arrived = exchange(messages).reshape(BLOCKS * 2 * WIDTH, LANES)
    filt = long_filter.reshape(2, BLOCKS * TILES, LANES).swapaxes(0, 1)
    filt = filt.reshape(2 * BLOCKS * TILES, LANES)
    spec, query, direct_term = beside(filt, consts, q, k, v, short_taps, skip)
    returned = exchange(conv(arrived, spec, consts, touch(spec, consts)))
    return final(returned, query, direct_term)


def solution(mesh):
    tokens = P(None, AXES)
    placed = (tokens, tokens, tokens, P(), P("ch", "seq", None, None), P())
    return jax.shard_map(
        functools.partial(shards, tables()),
        mesh=mesh,
        in_specs=placed,
        out_specs=tokens,
        check_vma=False,
    )
```

```python
import functools
import math

import jax
import jax.numpy as jnp
import ml_dtypes
import numpy as np
from jax import lax
from jax.experimental import pallas as pl
from jax.experimental.pallas import tpu as pltpu
from jax.sharding import PartitionSpec as P

F32 = jnp.float32
BF16 = jnp.bfloat16
LANES = 128
TOKENS = 1024
TILES = TOKENS // LANES
BLOCKS = 128
LENGTH = BLOCKS * TOKENS
CHANNELS = 256
SEQ = 8
CH = 16
BODY = 2 * TILES
WIDTH = TILES + 1
GATE_LIMIT, FILTER_LIMIT, DIRECT_LIMIT, CONV_LIMIT, FINAL_LIMIT = 60, 52, 60, 16, 16
ROWS = 64
STEPS = CHANNELS // ROWS
DIRECT_ROWS = 128
DIRECT_STEPS = CHANNELS // DIRECT_ROWS
AXES = ("seq", "ch")
OWNERS = ("ch", "seq")
VMEM = pl.BlockSpec(memory_space=pltpu.VMEM)
HBM = pl.BlockSpec(memory_space=pltpu.HBM)


def tables():
    step = 2.0 * math.pi
    tile = np.arange(TILES)[:, None, None]
    k1 = np.arange(BLOCKS)[None, :, None]
    block = np.arange(BLOCKS).reshape(SEQ, CH).T.reshape(1, 1, BLOCKS)
    phase = ((TILES * block + tile) * (4 * k1 + 1) % (4 * TOKENS)) * (step / (4 * TOKENS))
    outer = np.concatenate([np.cos(phase), -np.sin(phase)], axis=1)
    lane = np.arange(LANES)[None, :]
    phase = lane * (np.arange(BLOCKS)[:, None] + 0.25) * (step / LENGTH)
    turn = np.stack([np.cos(phase), -np.sin(phase)])
    lane = np.arange(LANES)[None, :, None]
    k2 = np.arange(LANES)[None, None, :]
    phase = (lane * (TILES * k2 + tile) % TOKENS) * (step / TOKENS)
    cos, sin = np.cos(phase), np.sin(phase)
    inner = np.concatenate(
        [np.concatenate([cos, -sin], axis=2), np.concatenate([sin, cos], axis=2)], axis=1
    )
    narrow = ml_dtypes.bfloat16
    return dict(
        outer=outer.astype(narrow),
        turn=turn.astype(np.float32),
        inner=inner.astype(narrow),
    )


def dot(left, right):
    return jnp.dot(left, right, preferred_element_type=F32)


def dot_back(left, right):
    dims = (((1,), (1,)), ((), ()))
    return lax.dot_general(left, right, dims, preferred_element_type=F32)


def call(body, name, out_shape, scratch, in_specs, out_specs, flops, nbytes, limit=16):
    return pl.pallas_call(
        body,
        out_shape=out_shape,
        in_specs=in_specs,
        out_specs=out_specs,
        scratch_shapes=scratch,
        compiler_params=pltpu.CompilerParams(vmem_limit_bytes=limit * 1024 * 1024),
        cost_estimate=pl.CostEstimate(flops=flops, bytes_accessed=nbytes, transcendentals=0),
        name=name,
    )


def shape(dims, dtype):
    return jax.ShapeDtypeStruct(dims, dtype)


def lanes_of(x):
    return lax.broadcasted_iota(jnp.int32, x.shape, 1)


def columns(rows, tap_rows):
    tap_rows[...] = jnp.zeros(tap_rows.shape, F32)
    at = 0
    for row in rows:
        tap_rows[at : at + row.shape[0], :] = row
        at += row.shape[0]
    return tap_rows[...].T


def taps_of(cols, stream):
    return [cols[:, 3 * stream + i : 3 * stream + i + 1] for i in range(3)]


def moved(x):
    src = lax.broadcasted_iota(jnp.int32, (2 * LANES, 2 * LANES), 0)
    dst = lax.broadcasted_iota(jnp.int32, (2 * LANES, 2 * LANES), 1)
    shift = (src - LANES == dst % LANES - 1 - dst // LANES).astype(BF16)
    count = x.shape[0]
    tiles = x.shape[1] // LANES
    wide = jnp.concatenate([x[:, -LANES:], x], axis=1)
    both = dot(
        jnp.concatenate([wide[:, c * LANES : (c + 2) * LANES] for c in range(tiles)], axis=0), shift
    )
    both = [both[c * count : (c + 1) * count] for c in range(tiles)]
    return tuple(
        jnp.concatenate([tile[:, i * LANES : (i + 1) * LANES] for tile in both], axis=1)
        for i in range(2)
    )


def causal(x, taps):
    back1, back2 = moved(x)
    return taps[0] * x.astype(F32) + taps[1] * back1 + taps[2] * back2


def with_edges(x, taps):
    back1, back2 = moved(x)
    sums = taps[0] * x.astype(F32) + taps[1] * back1 + taps[2] * back2
    lane = lax.broadcasted_iota(jnp.int32, (x.shape[0], LANES), 1)
    near = jnp.where(lane < 1, back1[:, :LANES], 0.0)
    far = jnp.where(lane < 2, back2[:, :LANES], 0.0)
    onward = taps[1] * near + taps[2] * far
    return sums, sums[:, :LANES] - onward, onward


def gate_body(
    q_ref, k_ref, v_ref, taps_ref, skip_ref, out_ref,
    taps_buf, skip_buf, q_buf, k_buf, v_buf, tap_rows, rows, small, sems
):
    def small_copies():
        pairs = [(taps_ref, taps_buf), (skip_ref, skip_buf)]
        pairs += [
            (q_ref.at[:, pl.ds(i * (TOKENS - LANES), LANES)], q_buf.at[i]) for i in range(2)
        ]
        return [pltpu.make_async_copy(a, b, small.at[i]) for i, (a, b) in enumerate(pairs)]

    copies = small_copies() + [
        pltpu.make_async_copy(k_ref, k_buf, sems.at[0]),
        pltpu.make_async_copy(v_ref, v_buf, sems.at[1]),
    ]
    for copy in copies:
        copy.start()
    for copy in copies[:2]:
        copy.wait()
    cols = columns([taps_buf[0], taps_buf[1], taps_buf[2], skip_buf[...]], tap_rows)
    for copy in copies[2:]:
        copy.wait()
    query_taps, key_taps, value_taps = (taps_of(cols, stream) for stream in range(3))
    key, key_own, key_onward = with_edges(k_buf[...], key_taps)
    value, value_own, value_onward = with_edges(v_buf[...], value_taps)
    query = jnp.concatenate([q_buf[0], q_buf[1]], axis=1)
    _, query_own, query_onward = with_edges(query, query_taps)
    gated = key * value
    for c in range(TILES):
        rows[pl.ds(c, CHANNELS, stride=WIDTH), :] = gated[:, c * LANES : (c + 1) * LANES]
    lane = lanes_of(key_own)
    own = jnp.where(lane < 2, key_own, pltpu.roll(query_own, 2, 1))
    own_value = pltpu.roll(jnp.where(lane < 2, value_own, cols[:, 9:10]), 4, 1)
    onward = key_onward + pltpu.roll(query_onward, 2, 1) + pltpu.roll(value_onward, 4, 1)
    edge = jnp.where(lane < 8, own_value, pltpu.roll(onward, 8, 1))
    rows[pl.ds(TILES, CHANNELS, stride=WIDTH), :] = jnp.where(lane < 4, own, edge)
    out_ref[...] = rows[...].astype(BF16)


def gate(q, k, v, taps, skip):
    return call(
        gate_body,
        "gate",
        shape((CHANNELS * WIDTH, LANES), BF16),
        [
            pltpu.VMEM((3, 3, CHANNELS), F32),
            pltpu.VMEM((1, CHANNELS), F32),
            pltpu.VMEM((2, CHANNELS, LANES), BF16),
            pltpu.VMEM((CHANNELS, TOKENS), BF16),
            pltpu.VMEM((CHANNELS, TOKENS), BF16),
            pltpu.VMEM((LANES, CHANNELS), F32),
            pltpu.VMEM((CHANNELS * WIDTH, LANES), F32),
            pltpu.SemaphoreType.DMA((4,)),
            pltpu.SemaphoreType.DMA((2,)),
        ],
        [HBM] * 5,
        VMEM,
        10**7,
        2 * 1024 * 1024,
        GATE_LIMIT,
    )(q, k, v, taps, skip)


def eight_points(re, im):
    half = math.sqrt(0.5)
    out_re, out_im = [None] * 8, [None] * 8

    def four_points(re, im, first):
        sum_re = [re[i] + re[i + 2] for i in range(2)]
        sum_im = [im[i] + im[i + 2] for i in range(2)]
        dif_re = [re[i] - re[i + 2] for i in range(2)]
        dif_im = [im[i] - im[i + 2] for i in range(2)]
        out_re[first], out_im[first] = sum_re[0] + sum_re[1], sum_im[0] + sum_im[1]
        out_re[first + 4], out_im[first + 4] = sum_re[0] - sum_re[1], sum_im[0] - sum_im[1]
        out_re[first + 2], out_im[first + 2] = dif_re[0] + dif_im[1], dif_im[0] - dif_re[1]
        out_re[first + 6], out_im[first + 6] = dif_re[0] - dif_im[1], dif_im[0] + dif_re[1]

    four_points([re[i] + re[i + 4] for i in range(4)], [im[i] + im[i + 4] for i in range(4)], 0)
    re = [re[i] - re[i + 4] for i in range(4)]
    im = [im[i] - im[i + 4] for i in range(4)]
    turned_re = [re[0], (re[1] + im[1]) * half, im[2], (im[3] - re[3]) * half]
    turned_im = [im[0], (im[1] - re[1]) * half, -re[2], (re[3] + im[3]) * -half]
    four_points(turned_re, turned_im, 1)
    return out_re, out_im


def forward(signals, outer_ref, turn_ref, section, turned):
    for c in range(TILES):
        section[c] = dot(outer_ref[c], signals[c])
    for row in range(0, BLOCKS, 16):
        turn_re, turn_im = turn_ref[0, row : row + 16, :], turn_ref[1, row : row + 16, :]
        for j in range(2):
            half = slice(j * LANES, (j + 1) * LANES)
            re = [section[c, row : row + 16, half] for c in range(TILES)]
            im = [section[c, BLOCKS + row : BLOCKS + row + 16, half] for c in range(TILES)]
            re, im = eight_points(re, im)
            at = slice(j * BLOCKS + row, j * BLOCKS + row + 16)
            for kc in range(TILES):
                turned[kc, at, :LANES] = (re[kc] * turn_re - im[kc] * turn_im).astype(BF16)
                turned[kc, at, LANES:] = (re[kc] * turn_im + im[kc] * turn_re).astype(BF16)


def filter_body(
    filt_ref, outer_ref, turn_ref, inner_ref, spec_ref,
    spec_buf, rows, section, turned, spec_sems
):
    rows[...] = filt_ref[...].astype(F32)
    signals = []
    for c in range(TILES):
        halves = []
        for j in range(2):
            parts = [
                rows[pl.ds(2 * (g * TILES + c) + j, SEQ, stride=2 * TILES * CH), :]
                for g in range(CH)
            ]
            halves.append(jnp.concatenate(parts, axis=0))
        signals.append(jnp.concatenate(halves, axis=1).astype(BF16))
    forward(signals, outer_ref, turn_ref, section, turned)
    out_copies = []
    for kc in range(TILES):
        spec_buf[kc] = (dot(turned[kc], inner_ref[kc]) * (1.0 / LENGTH)).astype(BF16)
        out_copies.append(pltpu.make_async_copy(spec_buf.at[kc], spec_ref.at[kc], spec_sems.at[kc]))
        out_copies[-1].start()
    for copy in out_copies:
        copy.wait()


def filter_spectra(filt, consts):
    names = ("outer", "turn", "inner")
    spec = (TILES, 2 * BLOCKS, 2 * LANES)
    return call(
        filter_body,
        "filter_spectra",
        shape(spec, BF16),
        [
            pltpu.VMEM(spec, BF16),
            pltpu.VMEM((2 * BLOCKS * TILES, LANES), F32),
            pltpu.VMEM(spec, F32),
            pltpu.VMEM(spec, BF16),
            pltpu.SemaphoreType.DMA((TILES,)),
        ],
        [VMEM] * 4,
        HBM,
        10**9,
        4 * 1024 * 1024,
        FILTER_LIMIT,
    )(filt, *(consts[name] for name in names))


def direct_body(
    q_ref, k_ref, v_ref, taps_ref, skip_ref, query_ref, direct_ref,
    streams, taps_buf, skip_buf, query_buf, direct_buf, tap_rows, cols_buf, small, in_sems, out_sems
):
    first = [
        pltpu.make_async_copy(taps_ref, taps_buf, small.at[0]),
        pltpu.make_async_copy(skip_ref, skip_buf, small.at[1]),
    ]
    places = [pl.ds(step * DIRECT_ROWS, DIRECT_ROWS) for step in range(DIRECT_STEPS)]
    copies = [
        [
            pltpu.make_async_copy(ref.at[place], streams.at[i, place], in_sems.at[i, step])
            for i, ref in enumerate((q_ref, k_ref, v_ref))
        ]
        for step, place in enumerate(places)
    ]
    for copy in first + [copy for group in copies for copy in group]:
        copy.start()
    for copy in first:
        copy.wait()
    out_copies = []
    cols_buf[...] = columns([taps_buf[0], taps_buf[1], taps_buf[2], skip_buf[...]], tap_rows)
    for step in range(DIRECT_STEPS):
        for copy in copies[step]:
            copy.wait()
        at = slice(step * DIRECT_ROWS, (step + 1) * DIRECT_ROWS)
        cols = cols_buf[at, :]
        query, key, value = (causal(streams[i, at, :], taps_of(cols, i)) for i in range(3))
        query_buf[at, :] = query
        direct_buf[at, :] = cols[:, 9:10] * (key * value).astype(BF16).astype(F32)
        for i, (buf, ref) in enumerate(((query_buf, query_ref), (direct_buf, direct_ref))):
            out_copies.append(
                pltpu.make_async_copy(buf.at[places[step]], ref.at[places[step]], out_sems.at[i, step])
            )
            out_copies[-1].start()
    for copy in out_copies:
        copy.wait()


def direct(q, k, v, taps, skip):
    return call(
        direct_body,
        "direct",
        (shape((CHANNELS, TOKENS), F32), shape((CHANNELS, TOKENS), F32)),
        [
            pltpu.VMEM((3, CHANNELS, TOKENS), BF16),
            pltpu.VMEM((3, 3, CHANNELS), F32),
            pltpu.VMEM((1, CHANNELS), F32),
            pltpu.VMEM((CHANNELS, TOKENS), F32),
            pltpu.VMEM((CHANNELS, TOKENS), F32),
            pltpu.VMEM((LANES, CHANNELS), F32),
            pltpu.VMEM((CHANNELS, LANES), F32),
            pltpu.SemaphoreType.DMA((2,)),
            pltpu.SemaphoreType.DMA((3, DIRECT_STEPS)),
            pltpu.SemaphoreType.DMA((2, DIRECT_STEPS)),
        ],
        [HBM] * 5,
        (HBM,) * 2,
        10**9,
        4 * 1024 * 1024,
        DIRECT_LIMIT,
    )(q, k, v, taps, skip)


def conv_body(
    arrived_ref, spec_ref, outer_ref, turn_ref, inner_ref, out_ref,
    rows, section, turned, back, edges
):
    rows[...] = arrived_ref[...].astype(F32)

    def arrived(j, c):
        return rows[pl.ds(j * WIDTH + c, BLOCKS, stride=2 * WIDTH), :]

    signals = []
    for c in range(TILES):
        halves = [arrived(j, c) for j in range(2)]
        if c == 0:
            for j in range(2):
                edge = arrived(j, TILES)
                last = edge[BLOCKS - SEQ :]
                step = lax.broadcasted_iota(jnp.int32, last.shape, 0)
                last = jnp.where(step == 0, 0.0, pltpu.roll(last, 1, 0))
                before = jnp.concatenate([last, edge[: BLOCKS - SEQ]], axis=0)
                total = edge + pltpu.roll(before, LANES - 8, 1)
                gated = (total * pltpu.roll(total, LANES - 4, 1)).astype(BF16).astype(F32)
                edges[0, j] = pltpu.roll(total, LANES - 2, 1)
                edges[1, j] = pltpu.roll(total, LANES - 6, 1) * gated
                halves[j] = jnp.where(lanes_of(gated) < 2, gated, halves[j])
        signals.append(jnp.concatenate(halves, axis=1).astype(BF16))
    forward(signals, outer_ref, turn_ref, section, turned)
    for kc in range(TILES):
        spectrum = dot(turned[kc], inner_ref[kc])
        re, im = spectrum[:, :LANES], spectrum[:, LANES:]
        spec = spec_ref[kc].astype(F32)
        filt_re, filt_im = spec[:, :LANES], spec[:, LANES:]
        parts = [re * filt_re - im * filt_im, re * filt_im + im * filt_re]
        section[kc] = dot_back(jnp.concatenate(parts, axis=1).astype(BF16), inner_ref[kc])
    for row in range(0, BLOCKS, 16):
        turn_re, turn_im = turn_ref[0, row : row + 16, :], turn_ref[1, row : row + 16, :]
        for j in range(2):
            at = slice(j * BLOCKS + row, j * BLOCKS + row + 16)
            re, im = [], []
            for kc in range(TILES):
                part_re, part_im = section[kc, at, :LANES], section[kc, at, LANES:]
                re.append(part_re * turn_re + part_im * turn_im)
                im.append(part_im * turn_re - part_re * turn_im)
            im, re = eight_points(im, re)
            half = slice(j * LANES, (j + 1) * LANES)
            for c in range(TILES):
                back[c, row : row + 16, half] = re[c].astype(BF16)
                back[c, BLOCKS + row : BLOCKS + row + 16, half] = im[c].astype(BF16)
    for c in range(TILES):
        result = lax.dot_general(
            outer_ref[c], back[c], (((0,), (0,)), ((), ())), preferred_element_type=F32
        )
        for j in range(2):
            half = result[:, j * LANES : (j + 1) * LANES]
            if c == 0:
                start = edges[0, j] * (half.astype(BF16).astype(F32) + edges[1, j])
                half = jnp.where(lanes_of(half) < 2, start, half)
            rows[pl.ds(j * TILES + c, BLOCKS, stride=BODY), :] = half
    out_ref[...] = rows[: BLOCKS * BODY, :].reshape(BLOCKS, BODY, LANES).astype(BF16)


def conv(arrived, spec, consts):
    names = ("outer", "turn", "inner")
    return call(
        conv_body,
        "conv",
        shape((BLOCKS, BODY, LANES), BF16),
        [
            pltpu.VMEM((BLOCKS * 2 * WIDTH, LANES), F32),
            pltpu.VMEM((TILES, 2 * BLOCKS, 2 * LANES), F32),
            pltpu.VMEM((TILES, 2 * BLOCKS, 2 * LANES), BF16),
            pltpu.VMEM((TILES, 2 * BLOCKS, 2 * LANES), BF16),
            pltpu.VMEM((2, 2, BLOCKS, LANES), F32),
        ],
        [VMEM] * 5,
        VMEM,
        10**9,
        8 * 1024 * 1024,
        CONV_LIMIT,
    )(arrived, spec, *(consts[name] for name in names))


def final_body(returned_ref, query_ref, direct_ref, out_ref, rows, out_buf, sems):
    copies = []
    for step in range(STEPS):
        at = slice(step * ROWS, (step + 1) * ROWS)
        message = returned_ref[step * ROWS // 2 : (step + 1) * ROWS // 2].astype(F32)
        rows[...] = message.reshape(ROWS * TILES, LANES)
        for c in range(TILES):
            lanes = slice(c * LANES, (c + 1) * LANES)
            long_result = rows[pl.ds(c, ROWS, stride=TILES), :]
            mixed = query_ref[at, lanes] * (long_result + direct_ref[at, lanes])
            if c == 0:
                mixed = jnp.where(lanes_of(mixed) < 2, long_result, mixed)
            out_buf[at, lanes] = mixed.astype(BF16)
        place = pl.ds(step * ROWS, ROWS)
        copies.append(pltpu.make_async_copy(out_buf.at[place], out_ref.at[place], sems.at[step]))
        copies[-1].start()
    for copy in copies:
        copy.wait()


def final(returned, query, direct_term):
    return call(
        final_body,
        "final",
        shape((CHANNELS, TOKENS), BF16),
        [
            pltpu.VMEM((ROWS * TILES, LANES), F32),
            pltpu.VMEM((CHANNELS, TOKENS), BF16),
            pltpu.SemaphoreType.DMA((STEPS,)),
        ],
        [VMEM] * 3,
        HBM,
        10**6,
        2 * 1024 * 1024,
        FINAL_LIMIT,
    )(returned, query, direct_term)


def exchange(messages):
    return lax.all_to_all(messages, OWNERS, split_axis=0, concat_axis=0, tiled=True)


def shards(consts, q, k, v, short_taps, long_filter, skip_gain):
    consts = {name: jnp.asarray(table) for name, table in consts.items()}
    skip = skip_gain[None]
    messages = gate(q, k, v, short_taps, skip).reshape(BLOCKS, WIDTH, 2, LANES)
    messages, q, k, v, long_filter = lax.optimization_barrier((messages, q, k, v, long_filter))
    arrived = exchange(messages).reshape(BLOCKS * 2 * WIDTH, LANES)
    filt = long_filter.reshape(2, BLOCKS * TILES, LANES).swapaxes(0, 1)
    filt = filt.reshape(2 * BLOCKS * TILES, LANES)
    spec = filter_spectra(filt, consts)
    spec, q, k, v = lax.optimization_barrier((spec, q, k, v))
    query, direct_term = direct(q, k, v, short_taps, skip)
    spec, query, direct_term = lax.optimization_barrier((spec, query, direct_term))
    returned = exchange(conv(arrived, spec, consts))
    return final(returned, query, direct_term)


def solution(mesh):
    tokens = P(None, AXES)
    placed = (tokens, tokens, tokens, P(), P("ch", "seq", None, None), P())
    return jax.shard_map(
        functools.partial(shards, tables()),
        mesh=mesh,
        in_specs=placed,
        out_specs=tokens,
        check_vma=False,
    )
```

```python
import functools
import math

import jax
import jax.numpy as jnp
import ml_dtypes
import numpy as np
from jax import lax
from jax.experimental import pallas as pl
from jax.experimental.pallas import tpu as pltpu
from jax.sharding import PartitionSpec as P

F32 = jnp.float32
BF16 = jnp.bfloat16
LANES = 128
TOKENS = 1024
TILES = TOKENS // LANES
HALF = TILES // 2
BLOCKS = 128
LENGTH = BLOCKS * TOKENS
CHANNELS = 256
SEQ = 8
CH = 16
BODY = 2 * TILES
WIDTH = TILES + 1
GATE_LIMIT, FILTER_LIMIT, DIRECT_LIMIT, CONV_LIMIT, FINAL_LIMIT = 60, 60, 60, 16, 16
ROWS = 64
STEPS = CHANNELS // ROWS
DIRECT_ROWS = 128
DIRECT_STEPS = CHANNELS // DIRECT_ROWS
AXES = ("seq", "ch")
OWNERS = ("ch", "seq")
VMEM = pl.BlockSpec(memory_space=pltpu.VMEM)
HBM = pl.BlockSpec(memory_space=pltpu.HBM)


def tables():
    step = 2.0 * math.pi
    tile = np.arange(TILES)[:, None, None]
    k1 = np.arange(BLOCKS)[None, :, None]
    block = np.arange(BLOCKS).reshape(SEQ, CH).T.reshape(1, 1, BLOCKS)
    phase = ((TILES * block + tile) * (4 * k1 + 1) % (4 * TOKENS)) * (step / (4 * TOKENS))
    outer = np.concatenate([np.cos(phase), -np.sin(phase)], axis=1)
    lane = np.arange(LANES)[None, :]
    phase = lane * (np.arange(BLOCKS)[:, None] + 0.25) * (step / LENGTH)
    turn = np.stack([np.cos(phase), -np.sin(phase)])
    lane = np.arange(LANES)[None, :, None]
    k2 = np.arange(LANES)[None, None, :]
    phase = (lane * (TILES * k2 + tile) % TOKENS) * (step / TOKENS)
    cos, sin = np.cos(phase), np.sin(phase)
    inner = np.concatenate([cos, -sin], axis=2)
    narrow = ml_dtypes.bfloat16
    return dict(
        outer=outer.astype(narrow),
        turn=turn.astype(np.float32),
        inner=inner.astype(narrow),
    )


def dot(left, right):
    return jnp.dot(left, right, preferred_element_type=F32)


def dot_back(left, right):
    dims = (((1,), (1,)), ((), ()))
    return lax.dot_general(left, right, dims, preferred_element_type=F32)


def call(body, name, out_shape, scratch, in_specs, out_specs, flops, nbytes, limit=16):
    return pl.pallas_call(
        body,
        out_shape=out_shape,
        in_specs=in_specs,
        out_specs=out_specs,
        scratch_shapes=scratch,
        compiler_params=pltpu.CompilerParams(vmem_limit_bytes=limit * 1024 * 1024),
        cost_estimate=pl.CostEstimate(flops=flops, bytes_accessed=nbytes, transcendentals=0),
        name=name,
    )


def shape(dims, dtype):
    return jax.ShapeDtypeStruct(dims, dtype)


def lanes_of(x):
    return lax.broadcasted_iota(jnp.int32, x.shape, 1)


def columns(rows, tap_rows):
    tap_rows[...] = jnp.zeros(tap_rows.shape, F32)
    at = 0
    for row in rows:
        tap_rows[at : at + row.shape[0], :] = row
        at += row.shape[0]
    return tap_rows[...].T


def taps_of(cols, stream):
    return [cols[:, 3 * stream + i : 3 * stream + i + 1] for i in range(3)]


def moved(x):
    src = lax.broadcasted_iota(jnp.int32, (2 * LANES, 2 * LANES), 0)
    dst = lax.broadcasted_iota(jnp.int32, (2 * LANES, 2 * LANES), 1)
    shift = (src - LANES == dst % LANES - 1 - dst // LANES).astype(BF16)
    count = x.shape[0]
    tiles = x.shape[1] // LANES
    wide = jnp.concatenate([x[:, -LANES:], x], axis=1)
    both = dot(
        jnp.concatenate([wide[:, c * LANES : (c + 2) * LANES] for c in range(tiles)], axis=0), shift
    )
    both = [both[c * count : (c + 1) * count] for c in range(tiles)]
    return tuple(
        jnp.concatenate([tile[:, i * LANES : (i + 1) * LANES] for tile in both], axis=1)
        for i in range(2)
    )


def causal(x, taps):
    back1, back2 = moved(x)
    return taps[0] * x.astype(F32) + taps[1] * back1 + taps[2] * back2


def with_edges(x, taps):
    back1, back2 = moved(x)
    sums = taps[0] * x.astype(F32) + taps[1] * back1 + taps[2] * back2
    lane = lax.broadcasted_iota(jnp.int32, (x.shape[0], LANES), 1)
    near = jnp.where(lane < 1, back1[:, :LANES], 0.0)
    far = jnp.where(lane < 2, back2[:, :LANES], 0.0)
    onward = taps[1] * near + taps[2] * far
    return sums, sums[:, :LANES] - onward, onward


def gate_body(
    q_ref, k_ref, v_ref, taps_ref, skip_ref, out_ref,
    taps_buf, skip_buf, q_buf, k_buf, v_buf, tap_rows, rows, small, sems
):
    def small_copies():
        pairs = [(taps_ref, taps_buf), (skip_ref, skip_buf)]
        pairs += [
            (q_ref.at[:, pl.ds(i * (TOKENS - LANES), LANES)], q_buf.at[i]) for i in range(2)
        ]
        return [pltpu.make_async_copy(a, b, small.at[i]) for i, (a, b) in enumerate(pairs)]

    copies = small_copies() + [
        pltpu.make_async_copy(k_ref, k_buf, sems.at[0]),
        pltpu.make_async_copy(v_ref, v_buf, sems.at[1]),
    ]
    for copy in copies:
        copy.start()
    for copy in copies[:2]:
        copy.wait()
    cols = columns([taps_buf[0], taps_buf[1], taps_buf[2], skip_buf[...]], tap_rows)
    for copy in copies[2:]:
        copy.wait()
    query_taps, key_taps, value_taps = (taps_of(cols, stream) for stream in range(3))
    key, key_own, key_onward = with_edges(k_buf[...], key_taps)
    value, value_own, value_onward = with_edges(v_buf[...], value_taps)
    query = jnp.concatenate([q_buf[0], q_buf[1]], axis=1)
    _, query_own, query_onward = with_edges(query, query_taps)
    gated = key * value
    for c in range(TILES):
        rows[pl.ds(c, CHANNELS, stride=WIDTH), :] = gated[:, c * LANES : (c + 1) * LANES]
    lane = lanes_of(key_own)
    own = jnp.where(lane < 2, key_own, pltpu.roll(query_own, 2, 1))
    own_value = pltpu.roll(jnp.where(lane < 2, value_own, cols[:, 9:10]), 4, 1)
    onward = key_onward + pltpu.roll(query_onward, 2, 1) + pltpu.roll(value_onward, 4, 1)
    edge = jnp.where(lane < 8, own_value, pltpu.roll(onward, 8, 1))
    rows[pl.ds(TILES, CHANNELS, stride=WIDTH), :] = jnp.where(lane < 4, own, edge)
    out_ref[...] = rows[...].astype(BF16)


def gate(q, k, v, taps, skip):
    return call(
        gate_body,
        "gate",
        shape((CHANNELS * WIDTH, LANES), BF16),
        [
            pltpu.VMEM((3, 3, CHANNELS), F32),
            pltpu.VMEM((1, CHANNELS), F32),
            pltpu.VMEM((2, CHANNELS, LANES), BF16),
            pltpu.VMEM((CHANNELS, TOKENS), BF16),
            pltpu.VMEM((CHANNELS, TOKENS), BF16),
            pltpu.VMEM((LANES, CHANNELS), F32),
            pltpu.VMEM((CHANNELS * WIDTH, LANES), F32),
            pltpu.SemaphoreType.DMA((4,)),
            pltpu.SemaphoreType.DMA((2,)),
        ],
        [HBM] * 5,
        VMEM,
        10**7,
        2 * 1024 * 1024,
        GATE_LIMIT,
    )(q, k, v, taps, skip)


def sums_and_differences(outer_ref, c):
    near, far = outer_ref[c], outer_ref[c + HALF]
    return jnp.concatenate(
        [jnp.concatenate([near, far], axis=1), jnp.concatenate([near, -far], axis=1)], axis=0
    )


def complex_table(inner_ref, kc):
    real = inner_ref[kc]
    imag = jnp.concatenate([-real[:, LANES:], real[:, :LANES]], axis=1)
    return jnp.concatenate([real, imag], axis=0)


def four_points(re, im):
    sum_re = [re[i] + re[i + 2] for i in range(2)]
    sum_im = [im[i] + im[i + 2] for i in range(2)]
    dif_re = [re[i] - re[i + 2] for i in range(2)]
    dif_im = [im[i] - im[i + 2] for i in range(2)]
    out_re = [sum_re[0] + sum_re[1], dif_re[0] + dif_im[1], sum_re[0] - sum_re[1], dif_re[0] - dif_im[1]]
    out_im = [sum_im[0] + sum_im[1], dif_im[0] - dif_re[1], sum_im[0] - sum_im[1], dif_im[0] + dif_re[1]]
    return out_re, out_im


def eighths(re, im):
    half = math.sqrt(0.5)
    out_re = [re[0], (re[1] + im[1]) * half, im[2], (im[3] - re[3]) * half]
    out_im = [im[0], (im[1] - re[1]) * half, -re[2], (re[3] + im[3]) * -half]
    return out_re, out_im


def forward(signals, outer_ref, turn_ref, section, turned):
    for c in range(HALF):
        section[c] = dot(
            sums_and_differences(outer_ref, c),
            jnp.concatenate([signals[c], signals[c + HALF]], axis=0),
        )
    for row in range(0, BLOCKS, 16):
        turn_re, turn_im = turn_ref[0, row : row + 16, :], turn_ref[1, row : row + 16, :]
        for j in range(2):
            half = slice(j * LANES, (j + 1) * LANES)
            parts = [
                [section[c, m * BLOCKS + row : m * BLOCKS + row + 16, half] for c in range(HALF)]
                for m in range(4)
            ]
            even = four_points(parts[0], parts[1])
            odd = four_points(*eighths(parts[2], parts[3]))
            at = slice(j * BLOCKS + row, j * BLOCKS + row + 16)
            for kc in range(TILES):
                re, im = (part[kc // 2] for part in (odd if kc % 2 else even))
                turned[kc, at, :LANES] = (re * turn_re - im * turn_im).astype(BF16)
                turned[kc, at, LANES:] = (re * turn_im + im * turn_re).astype(BF16)


def filter_body(
    filt_ref, outer_ref, turn_ref, inner_ref, spec_ref,
    spec_buf, rows, section, turned, spec_sems
):
    rows[...] = filt_ref[...].astype(F32)
    signals = []
    for c in range(TILES):
        halves = []
        for j in range(2):
            parts = [
                rows[pl.ds(2 * (g * TILES + c) + j, SEQ, stride=2 * TILES * CH), :]
                for g in range(CH)
            ]
            halves.append(jnp.concatenate(parts, axis=0))
        signals.append(jnp.concatenate(halves, axis=1).astype(BF16))
    forward(signals, outer_ref, turn_ref, section, turned)
    out_copies = []
    for kc in range(TILES):
        spec_buf[kc] = (dot(turned[kc], complex_table(inner_ref, kc)) * (1.0 / LENGTH)).astype(BF16)
        out_copies.append(pltpu.make_async_copy(spec_buf.at[kc], spec_ref.at[kc], spec_sems.at[kc]))
        out_copies[-1].start()
    for copy in out_copies:
        copy.wait()


def filter_spectra(filt, consts):
    names = ("outer", "turn", "inner")
    spec = (TILES, 2 * BLOCKS, 2 * LANES)
    return call(
        filter_body,
        "filter_spectra",
        shape(spec, BF16),
        [
            pltpu.VMEM(spec, BF16),
            pltpu.VMEM((2 * BLOCKS * TILES, LANES), F32),
            pltpu.VMEM((HALF, 4 * BLOCKS, 2 * LANES), F32),
            pltpu.VMEM(spec, BF16),
            pltpu.SemaphoreType.DMA((TILES,)),
        ],
        [VMEM] * 4,
        HBM,
        10**9,
        4 * 1024 * 1024,
        FILTER_LIMIT,
    )(filt, *(consts[name] for name in names))


def direct_body(
    q_ref, k_ref, v_ref, taps_ref, skip_ref, query_ref, direct_ref,
    streams, taps_buf, skip_buf, query_buf, direct_buf, tap_rows, cols_buf, small, in_sems, out_sems
):
    first = [
        pltpu.make_async_copy(taps_ref, taps_buf, small.at[0]),
        pltpu.make_async_copy(skip_ref, skip_buf, small.at[1]),
    ]
    places = [pl.ds(step * DIRECT_ROWS, DIRECT_ROWS) for step in range(DIRECT_STEPS)]
    copies = [
        [
            pltpu.make_async_copy(ref.at[place], streams.at[i, place], in_sems.at[i, step])
            for i, ref in enumerate((q_ref, k_ref, v_ref))
        ]
        for step, place in enumerate(places)
    ]
    for copy in first + [copy for group in copies for copy in group]:
        copy.start()
    for copy in first:
        copy.wait()
    out_copies = []
    cols_buf[...] = columns([taps_buf[0], taps_buf[1], taps_buf[2], skip_buf[...]], tap_rows)
    for step in range(DIRECT_STEPS):
        for copy in copies[step]:
            copy.wait()
        at = slice(step * DIRECT_ROWS, (step + 1) * DIRECT_ROWS)
        cols = cols_buf[at, :]
        query, key, value = (causal(streams[i, at, :], taps_of(cols, i)) for i in range(3))
        query_buf[at, :] = query
        direct_buf[at, :] = cols[:, 9:10] * (key * value).astype(BF16).astype(F32)
        for i, (buf, ref) in enumerate(((query_buf, query_ref), (direct_buf, direct_ref))):
            out_copies.append(
                pltpu.make_async_copy(buf.at[places[step]], ref.at[places[step]], out_sems.at[i, step])
            )
            out_copies[-1].start()
    for copy in out_copies:
        copy.wait()


def direct(q, k, v, taps, skip):
    return call(
        direct_body,
        "direct",
        (shape((CHANNELS, TOKENS), F32), shape((CHANNELS, TOKENS), F32)),
        [
            pltpu.VMEM((3, CHANNELS, TOKENS), BF16),
            pltpu.VMEM((3, 3, CHANNELS), F32),
            pltpu.VMEM((1, CHANNELS), F32),
            pltpu.VMEM((CHANNELS, TOKENS), F32),
            pltpu.VMEM((CHANNELS, TOKENS), F32),
            pltpu.VMEM((LANES, CHANNELS), F32),
            pltpu.VMEM((CHANNELS, LANES), F32),
            pltpu.SemaphoreType.DMA((2,)),
            pltpu.SemaphoreType.DMA((3, DIRECT_STEPS)),
            pltpu.SemaphoreType.DMA((2, DIRECT_STEPS)),
        ],
        [HBM] * 5,
        (HBM,) * 2,
        10**9,
        4 * 1024 * 1024,
        DIRECT_LIMIT,
    )(q, k, v, taps, skip)


def conv_body(
    arrived_ref, spec_ref, outer_ref, turn_ref, inner_ref, out_ref,
    rows, section, turned, product, back, edges
):
    rows[...] = arrived_ref[...].astype(F32)

    def arrived(j, c):
        return rows[pl.ds(j * WIDTH + c, BLOCKS, stride=2 * WIDTH), :]

    signals = []
    for c in range(TILES):
        halves = [arrived(j, c) for j in range(2)]
        if c == 0:
            for j in range(2):
                edge = arrived(j, TILES)
                last = edge[BLOCKS - SEQ :]
                step = lax.broadcasted_iota(jnp.int32, last.shape, 0)
                last = jnp.where(step == 0, 0.0, pltpu.roll(last, 1, 0))
                before = jnp.concatenate([last, edge[: BLOCKS - SEQ]], axis=0)
                total = edge + pltpu.roll(before, LANES - 8, 1)
                gated = (total * pltpu.roll(total, LANES - 4, 1)).astype(BF16).astype(F32)
                edges[0, j] = pltpu.roll(total, LANES - 2, 1)
                edges[1, j] = pltpu.roll(total, LANES - 6, 1) * gated
                halves[j] = jnp.where(lanes_of(gated) < 2, gated, halves[j])
        signals.append(jnp.concatenate(halves, axis=1).astype(BF16))
    forward(signals, outer_ref, turn_ref, section, turned)
    for kc in range(TILES):
        table = complex_table(inner_ref, kc)
        spectrum = dot(turned[kc], table)
        re, im = spectrum[:, :LANES], spectrum[:, LANES:]
        spec = spec_ref[kc].astype(F32)
        filt_re, filt_im = spec[:, :LANES], spec[:, LANES:]
        parts = [re * filt_re - im * filt_im, re * filt_im + im * filt_re]
        product[kc] = dot_back(jnp.concatenate(parts, axis=1).astype(BF16), table)
    for row in range(0, BLOCKS, 16):
        turn_re, turn_im = turn_ref[0, row : row + 16, :], turn_ref[1, row : row + 16, :]
        for j in range(2):
            at = slice(j * BLOCKS + row, j * BLOCKS + row + 16)
            re, im = [], []
            for kc in range(TILES):
                part_re, part_im = product[kc, at, :LANES], product[kc, at, LANES:]
                re.append(part_re * turn_re + part_im * turn_im)
                im.append(part_im * turn_re - part_re * turn_im)
            even_im, even_re = four_points(im[0::2], re[0::2])
            odd_im, odd_re = eighths(*four_points(im[1::2], re[1::2]))
            half = slice(j * LANES, (j + 1) * LANES)
            for m, part in enumerate((even_re, even_im, odd_re, odd_im)):
                for c in range(HALF):
                    back[c, m * BLOCKS + row : m * BLOCKS + row + 16, half] = part[c].astype(BF16)
    for c in range(HALF):
        result = lax.dot_general(
            sums_and_differences(outer_ref, c),
            back[c],
            (((0,), (0,)), ((), ())),
            preferred_element_type=F32,
        )
        for tile in (c, c + HALF):
            for j in range(2):
                first = BLOCKS if tile >= HALF else 0
                half = result[first : first + BLOCKS, j * LANES : (j + 1) * LANES]
                if tile == 0:
                    start = edges[0, j] * (half.astype(BF16).astype(F32) + edges[1, j])
                    half = jnp.where(lanes_of(half) < 2, start, half)
                rows[pl.ds(j * TILES + tile, BLOCKS, stride=BODY), :] = half
    out_ref[...] = rows[: BLOCKS * BODY, :].reshape(BLOCKS, BODY, LANES).astype(BF16)


def conv(arrived, spec, consts):
    names = ("outer", "turn", "inner")
    return call(
        conv_body,
        "conv",
        shape((BLOCKS, BODY, LANES), BF16),
        [
            pltpu.VMEM((BLOCKS * 2 * WIDTH, LANES), F32),
            pltpu.VMEM((HALF, 4 * BLOCKS, 2 * LANES), F32),
            pltpu.VMEM((TILES, 2 * BLOCKS, 2 * LANES), BF16),
            pltpu.VMEM((TILES, 2 * BLOCKS, 2 * LANES), F32),
            pltpu.VMEM((HALF, 4 * BLOCKS, 2 * LANES), BF16),
            pltpu.VMEM((2, 2, BLOCKS, LANES), F32),
        ],
        [VMEM] * 5,
        VMEM,
        10**9,
        8 * 1024 * 1024,
        CONV_LIMIT,
    )(arrived, spec, *(consts[name] for name in names))


def final_body(returned_ref, query_ref, direct_ref, out_ref, rows, out_buf, sems):
    copies = []
    for step in range(STEPS):
        at = slice(step * ROWS, (step + 1) * ROWS)
        message = returned_ref[step * ROWS // 2 : (step + 1) * ROWS // 2].astype(F32)
        rows[...] = message.reshape(ROWS * TILES, LANES)
        for c in range(TILES):
            lanes = slice(c * LANES, (c + 1) * LANES)
            long_result = rows[pl.ds(c, ROWS, stride=TILES), :]
            mixed = query_ref[at, lanes] * (long_result + direct_ref[at, lanes])
            if c == 0:
                mixed = jnp.where(lanes_of(mixed) < 2, long_result, mixed)
            out_buf[at, lanes] = mixed.astype(BF16)
        place = pl.ds(step * ROWS, ROWS)
        copies.append(pltpu.make_async_copy(out_buf.at[place], out_ref.at[place], sems.at[step]))
        copies[-1].start()
    for copy in copies:
        copy.wait()


def final(returned, query, direct_term):
    return call(
        final_body,
        "final",
        shape((CHANNELS, TOKENS), BF16),
        [
            pltpu.VMEM((ROWS * TILES, LANES), F32),
            pltpu.VMEM((CHANNELS, TOKENS), BF16),
            pltpu.SemaphoreType.DMA((STEPS,)),
        ],
        [VMEM] * 3,
        HBM,
        10**6,
        2 * 1024 * 1024,
        FINAL_LIMIT,
    )(returned, query, direct_term)


def exchange(messages):
    return lax.all_to_all(messages, OWNERS, split_axis=0, concat_axis=0, tiled=True)


def shards(consts, q, k, v, short_taps, long_filter, skip_gain):
    consts = {name: jnp.asarray(table) for name, table in consts.items()}
    skip = skip_gain[None]
    messages = gate(q, k, v, short_taps, skip).reshape(BLOCKS, WIDTH, 2, LANES)
    messages, q, k, v, long_filter = lax.optimization_barrier((messages, q, k, v, long_filter))
    arrived = exchange(messages).reshape(BLOCKS * 2 * WIDTH, LANES)
    filt = long_filter.reshape(2, BLOCKS * TILES, LANES).swapaxes(0, 1)
    filt = filt.reshape(2 * BLOCKS * TILES, LANES)
    spec = filter_spectra(filt, consts)
    spec, q, k, v = lax.optimization_barrier((spec, q, k, v))
    query, direct_term = direct(q, k, v, short_taps, skip)
    spec, query, direct_term = lax.optimization_barrier((spec, query, direct_term))
    returned = exchange(conv(arrived, spec, consts))
    return final(returned, query, direct_term)


def solution(mesh):
    tokens = P(None, AXES)
    placed = (tokens, tokens, tokens, P(), P("ch", "seq", None, None), P())
    return jax.shard_map(
        functools.partial(shards, tables()),
        mesh=mesh,
        in_specs=placed,
        out_specs=tokens,
        check_vma=False,
    )
```

```python
import functools
import math

import jax
import jax.numpy as jnp
import ml_dtypes
import numpy as np
from jax import lax
from jax.experimental import pallas as pl
from jax.experimental.pallas import tpu as pltpu
from jax.sharding import PartitionSpec as P

F32 = jnp.float32
BF16 = jnp.bfloat16
LANES = 128
TOKENS = 1024
TILES = TOKENS // LANES
HALF = TILES // 2
BLOCKS = 128
LENGTH = BLOCKS * TOKENS
CHANNELS = 256
SEQ = 8
CH = 16
BODY = 2 * TILES
WIDTH = TILES + 1
GATE_LIMIT, FILTER_LIMIT, DIRECT_LIMIT, CONV_LIMIT, FINAL_LIMIT = 60, 60, 60, 16, 16
ROWS = 64
STEPS = CHANNELS // ROWS
DIRECT_ROWS = 128
DIRECT_STEPS = CHANNELS // DIRECT_ROWS
AXES = ("seq", "ch")
ORDER = (0, 8, 4, 12, 2, 10, 6, 14, 1, 9, 5, 13, 3, 11, 7, 15)
PLACE = tuple(ORDER.index(g) for g in range(CH))
VMEM = pl.BlockSpec(memory_space=pltpu.VMEM)
HBM = pl.BlockSpec(memory_space=pltpu.HBM)


def tables():
    step = 2.0 * math.pi
    tile = np.arange(TILES)[:, None, None]
    k1 = np.arange(BLOCKS)[None, :, None]
    block = np.arange(BLOCKS).reshape(SEQ, CH).T[list(ORDER)].reshape(1, 1, BLOCKS)
    phase = ((TILES * block + tile) * (4 * k1 + 1) % (4 * TOKENS)) * (step / (4 * TOKENS))
    outer = np.concatenate([np.cos(phase), -np.sin(phase)], axis=1)
    lane = np.arange(LANES)[None, :]
    phase = lane * (np.arange(BLOCKS)[:, None] + 0.25) * (step / LENGTH)
    turn = np.stack([np.cos(phase), -np.sin(phase)])
    lane = np.arange(LANES)[None, :, None]
    k2 = np.arange(LANES)[None, None, :]
    phase = (lane * (TILES * k2 + tile) % TOKENS) * (step / TOKENS)
    cos, sin = np.cos(phase), np.sin(phase)
    inner = np.concatenate([cos, -sin], axis=2)
    narrow = ml_dtypes.bfloat16
    return dict(
        outer=outer.astype(narrow),
        turn=turn.astype(np.float32),
        inner=inner.astype(narrow),
    )


def dot(left, right):
    return jnp.dot(left, right, preferred_element_type=F32)


def dot_back(left, right):
    dims = (((1,), (1,)), ((), ()))
    return lax.dot_general(left, right, dims, preferred_element_type=F32)


def call(body, name, out_shape, scratch, in_specs, out_specs, flops, nbytes, limit=16):
    return pl.pallas_call(
        body,
        out_shape=out_shape,
        in_specs=in_specs,
        out_specs=out_specs,
        scratch_shapes=scratch,
        compiler_params=pltpu.CompilerParams(vmem_limit_bytes=limit * 1024 * 1024),
        cost_estimate=pl.CostEstimate(flops=flops, bytes_accessed=nbytes, transcendentals=0),
        name=name,
    )


def shape(dims, dtype):
    return jax.ShapeDtypeStruct(dims, dtype)


def lanes_of(x):
    return lax.broadcasted_iota(jnp.int32, x.shape, 1)


def columns(rows, tap_rows):
    tap_rows[...] = jnp.zeros(tap_rows.shape, F32)
    at = 0
    for row in rows:
        tap_rows[at : at + row.shape[0], :] = row
        at += row.shape[0]
    return tap_rows[...].T


def taps_of(cols, stream):
    return [cols[:, 3 * stream + i : 3 * stream + i + 1] for i in range(3)]


def moved(x):
    src = lax.broadcasted_iota(jnp.int32, (2 * LANES, 2 * LANES), 0)
    dst = lax.broadcasted_iota(jnp.int32, (2 * LANES, 2 * LANES), 1)
    shift = (src - LANES == dst % LANES - 1 - dst // LANES).astype(BF16)
    count = x.shape[0]
    tiles = x.shape[1] // LANES
    wide = jnp.concatenate([x[:, -LANES:], x], axis=1)
    both = dot(
        jnp.concatenate([wide[:, c * LANES : (c + 2) * LANES] for c in range(tiles)], axis=0), shift
    )
    both = [both[c * count : (c + 1) * count] for c in range(tiles)]
    return tuple(
        jnp.concatenate([tile[:, i * LANES : (i + 1) * LANES] for tile in both], axis=1)
        for i in range(2)
    )


def causal(x, taps):
    back1, back2 = moved(x)
    return taps[0] * x.astype(F32) + taps[1] * back1 + taps[2] * back2


def with_edges(x, taps):
    back1, back2 = moved(x)
    sums = taps[0] * x.astype(F32) + taps[1] * back1 + taps[2] * back2
    lane = lax.broadcasted_iota(jnp.int32, (x.shape[0], LANES), 1)
    near = jnp.where(lane < 1, back1[:, :LANES], 0.0)
    far = jnp.where(lane < 2, back2[:, :LANES], 0.0)
    onward = taps[1] * near + taps[2] * far
    return sums, sums[:, :LANES] - onward, onward


def ordered(x):
    size = CHANNELS // CH
    return jnp.concatenate([x[g * size : (g + 1) * size] for g in ORDER], axis=0)


def gate_body(
    q_ref, k_ref, v_ref, taps_ref, skip_ref, out_ref,
    taps_buf, skip_buf, q_buf, k_buf, v_buf, tap_rows, rows, small, sems
):
    def small_copies():
        pairs = [(taps_ref, taps_buf), (skip_ref, skip_buf)]
        pairs += [
            (q_ref.at[:, pl.ds(i * (TOKENS - LANES), LANES)], q_buf.at[i]) for i in range(2)
        ]
        return [pltpu.make_async_copy(a, b, small.at[i]) for i, (a, b) in enumerate(pairs)]

    copies = small_copies() + [
        pltpu.make_async_copy(k_ref, k_buf, sems.at[0]),
        pltpu.make_async_copy(v_ref, v_buf, sems.at[1]),
    ]
    for copy in copies:
        copy.start()
    for copy in copies[:2]:
        copy.wait()
    cols = columns([taps_buf[0], taps_buf[1], taps_buf[2], skip_buf[...]], tap_rows)
    for copy in copies[2:]:
        copy.wait()
    query_taps, key_taps, value_taps = (taps_of(cols, stream) for stream in range(3))
    key, key_own, key_onward = with_edges(k_buf[...], key_taps)
    value, value_own, value_onward = with_edges(v_buf[...], value_taps)
    query = jnp.concatenate([q_buf[0], q_buf[1]], axis=1)
    _, query_own, query_onward = with_edges(query, query_taps)
    gated = key * value
    for c in range(TILES):
        rows[pl.ds(c, CHANNELS, stride=WIDTH), :] = ordered(gated[:, c * LANES : (c + 1) * LANES])
    lane = lanes_of(key_own)
    own = jnp.where(lane < 2, key_own, pltpu.roll(query_own, 2, 1))
    own_value = pltpu.roll(jnp.where(lane < 2, value_own, cols[:, 9:10]), 4, 1)
    onward = key_onward + pltpu.roll(query_onward, 2, 1) + pltpu.roll(value_onward, 4, 1)
    edge = jnp.where(lane < 8, own_value, pltpu.roll(onward, 8, 1))
    rows[pl.ds(TILES, CHANNELS, stride=WIDTH), :] = ordered(jnp.where(lane < 4, own, edge))
    out_ref[...] = rows[...].astype(BF16)


def gate(q, k, v, taps, skip):
    return call(
        gate_body,
        "gate",
        shape((CHANNELS * WIDTH, LANES), BF16),
        [
            pltpu.VMEM((3, 3, CHANNELS), F32),
            pltpu.VMEM((1, CHANNELS), F32),
            pltpu.VMEM((2, CHANNELS, LANES), BF16),
            pltpu.VMEM((CHANNELS, TOKENS), BF16),
            pltpu.VMEM((CHANNELS, TOKENS), BF16),
            pltpu.VMEM((LANES, CHANNELS), F32),
            pltpu.VMEM((CHANNELS * WIDTH, LANES), F32),
            pltpu.SemaphoreType.DMA((4,)),
            pltpu.SemaphoreType.DMA((2,)),
        ],
        [HBM] * 5,
        VMEM,
        10**7,
        2 * 1024 * 1024,
        GATE_LIMIT,
    )(q, k, v, taps, skip)


def sums_and_differences(outer_ref, c):
    near, far = outer_ref[c], outer_ref[c + HALF]
    return jnp.concatenate(
        [jnp.concatenate([near, far], axis=1), jnp.concatenate([near, -far], axis=1)], axis=0
    )


def complex_table(inner_ref, kc):
    real = inner_ref[kc]
    imag = jnp.concatenate([-real[:, LANES:], real[:, :LANES]], axis=1)
    return jnp.concatenate([real, imag], axis=0)


def four_points(re, im):
    sum_re = [re[i] + re[i + 2] for i in range(2)]
    sum_im = [im[i] + im[i + 2] for i in range(2)]
    dif_re = [re[i] - re[i + 2] for i in range(2)]
    dif_im = [im[i] - im[i + 2] for i in range(2)]
    out_re = [sum_re[0] + sum_re[1], dif_re[0] + dif_im[1], sum_re[0] - sum_re[1], dif_re[0] - dif_im[1]]
    out_im = [sum_im[0] + sum_im[1], dif_im[0] - dif_re[1], sum_im[0] - sum_im[1], dif_im[0] + dif_re[1]]
    return out_re, out_im


def eighths(re, im):
    half = math.sqrt(0.5)
    out_re = [re[0], (re[1] + im[1]) * half, im[2], (im[3] - re[3]) * half]
    out_im = [im[0], (im[1] - re[1]) * half, -re[2], (re[3] + im[3]) * -half]
    return out_re, out_im


def forward(signals, outer_ref, turn_ref, section, turned):
    for c in range(HALF):
        section[c] = dot(
            sums_and_differences(outer_ref, c),
            jnp.concatenate([signals[c], signals[c + HALF]], axis=0),
        )
    for row in range(0, BLOCKS, 16):
        turn_re, turn_im = turn_ref[0, row : row + 16, :], turn_ref[1, row : row + 16, :]
        for j in range(2):
            half = slice(j * LANES, (j + 1) * LANES)
            parts = [
                [section[c, m * BLOCKS + row : m * BLOCKS + row + 16, half] for c in range(HALF)]
                for m in range(4)
            ]
            even = four_points(parts[0], parts[1])
            odd = four_points(*eighths(parts[2], parts[3]))
            at = slice(j * BLOCKS + row, j * BLOCKS + row + 16)
            for kc in range(TILES):
                re, im = (part[kc // 2] for part in (odd if kc % 2 else even))
                turned[kc, at, :LANES] = (re * turn_re - im * turn_im).astype(BF16)
                turned[kc, at, LANES:] = (re * turn_im + im * turn_re).astype(BF16)


def filter_body(
    filt_ref, outer_ref, turn_ref, inner_ref, spec_ref,
    spec_buf, rows, section, turned, spec_sems
):
    rows[...] = filt_ref[...].astype(F32)
    signals = []
    for c in range(TILES):
        halves = []
        for j in range(2):
            parts = [
                rows[pl.ds(2 * (g * TILES + c) + j, SEQ, stride=2 * TILES * CH), :]
                for g in ORDER
            ]
            halves.append(jnp.concatenate(parts, axis=0))
        signals.append(jnp.concatenate(halves, axis=1).astype(BF16))
    forward(signals, outer_ref, turn_ref, section, turned)
    out_copies = []
    for kc in range(TILES):
        spec_buf[kc] = (dot(turned[kc], complex_table(inner_ref, kc)) * (1.0 / LENGTH)).astype(BF16)
        out_copies.append(pltpu.make_async_copy(spec_buf.at[kc], spec_ref.at[kc], spec_sems.at[kc]))
        out_copies[-1].start()
    for copy in out_copies:
        copy.wait()


def filter_spectra(filt, consts):
    names = ("outer", "turn", "inner")
    spec = (TILES, 2 * BLOCKS, 2 * LANES)
    return call(
        filter_body,
        "filter_spectra",
        shape(spec, BF16),
        [
            pltpu.VMEM(spec, BF16),
            pltpu.VMEM((2 * BLOCKS * TILES, LANES), F32),
            pltpu.VMEM((HALF, 4 * BLOCKS, 2 * LANES), F32),
            pltpu.VMEM(spec, BF16),
            pltpu.SemaphoreType.DMA((TILES,)),
        ],
        [VMEM] * 4,
        HBM,
        10**9,
        4 * 1024 * 1024,
        FILTER_LIMIT,
    )(filt, *(consts[name] for name in names))


def direct_body(
    q_ref, k_ref, v_ref, taps_ref, skip_ref, query_ref, direct_ref,
    streams, taps_buf, skip_buf, query_buf, direct_buf, tap_rows, cols_buf, small, in_sems, out_sems
):
    first = [
        pltpu.make_async_copy(taps_ref, taps_buf, small.at[0]),
        pltpu.make_async_copy(skip_ref, skip_buf, small.at[1]),
    ]
    places = [pl.ds(step * DIRECT_ROWS, DIRECT_ROWS) for step in range(DIRECT_STEPS)]
    copies = [
        [
            pltpu.make_async_copy(ref.at[place], streams.at[i, place], in_sems.at[i, step])
            for i, ref in enumerate((q_ref, k_ref, v_ref))
        ]
        for step, place in enumerate(places)
    ]
    for copy in first + [copy for group in copies for copy in group]:
        copy.start()
    for copy in first:
        copy.wait()
    out_copies = []
    cols_buf[...] = columns([taps_buf[0], taps_buf[1], taps_buf[2], skip_buf[...]], tap_rows)
    for step in range(DIRECT_STEPS):
        for copy in copies[step]:
            copy.wait()
        at = slice(step * DIRECT_ROWS, (step + 1) * DIRECT_ROWS)
        cols = cols_buf[at, :]
        query, key, value = (causal(streams[i, at, :], taps_of(cols, i)) for i in range(3))
        query_buf[at, :] = query
        direct_buf[at, :] = cols[:, 9:10] * (key * value).astype(BF16).astype(F32)
        for i, (buf, ref) in enumerate(((query_buf, query_ref), (direct_buf, direct_ref))):
            out_copies.append(
                pltpu.make_async_copy(buf.at[places[step]], ref.at[places[step]], out_sems.at[i, step])
            )
            out_copies[-1].start()
    for copy in out_copies:
        copy.wait()


def direct(q, k, v, taps, skip):
    return call(
        direct_body,
        "direct",
        (shape((CHANNELS, TOKENS), F32), shape((CHANNELS, TOKENS), F32)),
        [
            pltpu.VMEM((3, CHANNELS, TOKENS), BF16),
            pltpu.VMEM((3, 3, CHANNELS), F32),
            pltpu.VMEM((1, CHANNELS), F32),
            pltpu.VMEM((CHANNELS, TOKENS), F32),
            pltpu.VMEM((CHANNELS, TOKENS), F32),
            pltpu.VMEM((LANES, CHANNELS), F32),
            pltpu.VMEM((CHANNELS, LANES), F32),
            pltpu.SemaphoreType.DMA((2,)),
            pltpu.SemaphoreType.DMA((3, DIRECT_STEPS)),
            pltpu.SemaphoreType.DMA((2, DIRECT_STEPS)),
        ],
        [HBM] * 5,
        (HBM,) * 2,
        10**9,
        4 * 1024 * 1024,
        DIRECT_LIMIT,
    )(q, k, v, taps, skip)


def conv_body(
    arrived_ref, spec_ref, outer_ref, turn_ref, inner_ref, out_ref,
    rows, section, turned, product, back, edges
):
    rows[...] = arrived_ref[...].astype(F32)

    def arrived(j, c):
        return rows[pl.ds(j * WIDTH + c, BLOCKS, stride=2 * WIDTH), :]

    signals = []
    for c in range(TILES):
        halves = [arrived(j, c) for j in range(2)]
        if c == 0:
            for j in range(2):
                edge = arrived(j, TILES)
                pieces = [edge[n * SEQ : (n + 1) * SEQ] for n in range(CH)]
                step = lax.broadcasted_iota(jnp.int32, pieces[0].shape, 0)
                last = jnp.where(step == 0, 0.0, pltpu.roll(pieces[PLACE[CH - 1]], 1, 0))
                before = jnp.concatenate(
                    [pieces[PLACE[g - 1]] if g else last for g in ORDER], axis=0
                )
                total = edge + pltpu.roll(before, LANES - 8, 1)
                gated = (total * pltpu.roll(total, LANES - 4, 1)).astype(BF16).astype(F32)
                edges[0, j] = pltpu.roll(total, LANES - 2, 1)
                edges[1, j] = pltpu.roll(total, LANES - 6, 1) * gated
                halves[j] = jnp.where(lanes_of(gated) < 2, gated, halves[j])
        signals.append(jnp.concatenate(halves, axis=1).astype(BF16))
    forward(signals, outer_ref, turn_ref, section, turned)
    for kc in range(TILES):
        table = complex_table(inner_ref, kc)
        spectrum = dot(turned[kc], table)
        re, im = spectrum[:, :LANES], spectrum[:, LANES:]
        spec = spec_ref[kc].astype(F32)
        filt_re, filt_im = spec[:, :LANES], spec[:, LANES:]
        parts = [re * filt_re - im * filt_im, re * filt_im + im * filt_re]
        product[kc] = dot_back(jnp.concatenate(parts, axis=1).astype(BF16), table)
    for row in range(0, BLOCKS, 16):
        turn_re, turn_im = turn_ref[0, row : row + 16, :], turn_ref[1, row : row + 16, :]
        for j in range(2):
            at = slice(j * BLOCKS + row, j * BLOCKS + row + 16)
            re, im = [], []
            for kc in range(TILES):
                part_re, part_im = product[kc, at, :LANES], product[kc, at, LANES:]
                re.append(part_re * turn_re + part_im * turn_im)
                im.append(part_im * turn_re - part_re * turn_im)
            even_im, even_re = four_points(im[0::2], re[0::2])
            odd_im, odd_re = eighths(*four_points(im[1::2], re[1::2]))
            half = slice(j * LANES, (j + 1) * LANES)
            for m, part in enumerate((even_re, even_im, odd_re, odd_im)):
                for c in range(HALF):
                    back[c, m * BLOCKS + row : m * BLOCKS + row + 16, half] = part[c].astype(BF16)
    for c in range(HALF):
        result = lax.dot_general(
            sums_and_differences(outer_ref, c),
            back[c],
            (((0,), (0,)), ((), ())),
            preferred_element_type=F32,
        )
        for tile in (c, c + HALF):
            for j in range(2):
                first = BLOCKS if tile >= HALF else 0
                half = result[first : first + BLOCKS, j * LANES : (j + 1) * LANES]
                if tile == 0:
                    start = edges[0, j] * (half.astype(BF16).astype(F32) + edges[1, j])
                    half = jnp.where(lanes_of(half) < 2, start, half)
                rows[pl.ds(j * TILES + tile, BLOCKS, stride=BODY), :] = half
    out_ref[...] = rows[: BLOCKS * BODY, :].reshape(BLOCKS, BODY, LANES).astype(BF16)


def conv(arrived, spec, consts):
    names = ("outer", "turn", "inner")
    return call(
        conv_body,
        "conv",
        shape((BLOCKS, BODY, LANES), BF16),
        [
            pltpu.VMEM((BLOCKS * 2 * WIDTH, LANES), F32),
            pltpu.VMEM((HALF, 4 * BLOCKS, 2 * LANES), F32),
            pltpu.VMEM((TILES, 2 * BLOCKS, 2 * LANES), BF16),
            pltpu.VMEM((TILES, 2 * BLOCKS, 2 * LANES), F32),
            pltpu.VMEM((HALF, 4 * BLOCKS, 2 * LANES), BF16),
            pltpu.VMEM((2, 2, BLOCKS, LANES), F32),
        ],
        [VMEM] * 5,
        VMEM,
        10**9,
        8 * 1024 * 1024,
        CONV_LIMIT,
    )(arrived, spec, *(consts[name] for name in names))


def final_body(returned_ref, query_ref, direct_ref, out_ref, rows, out_buf, sems):
    copies = []
    for step in range(STEPS):
        at = slice(step * ROWS, (step + 1) * ROWS)
        groups = range(step * ROWS // (2 * SEQ), (step + 1) * ROWS // (2 * SEQ))
        message = jnp.concatenate(
            [returned_ref[PLACE[g] * SEQ : (PLACE[g] + 1) * SEQ] for g in groups], axis=0
        ).astype(F32)
        rows[...] = message.reshape(ROWS * TILES, LANES)
        for c in range(TILES):
            lanes = slice(c * LANES, (c + 1) * LANES)
            long_result = rows[pl.ds(c, ROWS, stride=TILES), :]
            mixed = query_ref[at, lanes] * (long_result + direct_ref[at, lanes])
            if c == 0:
                mixed = jnp.where(lanes_of(mixed) < 2, long_result, mixed)
            out_buf[at, lanes] = mixed.astype(BF16)
        place = pl.ds(step * ROWS, ROWS)
        copies.append(pltpu.make_async_copy(out_buf.at[place], out_ref.at[place], sems.at[step]))
        copies[-1].start()
    for copy in copies:
        copy.wait()


def final(returned, query, direct_term):
    return call(
        final_body,
        "final",
        shape((CHANNELS, TOKENS), BF16),
        [
            pltpu.VMEM((ROWS * TILES, LANES), F32),
            pltpu.VMEM((CHANNELS, TOKENS), BF16),
            pltpu.SemaphoreType.DMA((STEPS,)),
        ],
        [VMEM] * 3,
        HBM,
        10**6,
        2 * 1024 * 1024,
        FINAL_LIMIT,
    )(returned, query, direct_term)


def exchange(messages):
    group = [s * CH + g for g in ORDER for s in range(SEQ)]
    return lax.all_to_all(
        messages, AXES, split_axis=0, concat_axis=0, axis_index_groups=[group], tiled=True
    )


def shards(consts, q, k, v, short_taps, long_filter, skip_gain):
    consts = {name: jnp.asarray(table) for name, table in consts.items()}
    skip = skip_gain[None]
    messages = gate(q, k, v, short_taps, skip).reshape(BLOCKS, WIDTH, 2, LANES)
    messages, q, k, v, long_filter = lax.optimization_barrier((messages, q, k, v, long_filter))
    arrived = exchange(messages).reshape(BLOCKS * 2 * WIDTH, LANES)
    filt = long_filter.reshape(2, BLOCKS * TILES, LANES).swapaxes(0, 1)
    filt = filt.reshape(2 * BLOCKS * TILES, LANES)
    spec = filter_spectra(filt, consts)
    spec, q, k, v = lax.optimization_barrier((spec, q, k, v))
    query, direct_term = direct(q, k, v, short_taps, skip)
    spec, query, direct_term = lax.optimization_barrier((spec, query, direct_term))
    returned = exchange(conv(arrived, spec, consts))
    return final(returned, query, direct_term)


def solution(mesh):
    tokens = P(None, AXES)
    placed = (tokens, tokens, tokens, P(), P("ch", "seq", None, None), P())
    return jax.shard_map(
        functools.partial(shards, tables()),
        mesh=mesh,
        in_specs=placed,
        out_specs=tokens,
        check_vma=False,
    )
```

```python
import functools
import math

import jax
import jax.numpy as jnp
import ml_dtypes
import numpy as np
from jax import lax
from jax.experimental import pallas as pl
from jax.experimental.pallas import tpu as pltpu
from jax.sharding import PartitionSpec as P

F32 = jnp.float32
BF16 = jnp.bfloat16
LANES = 128
TOKENS = 1024
TILES = TOKENS // LANES
HALF = TILES // 2
BLOCKS = 128
LENGTH = BLOCKS * TOKENS
CHANNELS = 256
SEQ = 8
CH = 16
BODY = 2 * TILES
WIDTH = TILES + 1
GATE_LIMIT, FILTER_LIMIT, DIRECT_LIMIT, CONV_LIMIT, FINAL_LIMIT = 60, 60, 60, 16, 16
ROWS = 64
STEPS = CHANNELS // ROWS
DIRECT_ROWS = 128
DIRECT_STEPS = CHANNELS // DIRECT_ROWS
AXES = ("seq", "ch")
ORDER = (9, 1, 13, 5, 11, 3, 15, 7, 8, 0, 12, 4, 10, 2, 14, 6)
PLACE = tuple(ORDER.index(g) for g in range(CH))
VMEM = pl.BlockSpec(memory_space=pltpu.VMEM)
HBM = pl.BlockSpec(memory_space=pltpu.HBM)


def tables():
    step = 2.0 * math.pi
    tile = np.arange(TILES)[:, None, None]
    k1 = np.arange(BLOCKS)[None, :, None]
    block = np.arange(BLOCKS).reshape(SEQ, CH).T[list(ORDER)].reshape(1, 1, BLOCKS)
    phase = ((TILES * block + tile) * (4 * k1 + 1) % (4 * TOKENS)) * (step / (4 * TOKENS))
    outer = np.concatenate([np.cos(phase), -np.sin(phase)], axis=1)
    lane = np.arange(LANES)[None, :]
    phase = lane * (np.arange(BLOCKS)[:, None] + 0.25) * (step / LENGTH)
    turn = np.stack([np.cos(phase), -np.sin(phase)])
    lane = np.arange(LANES)[None, :, None]
    k2 = np.arange(LANES)[None, None, :]
    phase = (lane * (TILES * k2 + tile) % TOKENS) * (step / TOKENS)
    cos, sin = np.cos(phase), np.sin(phase)
    inner = np.concatenate([cos, -sin], axis=2)
    narrow = ml_dtypes.bfloat16
    return dict(
        outer=outer.astype(narrow),
        turn=turn.astype(np.float32),
        inner=inner.astype(narrow),
    )


def dot(left, right):
    return jnp.dot(left, right, preferred_element_type=F32)


def dot_back(left, right):
    dims = (((1,), (1,)), ((), ()))
    return lax.dot_general(left, right, dims, preferred_element_type=F32)


def call(body, name, out_shape, scratch, in_specs, out_specs, flops, nbytes, limit=16):
    return pl.pallas_call(
        body,
        out_shape=out_shape,
        in_specs=in_specs,
        out_specs=out_specs,
        scratch_shapes=scratch,
        compiler_params=pltpu.CompilerParams(vmem_limit_bytes=limit * 1024 * 1024),
        cost_estimate=pl.CostEstimate(flops=flops, bytes_accessed=nbytes, transcendentals=0),
        name=name,
    )


def shape(dims, dtype):
    return jax.ShapeDtypeStruct(dims, dtype)


def lanes_of(x):
    return lax.broadcasted_iota(jnp.int32, x.shape, 1)


def columns(rows, tap_rows):
    tap_rows[...] = jnp.zeros(tap_rows.shape, F32)
    at = 0
    for row in rows:
        tap_rows[at : at + row.shape[0], :] = row
        at += row.shape[0]
    return tap_rows[...].T


def taps_of(cols, stream):
    return [cols[:, 3 * stream + i : 3 * stream + i + 1] for i in range(3)]


def moved(x):
    src = lax.broadcasted_iota(jnp.int32, (2 * LANES, 2 * LANES), 0)
    dst = lax.broadcasted_iota(jnp.int32, (2 * LANES, 2 * LANES), 1)
    shift = (src - LANES == dst % LANES - 1 - dst // LANES).astype(BF16)
    count = x.shape[0]
    tiles = x.shape[1] // LANES
    wide = jnp.concatenate([x[:, -LANES:], x], axis=1)
    both = dot(
        jnp.concatenate([wide[:, c * LANES : (c + 2) * LANES] for c in range(tiles)], axis=0), shift
    )
    both = [both[c * count : (c + 1) * count] for c in range(tiles)]
    return tuple(
        jnp.concatenate([tile[:, i * LANES : (i + 1) * LANES] for tile in both], axis=1)
        for i in range(2)
    )


def causal(x, taps):
    back1, back2 = moved(x)
    return taps[0] * x.astype(F32) + taps[1] * back1 + taps[2] * back2


def with_edges(x, taps):
    back1, back2 = moved(x)
    sums = taps[0] * x.astype(F32) + taps[1] * back1 + taps[2] * back2
    lane = lax.broadcasted_iota(jnp.int32, (x.shape[0], LANES), 1)
    near = jnp.where(lane < 1, back1[:, :LANES], 0.0)
    far = jnp.where(lane < 2, back2[:, :LANES], 0.0)
    onward = taps[1] * near + taps[2] * far
    return sums, sums[:, :LANES] - onward, onward


def ordered(x):
    size = CHANNELS // CH
    return jnp.concatenate([x[g * size : (g + 1) * size] for g in ORDER], axis=0)


def gate_body(
    q_ref, k_ref, v_ref, taps_ref, skip_ref, out_ref,
    taps_buf, skip_buf, q_buf, k_buf, v_buf, tap_rows, rows, small, sems
):
    def small_copies():
        pairs = [(taps_ref, taps_buf), (skip_ref, skip_buf)]
        pairs += [
            (q_ref.at[:, pl.ds(i * (TOKENS - LANES), LANES)], q_buf.at[i]) for i in range(2)
        ]
        return [pltpu.make_async_copy(a, b, small.at[i]) for i, (a, b) in enumerate(pairs)]

    first, last = small_copies()[:2], small_copies()[2:]
    copies = first + [
        pltpu.make_async_copy(k_ref, k_buf, sems.at[0]),
        pltpu.make_async_copy(v_ref, v_buf, sems.at[1]),
    ]
    copies += last
    for copy in copies:
        copy.start()
    for copy in copies[:2]:
        copy.wait()
    cols = columns([taps_buf[0], taps_buf[1], taps_buf[2], skip_buf[...]], tap_rows)
    for copy in copies[2:]:
        copy.wait()
    query_taps, key_taps, value_taps = (taps_of(cols, stream) for stream in range(3))
    key, key_own, key_onward = with_edges(k_buf[...], key_taps)
    value, value_own, value_onward = with_edges(v_buf[...], value_taps)
    query = jnp.concatenate([q_buf[0], q_buf[1]], axis=1)
    _, query_own, query_onward = with_edges(query, query_taps)
    gated = key * value
    for c in range(TILES):
        rows[pl.ds(c, CHANNELS, stride=WIDTH), :] = ordered(gated[:, c * LANES : (c + 1) * LANES])
    lane = lanes_of(key_own)
    own = jnp.where(lane < 2, key_own, pltpu.roll(query_own, 2, 1))
    own_value = pltpu.roll(jnp.where(lane < 2, value_own, cols[:, 9:10]), 4, 1)
    onward = key_onward + pltpu.roll(query_onward, 2, 1) + pltpu.roll(value_onward, 4, 1)
    edge = jnp.where(lane < 8, own_value, pltpu.roll(onward, 8, 1))
    rows[pl.ds(TILES, CHANNELS, stride=WIDTH), :] = ordered(jnp.where(lane < 4, own, edge))
    out_ref[...] = rows[...].astype(BF16)


def gate(q, k, v, taps, skip):
    return call(
        gate_body,
        "gate",
        shape((CHANNELS * WIDTH, LANES), BF16),
        [
            pltpu.VMEM((3, 3, CHANNELS), F32),
            pltpu.VMEM((1, CHANNELS), F32),
            pltpu.VMEM((2, CHANNELS, LANES), BF16),
            pltpu.VMEM((CHANNELS, TOKENS), BF16),
            pltpu.VMEM((CHANNELS, TOKENS), BF16),
            pltpu.VMEM((LANES, CHANNELS), F32),
            pltpu.VMEM((CHANNELS * WIDTH, LANES), F32),
            pltpu.SemaphoreType.DMA((4,)),
            pltpu.SemaphoreType.DMA((2,)),
        ],
        [HBM] * 5,
        VMEM,
        10**7,
        2 * 1024 * 1024,
        GATE_LIMIT,
    )(q, k, v, taps, skip)


def sums_and_differences(outer_ref, c):
    near, far = outer_ref[c], outer_ref[c + HALF]
    return jnp.concatenate(
        [jnp.concatenate([near, far], axis=1), jnp.concatenate([near, -far], axis=1)], axis=0
    )


def complex_table(inner_ref, kc):
    real = inner_ref[kc]
    imag = jnp.concatenate([-real[:, LANES:], real[:, :LANES]], axis=1)
    return jnp.concatenate([real, imag], axis=0)


def four_points(re, im):
    sum_re = [re[i] + re[i + 2] for i in range(2)]
    sum_im = [im[i] + im[i + 2] for i in range(2)]
    dif_re = [re[i] - re[i + 2] for i in range(2)]
    dif_im = [im[i] - im[i + 2] for i in range(2)]
    out_re = [sum_re[0] + sum_re[1], dif_re[0] + dif_im[1], sum_re[0] - sum_re[1], dif_re[0] - dif_im[1]]
    out_im = [sum_im[0] + sum_im[1], dif_im[0] - dif_re[1], sum_im[0] - sum_im[1], dif_im[0] + dif_re[1]]
    return out_re, out_im


def eighths(re, im):
    half = math.sqrt(0.5)
    out_re = [re[0], (re[1] + im[1]) * half, im[2], (im[3] - re[3]) * half]
    out_im = [im[0], (im[1] - re[1]) * half, -re[2], (re[3] + im[3]) * -half]
    return out_re, out_im


def forward(signals, outer_ref, turn_ref, section, turned):
    for c in range(HALF):
        section[c] = dot(
            sums_and_differences(outer_ref, c),
            jnp.concatenate([signals[c], signals[c + HALF]], axis=0),
        )
    for row in range(0, BLOCKS, 16):
        turn_re, turn_im = turn_ref[0, row : row + 16, :], turn_ref[1, row : row + 16, :]
        for j in range(2):
            half = slice(j * LANES, (j + 1) * LANES)
            parts = [
                [section[c, m * BLOCKS + row : m * BLOCKS + row + 16, half] for c in range(HALF)]
                for m in range(4)
            ]
            even = four_points(parts[0], parts[1])
            odd = four_points(*eighths(parts[2], parts[3]))
            at = slice(j * BLOCKS + row, j * BLOCKS + row + 16)
            for kc in range(TILES):
                re, im = (part[kc // 2] for part in (odd if kc % 2 else even))
                turned[kc, at, :LANES] = (re * turn_re - im * turn_im).astype(BF16)
                turned[kc, at, LANES:] = (re * turn_im + im * turn_re).astype(BF16)


def filter_body(
    filt_ref, outer_ref, turn_ref, inner_ref, spec_ref,
    spec_buf, rows, section, turned, spec_sems
):
    rows[...] = filt_ref[...].astype(F32)
    signals = []
    for c in range(TILES):
        halves = []
        for j in range(2):
            parts = [
                rows[pl.ds(2 * (g * TILES + c) + j, SEQ, stride=2 * TILES * CH), :]
                for g in ORDER
            ]
            halves.append(jnp.concatenate(parts, axis=0))
        signals.append(jnp.concatenate(halves, axis=1).astype(BF16))
    forward(signals, outer_ref, turn_ref, section, turned)
    out_copies = []
    for kc in range(TILES):
        spec_buf[kc] = (dot(turned[kc], complex_table(inner_ref, kc)) * (1.0 / LENGTH)).astype(BF16)
        out_copies.append(pltpu.make_async_copy(spec_buf.at[kc], spec_ref.at[kc], spec_sems.at[kc]))
        out_copies[-1].start()
    for copy in out_copies:
        copy.wait()


def filter_spectra(filt, consts):
    names = ("outer", "turn", "inner")
    spec = (TILES, 2 * BLOCKS, 2 * LANES)
    return call(
        filter_body,
        "filter_spectra",
        shape(spec, BF16),
        [
            pltpu.VMEM(spec, BF16),
            pltpu.VMEM((2 * BLOCKS * TILES, LANES), F32),
            pltpu.VMEM((HALF, 4 * BLOCKS, 2 * LANES), F32),
            pltpu.VMEM(spec, BF16),
            pltpu.SemaphoreType.DMA((TILES,)),
        ],
        [VMEM] * 4,
        HBM,
        10**9,
        4 * 1024 * 1024,
        FILTER_LIMIT,
    )(filt, *(consts[name] for name in names))


def direct_body(
    q_ref, k_ref, v_ref, taps_ref, skip_ref, query_ref, direct_ref,
    streams, taps_buf, skip_buf, query_buf, direct_buf, tap_rows, cols_buf, small, in_sems, out_sems
):
    first = [
        pltpu.make_async_copy(taps_ref, taps_buf, small.at[0]),
        pltpu.make_async_copy(skip_ref, skip_buf, small.at[1]),
    ]
    places = [pl.ds(step * DIRECT_ROWS, DIRECT_ROWS) for step in range(DIRECT_STEPS)]
    copies = [
        [
            pltpu.make_async_copy(ref.at[place], streams.at[i, place], in_sems.at[i, step])
            for i, ref in enumerate((q_ref, k_ref, v_ref))
        ]
        for step, place in enumerate(places)
    ]
    for copy in first + [copy for group in copies for copy in group]:
        copy.start()
    for copy in first:
        copy.wait()
    out_copies = []
    cols_buf[...] = columns([taps_buf[0], taps_buf[1], taps_buf[2], skip_buf[...]], tap_rows)
    for step in range(DIRECT_STEPS):
        for copy in copies[step]:
            copy.wait()
        at = slice(step * DIRECT_ROWS, (step + 1) * DIRECT_ROWS)
        cols = cols_buf[at, :]
        query, key, value = (causal(streams[i, at, :], taps_of(cols, i)) for i in range(3))
        query_buf[at, :] = query
        direct_buf[at, :] = cols[:, 9:10] * (key * value).astype(BF16).astype(F32)
        for i, (buf, ref) in enumerate(((query_buf, query_ref), (direct_buf, direct_ref))):
            out_copies.append(
                pltpu.make_async_copy(buf.at[places[step]], ref.at[places[step]], out_sems.at[i, step])
            )
            out_copies[-1].start()
    for copy in out_copies:
        copy.wait()


def direct(q, k, v, taps, skip):
    return call(
        direct_body,
        "direct",
        (shape((CHANNELS, TOKENS), F32), shape((CHANNELS, TOKENS), F32)),
        [
            pltpu.VMEM((3, CHANNELS, TOKENS), BF16),
            pltpu.VMEM((3, 3, CHANNELS), F32),
            pltpu.VMEM((1, CHANNELS), F32),
            pltpu.VMEM((CHANNELS, TOKENS), F32),
            pltpu.VMEM((CHANNELS, TOKENS), F32),
            pltpu.VMEM((LANES, CHANNELS), F32),
            pltpu.VMEM((CHANNELS, LANES), F32),
            pltpu.SemaphoreType.DMA((2,)),
            pltpu.SemaphoreType.DMA((3, DIRECT_STEPS)),
            pltpu.SemaphoreType.DMA((2, DIRECT_STEPS)),
        ],
        [HBM] * 5,
        (HBM,) * 2,
        10**9,
        4 * 1024 * 1024,
        DIRECT_LIMIT,
    )(q, k, v, taps, skip)


def conv_body(
    arrived_ref, spec_ref, outer_ref, turn_ref, inner_ref, out_ref,
    rows, section, turned, product, back, edges
):
    rows[...] = arrived_ref[...].astype(F32)

    def arrived(j, c):
        return rows[pl.ds(j * WIDTH + c, BLOCKS, stride=2 * WIDTH), :]

    signals = []
    for c in range(TILES):
        halves = [arrived(j, c) for j in range(2)]
        if c == 0:
            for j in range(2):
                edge = arrived(j, TILES)
                pieces = [edge[n * SEQ : (n + 1) * SEQ] for n in range(CH)]
                step = lax.broadcasted_iota(jnp.int32, pieces[0].shape, 0)
                last = jnp.where(step == 0, 0.0, pltpu.roll(pieces[PLACE[CH - 1]], 1, 0))
                before = jnp.concatenate(
                    [pieces[PLACE[g - 1]] if g else last for g in ORDER], axis=0
                )
                total = edge + pltpu.roll(before, LANES - 8, 1)
                gated = (total * pltpu.roll(total, LANES - 4, 1)).astype(BF16).astype(F32)
                edges[0, j] = pltpu.roll(total, LANES - 2, 1)
                edges[1, j] = pltpu.roll(total, LANES - 6, 1) * gated
                halves[j] = jnp.where(lanes_of(gated) < 2, gated, halves[j])
        signals.append(jnp.concatenate(halves, axis=1).astype(BF16))
    forward(signals, outer_ref, turn_ref, section, turned)
    for kc in range(TILES):
        table = complex_table(inner_ref, kc)
        spectrum = dot(turned[kc], table)
        re, im = spectrum[:, :LANES], spectrum[:, LANES:]
        spec = spec_ref[kc].astype(F32)
        filt_re, filt_im = spec[:, :LANES], spec[:, LANES:]
        parts = [re * filt_re - im * filt_im, re * filt_im + im * filt_re]
        product[kc] = dot_back(jnp.concatenate(parts, axis=1).astype(BF16), table)
    for row in range(0, BLOCKS, 16):
        turn_re, turn_im = turn_ref[0, row : row + 16, :], turn_ref[1, row : row + 16, :]
        for j in range(2):
            at = slice(j * BLOCKS + row, j * BLOCKS + row + 16)
            re, im = [], []
            for kc in range(TILES):
                part_re, part_im = product[kc, at, :LANES], product[kc, at, LANES:]
                re.append(part_re * turn_re + part_im * turn_im)
                im.append(part_im * turn_re - part_re * turn_im)
            even_im, even_re = four_points(im[0::2], re[0::2])
            odd_im, odd_re = eighths(*four_points(im[1::2], re[1::2]))
            half = slice(j * LANES, (j + 1) * LANES)
            for m, part in enumerate((even_re, even_im, odd_re, odd_im)):
                for c in range(HALF):
                    back[c, m * BLOCKS + row : m * BLOCKS + row + 16, half] = part[c].astype(BF16)
    for c in range(HALF):
        result = lax.dot_general(
            sums_and_differences(outer_ref, c),
            back[c],
            (((0,), (0,)), ((), ())),
            preferred_element_type=F32,
        )
        for tile in (c, c + HALF):
            for j in range(2):
                first = BLOCKS if tile >= HALF else 0
                half = result[first : first + BLOCKS, j * LANES : (j + 1) * LANES]
                if tile == 0:
                    start = edges[0, j] * (half.astype(BF16).astype(F32) + edges[1, j])
                    half = jnp.where(lanes_of(half) < 2, start, half)
                rows[pl.ds(j * TILES + tile, BLOCKS, stride=BODY), :] = half
    out_ref[...] = rows[: BLOCKS * BODY, :].reshape(BLOCKS, BODY, LANES).astype(BF16)


def conv(arrived, spec, consts):
    names = ("outer", "turn", "inner")
    return call(
        conv_body,
        "conv",
        shape((BLOCKS, BODY, LANES), BF16),
        [
            pltpu.VMEM((BLOCKS * 2 * WIDTH, LANES), F32),
            pltpu.VMEM((HALF, 4 * BLOCKS, 2 * LANES), F32),
            pltpu.VMEM((TILES, 2 * BLOCKS, 2 * LANES), BF16),
            pltpu.VMEM((TILES, 2 * BLOCKS, 2 * LANES), F32),
            pltpu.VMEM((HALF, 4 * BLOCKS, 2 * LANES), BF16),
            pltpu.VMEM((2, 2, BLOCKS, LANES), F32),
        ],
        [VMEM] * 5,
        VMEM,
        10**9,
        8 * 1024 * 1024,
        CONV_LIMIT,
    )(arrived, spec, *(consts[name] for name in names))


def final_body(returned_ref, query_ref, direct_ref, out_ref, rows, out_buf, sems):
    copies = []
    for step in range(STEPS):
        at = slice(step * ROWS, (step + 1) * ROWS)
        groups = range(step * ROWS // (2 * SEQ), (step + 1) * ROWS // (2 * SEQ))
        message = jnp.concatenate(
            [returned_ref[PLACE[g] * SEQ : (PLACE[g] + 1) * SEQ] for g in groups], axis=0
        ).astype(F32)
        rows[...] = message.reshape(ROWS * TILES, LANES)
        for c in range(TILES):
            lanes = slice(c * LANES, (c + 1) * LANES)
            long_result = rows[pl.ds(c, ROWS, stride=TILES), :]
            mixed = query_ref[at, lanes] * (long_result + direct_ref[at, lanes])
            if c == 0:
                mixed = jnp.where(lanes_of(mixed) < 2, long_result, mixed)
            out_buf[at, lanes] = mixed.astype(BF16)
        place = pl.ds(step * ROWS, ROWS)
        copies.append(pltpu.make_async_copy(out_buf.at[place], out_ref.at[place], sems.at[step]))
        copies[-1].start()
    for copy in copies:
        copy.wait()


def final(returned, query, direct_term):
    return call(
        final_body,
        "final",
        shape((CHANNELS, TOKENS), BF16),
        [
            pltpu.VMEM((ROWS * TILES, LANES), F32),
            pltpu.VMEM((CHANNELS, TOKENS), BF16),
            pltpu.SemaphoreType.DMA((STEPS,)),
        ],
        [VMEM] * 3,
        HBM,
        10**6,
        2 * 1024 * 1024,
        FINAL_LIMIT,
    )(returned, query, direct_term)


def exchange(messages):
    group = [s * CH + g for g in ORDER for s in range(SEQ)]
    return lax.all_to_all(
        messages, AXES, split_axis=0, concat_axis=0, axis_index_groups=[group], tiled=True
    )


def shards(consts, q, k, v, short_taps, long_filter, skip_gain):
    consts = {name: jnp.asarray(table) for name, table in consts.items()}
    skip = skip_gain[None]
    messages = gate(q, k, v, short_taps, skip).reshape(BLOCKS, WIDTH, 2, LANES)
    messages, q, k, v, long_filter = lax.optimization_barrier((messages, q, k, v, long_filter))
    arrived = exchange(messages).reshape(BLOCKS * 2 * WIDTH, LANES)
    filt = long_filter.reshape(2, BLOCKS * TILES, LANES).swapaxes(0, 1)
    filt = filt.reshape(2 * BLOCKS * TILES, LANES)
    spec = filter_spectra(filt, consts)
    spec, q, k, v = lax.optimization_barrier((spec, q, k, v))
    query, direct_term = direct(q, k, v, short_taps, skip)
    spec, query, direct_term = lax.optimization_barrier((spec, query, direct_term))
    returned = exchange(conv(arrived, spec, consts))
    return final(returned, query, direct_term)


def solution(mesh):
    tokens = P(None, AXES)
    placed = (tokens, tokens, tokens, P(), P("ch", "seq", None, None), P())
    return jax.shard_map(
        functools.partial(shards, tables()),
        mesh=mesh,
        in_specs=placed,
        out_specs=tokens,
        check_vma=False,
    )
```

```python
import functools
import math

import jax
import jax.numpy as jnp
import ml_dtypes
import numpy as np
from jax import lax
from jax.experimental import pallas as pl
from jax.experimental.pallas import tpu as pltpu
from jax.sharding import PartitionSpec as P

F32 = jnp.float32
BF16 = jnp.bfloat16
LANES = 128
TOKENS = 1024
TILES = TOKENS // LANES
HALF = TILES // 2
BLOCKS = 128
LENGTH = BLOCKS * TOKENS
CHANNELS = 256
SEQ = 8
CH = 16
BODY = 2 * TILES
WIDTH = TILES + 1
GATE_LIMIT, FILTER_LIMIT, DIRECT_LIMIT, CONV_LIMIT, FINAL_LIMIT = 60, 60, 60, 16, 16
ROWS = 64
STEPS = CHANNELS // ROWS
DIRECT_ROWS = 128
DIRECT_STEPS = CHANNELS // DIRECT_ROWS
AXES = ("seq", "ch")
ORDER = (9, 1, 13, 5, 11, 3, 15, 7, 8, 0, 12, 4, 10, 2, 14, 6)
PLACE = tuple(ORDER.index(g) for g in range(CH))
VMEM = pl.BlockSpec(memory_space=pltpu.VMEM)
HBM = pl.BlockSpec(memory_space=pltpu.HBM)


def tables():
    step = 2.0 * math.pi
    tile = np.arange(TILES)[:, None, None]
    k1 = np.arange(BLOCKS)[None, :, None]
    block = np.arange(BLOCKS).reshape(SEQ, CH).T[list(ORDER)].reshape(1, 1, BLOCKS)
    phase = ((TILES * block + tile) * (4 * k1 + 1) % (4 * TOKENS)) * (step / (4 * TOKENS))
    outer = np.concatenate([np.cos(phase), -np.sin(phase)], axis=1)
    lane = np.arange(LANES)[None, :]
    phase = lane * (np.arange(BLOCKS)[:, None] + 0.25) * (step / LENGTH)
    turn = np.stack([np.cos(phase), -np.sin(phase)])
    lane = np.arange(LANES)[None, :, None]
    k2 = np.arange(LANES)[None, None, :]
    phase = (lane * (TILES * k2 + tile) % TOKENS) * (step / TOKENS)
    cos, sin = np.cos(phase), np.sin(phase)
    inner = np.concatenate([cos, -sin], axis=2)
    narrow = ml_dtypes.bfloat16
    return dict(
        outer=outer.astype(narrow),
        turn=turn.astype(np.float32),
        inner=inner.astype(narrow),
    )


def dot(left, right):
    return jnp.dot(left, right, preferred_element_type=F32)


def dot_back(left, right):
    dims = (((1,), (1,)), ((), ()))
    return lax.dot_general(left, right, dims, preferred_element_type=F32)


def call(body, name, out_shape, scratch, in_specs, out_specs, flops, nbytes, limit=16):
    return pl.pallas_call(
        body,
        out_shape=out_shape,
        in_specs=in_specs,
        out_specs=out_specs,
        scratch_shapes=scratch,
        compiler_params=pltpu.CompilerParams(vmem_limit_bytes=limit * 1024 * 1024),
        cost_estimate=pl.CostEstimate(flops=flops, bytes_accessed=nbytes, transcendentals=0),
        name=name,
    )


def shape(dims, dtype):
    return jax.ShapeDtypeStruct(dims, dtype)


def lanes_of(x):
    return lax.broadcasted_iota(jnp.int32, x.shape, 1)


def columns(rows, tap_rows):
    tap_rows[...] = jnp.zeros(tap_rows.shape, F32)
    at = 0
    for row in rows:
        tap_rows[at : at + row.shape[0], :] = row
        at += row.shape[0]
    return tap_rows[...].T


def taps_of(cols, stream):
    return [cols[:, 3 * stream + i : 3 * stream + i + 1] for i in range(3)]


def moved(x):
    src = lax.broadcasted_iota(jnp.int32, (2 * LANES, 2 * LANES), 0)
    dst = lax.broadcasted_iota(jnp.int32, (2 * LANES, 2 * LANES), 1)
    shift = (src - LANES == dst % LANES - 1 - dst // LANES).astype(BF16)
    count = x.shape[0]
    tiles = x.shape[1] // LANES
    wide = jnp.concatenate([x[:, -LANES:], x], axis=1)
    both = dot(
        jnp.concatenate([wide[:, c * LANES : (c + 2) * LANES] for c in range(tiles)], axis=0), shift
    )
    both = [both[c * count : (c + 1) * count] for c in range(tiles)]
    return tuple(
        jnp.concatenate([tile[:, i * LANES : (i + 1) * LANES] for tile in both], axis=1)
        for i in range(2)
    )


def causal(x, taps):
    back1, back2 = moved(x)
    return taps[0] * x.astype(F32) + taps[1] * back1 + taps[2] * back2


def with_edges(x, taps):
    back1, back2 = moved(x)
    sums = taps[0] * x.astype(F32) + taps[1] * back1 + taps[2] * back2
    lane = lax.broadcasted_iota(jnp.int32, (x.shape[0], LANES), 1)
    near = jnp.where(lane < 1, back1[:, :LANES], 0.0)
    far = jnp.where(lane < 2, back2[:, :LANES], 0.0)
    onward = taps[1] * near + taps[2] * far
    return sums, sums[:, :LANES] - onward, onward


def ordered(x):
    size = CHANNELS // CH
    return jnp.concatenate([x[g * size : (g + 1) * size] for g in ORDER], axis=0)


def gate_body(
    q_ref, k_ref, v_ref, taps_ref, skip_ref, out_ref,
    taps_buf, skip_buf, q_buf, k_buf, v_buf, tap_rows, rows, small, sems
):
    def small_copies():
        pairs = [(taps_ref, taps_buf), (skip_ref, skip_buf)]
        pairs += [
            (q_ref.at[:, pl.ds(i * (TOKENS - LANES), LANES)], q_buf.at[i]) for i in range(2)
        ]
        return [pltpu.make_async_copy(a, b, small.at[i]) for i, (a, b) in enumerate(pairs)]

    first, last = small_copies()[:2], small_copies()[2:]
    copies = first + [
        pltpu.make_async_copy(ref.at[pl.ds(p * 128, 128)], buf.at[pl.ds(p * 128, 128)], sems.at[i, p])
        for i, (ref, buf) in enumerate(((k_ref, k_buf), (v_ref, v_buf)))
        for p in range(2)
    ]
    copies += last
    for copy in copies:
        copy.start()
    for copy in copies[:2]:
        copy.wait()
    cols = columns([taps_buf[0], taps_buf[1], taps_buf[2], skip_buf[...]], tap_rows)
    for copy in copies[2:]:
        copy.wait()
    query_taps, key_taps, value_taps = (taps_of(cols, stream) for stream in range(3))
    key, key_own, key_onward = with_edges(k_buf[...], key_taps)
    value, value_own, value_onward = with_edges(v_buf[...], value_taps)
    query = jnp.concatenate([q_buf[0], q_buf[1]], axis=1)
    _, query_own, query_onward = with_edges(query, query_taps)
    gated = key * value
    for c in range(TILES):
        rows[pl.ds(c, CHANNELS, stride=WIDTH), :] = ordered(gated[:, c * LANES : (c + 1) * LANES])
    lane = lanes_of(key_own)
    own = jnp.where(lane < 2, key_own, pltpu.roll(query_own, 2, 1))
    own_value = pltpu.roll(jnp.where(lane < 2, value_own, cols[:, 9:10]), 4, 1)
    onward = key_onward + pltpu.roll(query_onward, 2, 1) + pltpu.roll(value_onward, 4, 1)
    edge = jnp.where(lane < 8, own_value, pltpu.roll(onward, 8, 1))
    rows[pl.ds(TILES, CHANNELS, stride=WIDTH), :] = ordered(jnp.where(lane < 4, own, edge))
    out_ref[...] = rows[...].astype(BF16)


def gate(q, k, v, taps, skip):
    return call(
        gate_body,
        "gate",
        shape((CHANNELS * WIDTH, LANES), BF16),
        [
            pltpu.VMEM((3, 3, CHANNELS), F32),
            pltpu.VMEM((1, CHANNELS), F32),
            pltpu.VMEM((2, CHANNELS, LANES), BF16),
            pltpu.VMEM((CHANNELS, TOKENS), BF16),
            pltpu.VMEM((CHANNELS, TOKENS), BF16),
            pltpu.VMEM((LANES, CHANNELS), F32),
            pltpu.VMEM((CHANNELS * WIDTH, LANES), F32),
            pltpu.SemaphoreType.DMA((4,)),
            pltpu.SemaphoreType.DMA((2, 2)),
        ],
        [HBM] * 5,
        VMEM,
        10**7,
        2 * 1024 * 1024,
        GATE_LIMIT,
    )(q, k, v, taps, skip)


def sums_and_differences(outer_ref, c):
    near, far = outer_ref[c], outer_ref[c + HALF]
    return jnp.concatenate(
        [jnp.concatenate([near, far], axis=1), jnp.concatenate([near, -far], axis=1)], axis=0
    )


def complex_table(inner_ref, kc):
    real = inner_ref[kc]
    imag = jnp.concatenate([-real[:, LANES:], real[:, :LANES]], axis=1)
    return jnp.concatenate([real, imag], axis=0)


def four_points(re, im):
    sum_re = [re[i] + re[i + 2] for i in range(2)]
    sum_im = [im[i] + im[i + 2] for i in range(2)]
    dif_re = [re[i] - re[i + 2] for i in range(2)]
    dif_im = [im[i] - im[i + 2] for i in range(2)]
    out_re = [sum_re[0] + sum_re[1], dif_re[0] + dif_im[1], sum_re[0] - sum_re[1], dif_re[0] - dif_im[1]]
    out_im = [sum_im[0] + sum_im[1], dif_im[0] - dif_re[1], sum_im[0] - sum_im[1], dif_im[0] + dif_re[1]]
    return out_re, out_im


def eighths(re, im):
    half = math.sqrt(0.5)
    out_re = [re[0], (re[1] + im[1]) * half, im[2], (im[3] - re[3]) * half]
    out_im = [im[0], (im[1] - re[1]) * half, -re[2], (re[3] + im[3]) * -half]
    return out_re, out_im


def forward(signals, outer_ref, turn_ref, section, turned):
    for c in range(HALF):
        section[c] = dot(
            sums_and_differences(outer_ref, c),
            jnp.concatenate([signals[c], signals[c + HALF]], axis=0),
        )
    for row in range(0, BLOCKS, 16):
        turn_re, turn_im = turn_ref[0, row : row + 16, :], turn_ref[1, row : row + 16, :]
        for j in range(2):
            half = slice(j * LANES, (j + 1) * LANES)
            parts = [
                [section[c, m * BLOCKS + row : m * BLOCKS + row + 16, half] for c in range(HALF)]
                for m in range(4)
            ]
            even = four_points(parts[0], parts[1])
            odd = four_points(*eighths(parts[2], parts[3]))
            at = slice(j * BLOCKS + row, j * BLOCKS + row + 16)
            for kc in range(TILES):
                re, im = (part[kc // 2] for part in (odd if kc % 2 else even))
                turned[kc, at, :LANES] = (re * turn_re - im * turn_im).astype(BF16)
                turned[kc, at, LANES:] = (re * turn_im + im * turn_re).astype(BF16)


def filter_body(
    filt_ref, outer_ref, turn_ref, inner_ref, spec_ref,
    spec_buf, rows, section, turned, spec_sems
):
    rows[...] = filt_ref[...].astype(F32)
    signals = []
    for c in range(TILES):
        halves = []
        for j in range(2):
            parts = [
                rows[pl.ds(2 * (g * TILES + c) + j, SEQ, stride=2 * TILES * CH), :]
                for g in ORDER
            ]
            halves.append(jnp.concatenate(parts, axis=0))
        signals.append(jnp.concatenate(halves, axis=1).astype(BF16))
    forward(signals, outer_ref, turn_ref, section, turned)
    out_copies = []
    for kc in range(TILES):
        spec_buf[kc] = (dot(turned[kc], complex_table(inner_ref, kc)) * (1.0 / LENGTH)).astype(BF16)
        out_copies.append(pltpu.make_async_copy(spec_buf.at[kc], spec_ref.at[kc], spec_sems.at[kc]))
        out_copies[-1].start()
    for copy in out_copies:
        copy.wait()


def filter_spectra(filt, consts):
    names = ("outer", "turn", "inner")
    spec = (TILES, 2 * BLOCKS, 2 * LANES)
    return call(
        filter_body,
        "filter_spectra",
        shape(spec, BF16),
        [
            pltpu.VMEM(spec, BF16),
            pltpu.VMEM((2 * BLOCKS * TILES, LANES), F32),
            pltpu.VMEM((HALF, 4 * BLOCKS, 2 * LANES), F32),
            pltpu.VMEM(spec, BF16),
            pltpu.SemaphoreType.DMA((TILES,)),
        ],
        [VMEM] * 4,
        HBM,
        10**9,
        4 * 1024 * 1024,
        FILTER_LIMIT,
    )(filt, *(consts[name] for name in names))


def direct_body(
    q_ref, k_ref, v_ref, taps_ref, skip_ref, query_ref, direct_ref,
    streams, taps_buf, skip_buf, query_buf, direct_buf, tap_rows, cols_buf, small, in_sems, out_sems
):
    first = [
        pltpu.make_async_copy(taps_ref, taps_buf, small.at[0]),
        pltpu.make_async_copy(skip_ref, skip_buf, small.at[1]),
    ]
    places = [pl.ds(step * DIRECT_ROWS, DIRECT_ROWS) for step in range(DIRECT_STEPS)]
    copies = [
        [
            pltpu.make_async_copy(ref.at[place], streams.at[i, place], in_sems.at[i, step])
            for i, ref in enumerate((q_ref, k_ref, v_ref))
        ]
        for step, place in enumerate(places)
    ]
    for copy in first + [copy for group in copies for copy in group]:
        copy.start()
    for copy in first:
        copy.wait()
    out_copies = []
    cols_buf[...] = columns([taps_buf[0], taps_buf[1], taps_buf[2], skip_buf[...]], tap_rows)
    for step in range(DIRECT_STEPS):
        for copy in copies[step]:
            copy.wait()
        at = slice(step * DIRECT_ROWS, (step + 1) * DIRECT_ROWS)
        cols = cols_buf[at, :]
        query, key, value = (causal(streams[i, at, :], taps_of(cols, i)) for i in range(3))
        query_buf[at, :] = query
        direct_buf[at, :] = cols[:, 9:10] * (key * value).astype(BF16).astype(F32)
        for i, (buf, ref) in enumerate(((query_buf, query_ref), (direct_buf, direct_ref))):
            out_copies.append(
                pltpu.make_async_copy(buf.at[places[step]], ref.at[places[step]], out_sems.at[i, step])
            )
            out_copies[-1].start()
    for copy in out_copies:
        copy.wait()


def direct(q, k, v, taps, skip):
    return call(
        direct_body,
        "direct",
        (shape((CHANNELS, TOKENS), F32), shape((CHANNELS, TOKENS), F32)),
        [
            pltpu.VMEM((3, CHANNELS, TOKENS), BF16),
            pltpu.VMEM((3, 3, CHANNELS), F32),
            pltpu.VMEM((1, CHANNELS), F32),
            pltpu.VMEM((CHANNELS, TOKENS), F32),
            pltpu.VMEM((CHANNELS, TOKENS), F32),
            pltpu.VMEM((LANES, CHANNELS), F32),
            pltpu.VMEM((CHANNELS, LANES), F32),
            pltpu.SemaphoreType.DMA((2,)),
            pltpu.SemaphoreType.DMA((3, DIRECT_STEPS)),
            pltpu.SemaphoreType.DMA((2, DIRECT_STEPS)),
        ],
        [HBM] * 5,
        (HBM,) * 2,
        10**9,
        4 * 1024 * 1024,
        DIRECT_LIMIT,
    )(q, k, v, taps, skip)


def conv_body(
    arrived_ref, spec_ref, outer_ref, turn_ref, inner_ref, out_ref,
    rows, section, turned, product, back, edges
):
    rows[...] = arrived_ref[...].astype(F32)

    def arrived(j, c):
        return rows[pl.ds(j * WIDTH + c, BLOCKS, stride=2 * WIDTH), :]

    signals = []
    for c in range(TILES):
        halves = [arrived(j, c) for j in range(2)]
        if c == 0:
            for j in range(2):
                edge = arrived(j, TILES)
                pieces = [edge[n * SEQ : (n + 1) * SEQ] for n in range(CH)]
                step = lax.broadcasted_iota(jnp.int32, pieces[0].shape, 0)
                last = jnp.where(step == 0, 0.0, pltpu.roll(pieces[PLACE[CH - 1]], 1, 0))
                before = jnp.concatenate(
                    [pieces[PLACE[g - 1]] if g else last for g in ORDER], axis=0
                )
                total = edge + pltpu.roll(before, LANES - 8, 1)
                gated = (total * pltpu.roll(total, LANES - 4, 1)).astype(BF16).astype(F32)
                edges[0, j] = pltpu.roll(total, LANES - 2, 1)
                edges[1, j] = pltpu.roll(total, LANES - 6, 1) * gated
                halves[j] = jnp.where(lanes_of(gated) < 2, gated, halves[j])
        signals.append(jnp.concatenate(halves, axis=1).astype(BF16))
    forward(signals, outer_ref, turn_ref, section, turned)
    for kc in range(TILES):
        table = complex_table(inner_ref, kc)
        spectrum = dot(turned[kc], table)
        re, im = spectrum[:, :LANES], spectrum[:, LANES:]
        spec = spec_ref[kc].astype(F32)
        filt_re, filt_im = spec[:, :LANES], spec[:, LANES:]
        parts = [re * filt_re - im * filt_im, re * filt_im + im * filt_re]
        product[kc] = dot_back(jnp.concatenate(parts, axis=1).astype(BF16), table)
    for row in range(0, BLOCKS, 16):
        turn_re, turn_im = turn_ref[0, row : row + 16, :], turn_ref[1, row : row + 16, :]
        for j in range(2):
            at = slice(j * BLOCKS + row, j * BLOCKS + row + 16)
            re, im = [], []
            for kc in range(TILES):
                part_re, part_im = product[kc, at, :LANES], product[kc, at, LANES:]
                re.append(part_re * turn_re + part_im * turn_im)
                im.append(part_im * turn_re - part_re * turn_im)
            even_im, even_re = four_points(im[0::2], re[0::2])
            odd_im, odd_re = eighths(*four_points(im[1::2], re[1::2]))
            half = slice(j * LANES, (j + 1) * LANES)
            for m, part in enumerate((even_re, even_im, odd_re, odd_im)):
                for c in range(HALF):
                    back[c, m * BLOCKS + row : m * BLOCKS + row + 16, half] = part[c].astype(BF16)
    for c in range(HALF):
        result = lax.dot_general(
            sums_and_differences(outer_ref, c),
            back[c],
            (((0,), (0,)), ((), ())),
            preferred_element_type=F32,
        )
        for tile in (c, c + HALF):
            for j in range(2):
                first = BLOCKS if tile >= HALF else 0
                half = result[first : first + BLOCKS, j * LANES : (j + 1) * LANES]
                if tile == 0:
                    start = edges[0, j] * (half.astype(BF16).astype(F32) + edges[1, j])
                    half = jnp.where(lanes_of(half) < 2, start, half)
                rows[pl.ds(j * TILES + tile, BLOCKS, stride=BODY), :] = half
    out_ref[...] = rows[: BLOCKS * BODY, :].reshape(BLOCKS, BODY, LANES).astype(BF16)


def conv(arrived, spec, consts):
    names = ("outer", "turn", "inner")
    return call(
        conv_body,
        "conv",
        shape((BLOCKS, BODY, LANES), BF16),
        [
            pltpu.VMEM((BLOCKS * 2 * WIDTH, LANES), F32),
            pltpu.VMEM((HALF, 4 * BLOCKS, 2 * LANES), F32),
            pltpu.VMEM((TILES, 2 * BLOCKS, 2 * LANES), BF16),
            pltpu.VMEM((TILES, 2 * BLOCKS, 2 * LANES), F32),
            pltpu.VMEM((HALF, 4 * BLOCKS, 2 * LANES), BF16),
            pltpu.VMEM((2, 2, BLOCKS, LANES), F32),
        ],
        [VMEM] * 5,
        VMEM,
        10**9,
        8 * 1024 * 1024,
        CONV_LIMIT,
    )(arrived, spec, *(consts[name] for name in names))


def final_body(returned_ref, query_ref, direct_ref, out_ref, rows, out_buf, sems):
    copies = []
    for step in range(STEPS):
        at = slice(step * ROWS, (step + 1) * ROWS)
        groups = range(step * ROWS // (2 * SEQ), (step + 1) * ROWS // (2 * SEQ))
        message = jnp.concatenate(
            [returned_ref[PLACE[g] * SEQ : (PLACE[g] + 1) * SEQ] for g in groups], axis=0
        ).astype(F32)
        rows[...] = message.reshape(ROWS * TILES, LANES)
        for c in range(TILES):
            lanes = slice(c * LANES, (c + 1) * LANES)
            long_result = rows[pl.ds(c, ROWS, stride=TILES), :]
            mixed = query_ref[at, lanes] * (long_result + direct_ref[at, lanes])
            if c == 0:
                mixed = jnp.where(lanes_of(mixed) < 2, long_result, mixed)
            out_buf[at, lanes] = mixed.astype(BF16)
        place = pl.ds(step * ROWS, ROWS)
        copies.append(pltpu.make_async_copy(out_buf.at[place], out_ref.at[place], sems.at[step]))
        copies[-1].start()
    for copy in copies:
        copy.wait()


def final(returned, query, direct_term):
    return call(
        final_body,
        "final",
        shape((CHANNELS, TOKENS), BF16),
        [
            pltpu.VMEM((ROWS * TILES, LANES), F32),
            pltpu.VMEM((CHANNELS, TOKENS), BF16),
            pltpu.SemaphoreType.DMA((STEPS,)),
        ],
        [VMEM] * 3,
        HBM,
        10**6,
        2 * 1024 * 1024,
        FINAL_LIMIT,
    )(returned, query, direct_term)


def exchange(messages):
    group = [s * CH + g for g in ORDER for s in range(SEQ)]
    return lax.all_to_all(
        messages, AXES, split_axis=0, concat_axis=0, axis_index_groups=[group], tiled=True
    )


def shards(consts, q, k, v, short_taps, long_filter, skip_gain):
    consts = {name: jnp.asarray(table) for name, table in consts.items()}
    skip = skip_gain[None]
    messages = gate(q, k, v, short_taps, skip).reshape(BLOCKS, WIDTH, 2, LANES)
    messages, q, k, v, long_filter = lax.optimization_barrier((messages, q, k, v, long_filter))
    arrived = exchange(messages).reshape(BLOCKS * 2 * WIDTH, LANES)
    filt = long_filter.reshape(2, BLOCKS * TILES, LANES).swapaxes(0, 1)
    filt = filt.reshape(2 * BLOCKS * TILES, LANES)
    spec = filter_spectra(filt, consts)
    spec, q, k, v = lax.optimization_barrier((spec, q, k, v))
    query, direct_term = direct(q, k, v, short_taps, skip)
    spec, query, direct_term = lax.optimization_barrier((spec, query, direct_term))
    returned = exchange(conv(arrived, spec, consts))
    return final(returned, query, direct_term)


def solution(mesh):
    tokens = P(None, AXES)
    placed = (tokens, tokens, tokens, P(), P("ch", "seq", None, None), P())
    return jax.shard_map(
        functools.partial(shards, tables()),
        mesh=mesh,
        in_specs=placed,
        out_specs=tokens,
        check_vma=False,
    )
```
